32 devices in a mesh: wide: 16 (over z, y, x), rep: 2 (over core).
Axes of the slice: x: 2, y: 2, z: 4, core: 2. Of those that a mesh axis runs over, the one named last changes fastest.
Arguments:
- images: bfloat16 [64, 256, 512], P('rep', 'wide'), may hold values from -6 to 6
- cotangent: bfloat16 [64, 256, 512], P('rep', 'wide'), may hold values from -6 to 6
- levels: int32 [64], P('rep'), may hold values from 0 to 1999
- noise_table: bfloat16 [2000, 512], replicated, may hold values from -6 to 6
- gain_one: float32 [512], replicated, may hold values from 0.1 to 1.9
- shift_one: float32 [512], replicated, may hold values from -3 to 3
- conv_one: bfloat16 [4608, 512], replicated, may hold values from -0.09375 to 0.09375
- bias_one: float32 [512], replicated, may hold values from -3 to 3
- embed_weight: bfloat16 [512, 512], replicated, may hold values from -0.25 to 0.25
- embed_bias: float32 [512], replicated, may hold values from -3 to 3
- gain_two: float32 [512], replicated, may hold values from 0.1 to 1.9
- shift_two: float32 [512], replicated, may hold values from -3 to 3
- conv_two: bfloat16 [4608, 512], replicated, may hold values from -0.09375 to 0.09375
- bias_two: float32 [512], replicated, may hold values from -3 to 3
- gain_three: float32 [512], replicated, may hold values from 0.1 to 1.9
- shift_three: float32 [512], replicated, may hold values from -3 to 3
- query_weight: bfloat16 [512, 512], replicated, may hold values from -0.25 to 0.25
- query_bias: float32 [512], replicated, may hold values from -3 to 3
- key_weight: bfloat16 [512, 512], replicated, may hold values from -0.25 to 0.25
- value_weight: bfloat16 [512, 512], replicated, may hold values from -0.25 to 0.25
- value_bias: float32 [512], replicated, may hold values from -3 to 3
- out_weight: bfloat16 [512, 512], replicated, may hold values from -2 to 2
- out_bias: float32 [512], replicated, may hold values from -3 to 3
Outputs:
- output: bfloat16 [64, 256, 512], P('rep', 'wide')
- input_grad: bfloat16 [64, 256, 512], P('rep', 'wide')
- table_grad: float32 [1024000], P(('wide', 'rep'))
- conv_one_grad: float32 [2359296], P(('wide', 'rep'))
- conv_two_grad: float32 [2359296], P(('wide', 'rep'))
- embed_weight_grad: float32 [262144], P(('wide', 'rep'))
- query_weight_grad: float32 [262144], P(('wide', 'rep'))
- key_weight_grad: float32 [262144], P(('wide', 'rep'))
- value_weight_grad: float32 [262144], P(('wide', 'rep'))
- out_weight_grad: float32 [262144], P(('wide', 'rep'))
- gain_one_grad: float32 [512], replicated
- shift_one_grad: float32 [512], replicated
- bias_one_grad: float32 [512], replicated
- embed_bias_grad: float32 [512], replicated
- gain_two_grad: float32 [512], replicated
- shift_two_grad: float32 [512], replicated
- bias_two_grad: float32 [512], replicated
- gain_three_grad: float32 [512], replicated
- shift_three_grad: float32 [512], replicated
- query_bias_grad: float32 [512], replicated
- value_bias_grad: float32 [512], replicated
- out_bias_grad: float32 [512], replicated
The draws below stay inside these ranges and needn't reach their ends.
All inputs are finite; a program needn't handle non-finite values.
Results may differ from the reference program's by a relative error of at most 0.015.
Values may be sent and summed in bfloat16 or wider, within the bound.
A program may use at most 192 MiB of HBM per device.

```python
import jax
import jax.numpy as jnp
from jax import lax

C = 512
GROUPS = 32
SIDE = 16
LEVELS = 2000
PIX = 256
IMAGES = 64


def with_ends(drawn, own_key, low, top_value):
    longest = drawn.shape.index(max(drawn.shape))
    spots = []
    for shift in (0, 1):
        where = [jax.random.randint(jax.random.fold_in(own_key, axis), (), 0, length) for axis, length in enumerate(drawn.shape)]
        where[longest] = (where[longest] + shift) % drawn.shape[longest]
        spots.append(tuple(where))
    return drawn.at[spots[0]].set(low).at[spots[1]].set(top_value)


def steps_of(stream_key, dims, cuts, least, high):
    def one(dim, shards_of):
        steps = jax.random.uniform(jax.random.fold_in(jax.random.fold_in(stream_key, 6), dim), (shards_of,), jnp.float32, least / len(cuts), high / len(cuts))
        return jnp.repeat(jnp.exp(steps), dims[dim] // shards_of).reshape((-1,) + (1,) * (len(dims) - dim - 1))

    factor_of = one(*cuts[0])
    for cut in cuts[1:]:
        factor_of = factor_of * one(*cut)
    return factor_of


def bell_draw(rng, shape, scale, limit, shards=(), kind=jnp.bfloat16):
    gain = steps_of(rng, shape, shards, -0.22, 0.18) if shards else 1.0
    values = jax.random.normal(rng, shape, jnp.float32) * scale * gain
    return jnp.minimum(jnp.maximum(values, -limit), limit).astype(kind)


def setup_inputs(seed: int = 0) -> dict:
    splits = jax.random.split(jax.random.key(seed), 24)
    return {
        "images": bell_draw(splits[0], (IMAGES, PIX, C), 1.0, 6.0, ((0, 2), (1, 16))),
        "cotangent": bell_draw(splits[1], (IMAGES, PIX, C), 1.0, 6.0, ((0, 2), (1, 16))),
        "levels": with_ends(jax.random.randint(splits[2], (IMAGES,), 0, LEVELS), jax.random.fold_in(splits[2], 1), 0, LEVELS - 1).astype(jnp.int32),
        "noise_table": bell_draw(splits[3], (LEVELS, C), 1.0, 6.0),
        "gain_one": jnp.clip(1.0 + 0.18 * jax.random.normal(splits[4], (C,), jnp.float32), 0.1, 1.9),
        "shift_one": bell_draw(splits[5], (C,), 0.5, 3.0, (), jnp.float32),
        "conv_one": bell_draw(splits[6], (9 * C, C), (9 * C) ** -0.5, 0.09375),
        "bias_one": bell_draw(splits[7], (C,), 0.5, 3.0, (), jnp.float32),
        "embed_weight": bell_draw(splits[8], (C, C), C ** -0.5, 0.25),
        "embed_bias": bell_draw(splits[9], (C,), 0.5, 3.0, (), jnp.float32),
        "gain_two": jnp.clip(1.0 + 0.18 * jax.random.normal(splits[10], (C,), jnp.float32), 0.1, 1.9),
        "shift_two": bell_draw(splits[11], (C,), 0.5, 3.0, (), jnp.float32),
        "conv_two": bell_draw(splits[12], (9 * C, C), (9 * C) ** -0.5, 0.09375),
        "bias_two": bell_draw(splits[13], (C,), 0.5, 3.0, (), jnp.float32),
        "gain_three": jnp.clip(1.0 + 0.18 * jax.random.normal(splits[14], (C,), jnp.float32), 0.1, 1.9),
        "shift_three": bell_draw(splits[15], (C,), 0.5, 3.0, (), jnp.float32),
        "query_weight": bell_draw(splits[16], (C, C), C ** -0.5, 0.25),
        "query_bias": bell_draw(splits[17], (C,), 0.5, 3.0, (), jnp.float32),
        "key_weight": bell_draw(splits[18], (C, C), C ** -0.5, 0.25),
        "value_weight": bell_draw(splits[19], (C, C), C ** -0.5, 0.25),
        "value_bias": bell_draw(splits[20], (C,), 0.5, 3.0, (), jnp.float32),
        "out_weight": bell_draw(splits[21], (C, C), (max(C // 64, 1)) ** -0.5, 2.0),
        "out_bias": bell_draw(splits[22], (C,), 0.5, 3.0, (), jnp.float32),
    }


@jax.custom_vjp
def low(v):
    return lax.optimization_barrier(v.astype(jnp.bfloat16)).astype(jnp.float32)

@jax.custom_vjp
def low_back(v):
    return v

def low_keep(v):
    return (low(v), None)

def low_pass(kept, grad):
    return (grad,)

def back_keep(v):
    return (v, None)

def back_low(kept, grad):
    return (low(grad),)
low.defvjp(low_keep, low_pass)
low_back.defvjp(back_keep, back_low)
epsilon = 1e-05
block_images = 16
highest = lax.Precision.HIGHEST

def swish(field):
    return field * jax.nn.sigmoid(field)

def group_norm(field, norm_gain, norm_shift):
    images_here = field.shape[0]
    grouped = field.reshape(images_here, PIX, GROUPS, C // GROUPS)
    center = lax.optimization_barrier(jnp.mean(grouped, axis=(1, 3), keepdims=True))
    spread = grouped - center
    variance = lax.optimization_barrier(jnp.mean(spread * spread, axis=(1, 3), keepdims=True))
    return (spread * lax.rsqrt(variance + epsilon)).reshape(field.shape) * norm_gain + norm_shift

def project(field, matrix):
    return jnp.einsum('npc,cd->npd', field, matrix, precision=highest)

def convolve(field, kernel):
    images_here = field.shape[0]
    padded = jnp.pad(field.reshape(images_here, SIDE, SIDE, C), ((0, 0), (1, 1), (1, 1), (0, 0)))
    summed = jnp.zeros(field.shape, jnp.float32)
    for kernel_tap in range(9):
        row_off = kernel_tap // 3
        col_off = kernel_tap % 3
        window = padded[:, row_off:row_off + SIDE, col_off:col_off + SIDE, :].reshape(images_here, PIX, C)
        summed = summed + project(window, kernel[kernel_tap * C:(kernel_tap + 1) * C])
    return summed

def forward(weights_all, inputs, embedded):
    gain_one, shift_one, conv_one, bias_one, embed_weight, embed_bias, gain_two, shift_two, conv_two, bias_two, gain_three, shift_three, query_weight, query_bias, key_weight, value_weight, value_bias, out_weight, out_bias = weights_all
    act_one = low(swish(group_norm(inputs, gain_one, shift_one)))
    embed_shift = jnp.dot(embedded, embed_weight, precision=highest) + embed_bias
    hidden_one = low_back(convolve(act_one, conv_one) + bias_one + embed_shift[:, None, :])
    act_two = low(swish(group_norm(hidden_one, gain_two, shift_two)))
    middle = inputs + low_back(convolve(act_two, conv_two) + bias_two)
    normed = low(group_norm(middle, gain_three, shift_three))
    query_block = low(low_back(project(normed, query_weight) + query_bias))
    key_block = low(low_back(project(normed, key_weight)))
    value_block = low(low_back(project(normed, value_weight) + value_bias))
    scores = low_back(C ** (-0.5) * jnp.einsum('npc,nqc->npq', query_block, key_block, precision=highest))
    probs = low(jax.nn.softmax(scores, axis=-1))
    mixed = low(low_back(jnp.einsum('npq,nqc->npc', probs, value_block, precision=highest)))
    return middle + project(mixed, out_weight) + out_bias

def reference(images, cotangent, levels, noise_table, gain_one, shift_one, conv_one, bias_one, embed_weight, embed_bias, gain_two, shift_two, conv_two, bias_two, gain_three, shift_three, query_weight, query_bias, key_weight, value_weight, value_bias, out_weight, out_bias):
    weights_all = tuple((member.astype(jnp.float32) for member in (gain_one, shift_one, conv_one, bias_one, embed_weight, embed_bias, gain_two, shift_two, conv_two, bias_two, gain_three, shift_three, query_weight, query_bias, key_weight, value_weight, value_bias, out_weight, out_bias)))
    table = noise_table.astype(jnp.float32)

    def scan_block(sums_so_far, blocks):
        block_in, block_cot, block_levels = blocks

        def local_pass(inputs, weights_here, table_here):
            return forward(weights_here, inputs, table_here[block_levels])
        result, pullback = jax.vjp(local_pass, block_in.astype(jnp.float32), weights_all, table)
        grad_in, grad_weights, grad_table = pullback(block_cot.astype(jnp.float32))
        sums_so_far = jax.tree.map(lambda left, right: left + right, sums_so_far, (grad_weights, grad_table))
        return (sums_so_far, (result.astype(jnp.bfloat16), grad_in.astype(jnp.bfloat16)))
    initial = jax.tree.map(jnp.zeros_like, (weights_all, table))
    turns = IMAGES // block_images
    shaped = (images.reshape(turns, block_images, PIX, C), cotangent.reshape(turns, block_images, PIX, C), levels.reshape(turns, block_images))
    (grad_weights, grad_table), (results, grads_in) = lax.scan(scan_block, initial, shaped)
    return (results.reshape(IMAGES, PIX, C), grads_in.reshape(IMAGES, PIX, C), grad_table.reshape(-1), grad_weights[2].reshape(-1), grad_weights[8].reshape(-1), grad_weights[4].reshape(-1), grad_weights[12].reshape(-1), grad_weights[14].reshape(-1), grad_weights[15].reshape(-1), grad_weights[17].reshape(-1), grad_weights[0], grad_weights[1], grad_weights[3], grad_weights[5], grad_weights[6], grad_weights[7], grad_weights[9], grad_weights[10], grad_weights[11], grad_weights[13], grad_weights[16], grad_weights[18])
```

```python
import functools
import types

import jax
import jax.numpy as jnp
from jax import lax
from jax.experimental import pallas as pl
from jax.experimental.pallas import tpu as pltpu
from jax.sharding import PartitionSpec as P

GROUPS = 32
SIDE = 16
MESH = pl.DeviceIdType.MESH
CHUNK = 64


epsilon = 1e-05
highest = lax.Precision.HIGHEST


def swish(field):
    return field * jax.nn.sigmoid(field)


def group_norm(field, norm_gain, norm_shift):
    images_here = field.shape[0]
    channels = field.shape[2]
    grouped = field.reshape(images_here, field.shape[1], GROUPS, channels // GROUPS)
    center = jnp.mean(grouped, axis=(1, 3), keepdims=True)
    spread = grouped - center
    variance = jnp.mean(spread * spread, axis=(1, 3), keepdims=True)
    return (spread * lax.rsqrt(variance + epsilon)).reshape(field.shape) * norm_gain + norm_shift


def norm_swish(field, norm_gain, norm_shift):
    return swish(group_norm(field, norm_gain, norm_shift))


def matmul(left, right):
    return jnp.dot(left, right, preferred_element_type=jnp.float32)


def contract_rows(left, right):
    return lax.dot_general(
        left, right, (((0,), (0,)), ((), ())), preferred_element_type=jnp.float32
    )


def against(left, right):
    return lax.dot_general(
        left, right, (((1,), (1,)), ((), ())), preferred_element_type=jnp.float32
    )


def patches(activation):
    images_here = activation.shape[0]
    grid = activation.reshape(images_here, SIDE, SIDE, activation.shape[2])
    padded = jnp.pad(grid, ((0, 0), (1, 1), (1, 1), (0, 0)))
    pieces = [
        padded[
            :, kernel_tap // 3 : kernel_tap // 3 + SIDE, kernel_tap % 3 : kernel_tap % 3 + SIDE, :
        ]
        for kernel_tap in range(9)
    ]
    return jnp.concatenate(pieces, axis=-1).reshape(images_here * SIDE * SIDE, -1)


def unpatch(columns, images_here):
    channels = columns.shape[1] // 9
    grid = columns.reshape(images_here, SIDE, SIDE, 9, channels)
    summed = jnp.zeros((images_here, SIDE + 2, SIDE + 2, channels), jnp.float32)
    for kernel_tap in range(9):
        row_off = kernel_tap // 3
        col_off = kernel_tap % 3
        summed = summed + jnp.pad(
            grid[:, :, :, kernel_tap, :],
            ((0, 0), (row_off, 2 - row_off), (col_off, 2 - col_off), (0, 0)),
        )
    return summed[:, 1 : SIDE + 1, 1 : SIDE + 1, :].reshape(images_here, SIDE * SIDE, channels)


def plain_device(
    images,
    cotangent,
    levels,
    noise_table,
    gain_one,
    shift_one,
    conv_one,
    bias_one,
    embed_weight,
    embed_bias,
    gain_two,
    shift_two,
    conv_two,
    bias_two,
    gain_three,
    shift_three,
    query_weight,
    query_bias,
    key_weight,
    value_weight,
    value_bias,
    out_weight,
    out_bias,
):
    arrived, upstream = (
        lax.all_to_all(images, "wide", split_axis=0, concat_axis=1, tiled=True),
        lax.all_to_all(cotangent, "wide", split_axis=0, concat_axis=1, tiled=True),
    )
    images_here = arrived.shape[0]
    pixels = arrived.shape[1]
    channels = arrived.shape[2]
    flat_rows = images_here * pixels
    score_scale = channels ** (-0.5)
    table_rows = noise_table.shape[0]
    offset = lax.axis_index("wide") * images_here
    own_levels = lax.dynamic_slice_in_dim(levels, offset, images_here)
    selector = own_levels[:, None] == jnp.arange(table_rows, dtype=jnp.int32)[None, :]
    embedded = matmul(selector.astype(jnp.bfloat16), noise_table).astype(jnp.bfloat16)
    embed_shift = matmul(embedded, embed_weight) + embed_bias
    inputs = arrived.astype(jnp.float32)
    act_one, back_one = jax.vjp(norm_swish, inputs, gain_one, shift_one)
    cols_one = patches(act_one.astype(jnp.bfloat16))
    hidden_one = (matmul(cols_one, conv_one) + bias_one).reshape(images_here, pixels, channels)
    hidden_one = hidden_one + embed_shift[:, None, :]
    act_two, back_two = jax.vjp(norm_swish, hidden_one, gain_two, shift_two)
    cols_two = patches(act_two.astype(jnp.bfloat16))
    branch_out = matmul(cols_two, conv_two) + bias_two
    middle = inputs + branch_out.reshape(images_here, pixels, channels)
    normed, back_three = jax.vjp(group_norm, middle, gain_three, shift_three)
    normed_low = normed.astype(jnp.bfloat16).reshape(flat_rows, channels)
    query_block = (matmul(normed_low, query_weight) + query_bias).astype(jnp.bfloat16)
    key_block = matmul(normed_low, key_weight).astype(jnp.bfloat16)
    value_block = (matmul(normed_low, value_weight) + value_bias).astype(jnp.bfloat16)
    query_block = query_block.reshape(images_here, pixels, channels)
    key_block = key_block.reshape(images_here, pixels, channels)
    value_block = value_block.reshape(images_here, pixels, channels)
    scores = (
        jnp.einsum("npc,nqc->npq", query_block, key_block, preferred_element_type=jnp.float32)
        * score_scale
    )
    row_top = jnp.max(scores, axis=-1, keepdims=True)
    exponent = jnp.exp(scores - row_top)
    row_total = jnp.sum(exponent, axis=-1, keepdims=True)
    probs_low = (exponent / row_total).astype(jnp.bfloat16)
    log_total = row_top + jnp.log(row_total)
    mixed = jnp.einsum("npq,nqc->npc", probs_low, value_block, preferred_element_type=jnp.float32)
    mixed_low = mixed.astype(jnp.bfloat16).reshape(flat_rows, channels)
    result = middle.reshape(flat_rows, channels) + matmul(mixed_low, out_weight) + out_bias
    grad_out = upstream.reshape(flat_rows, channels)
    grad_out_bias = jnp.sum(grad_out.astype(jnp.float32), axis=0)
    grad_out_weight = contract_rows(mixed_low, grad_out)
    grad_mixed = (
        against(grad_out, out_weight).astype(jnp.bfloat16).reshape(images_here, pixels, channels)
    )
    scores_again = (
        jnp.einsum("npc,nqc->npq", query_block, key_block, preferred_element_type=jnp.float32)
        * score_scale
    )
    probs = jnp.exp(scores_again - log_total)
    probs_again = probs.astype(jnp.bfloat16)
    grad_probs = jnp.einsum(
        "npc,nqc->npq", grad_mixed, value_block, preferred_element_type=jnp.float32
    )
    grad_values = jnp.einsum(
        "npq,npc->nqc", probs_again, grad_mixed, preferred_element_type=jnp.float32
    ).astype(jnp.bfloat16)
    grad_scores = probs * (grad_probs - jnp.sum(grad_probs * probs, axis=-1, keepdims=True))
    grad_scores = grad_scores.astype(jnp.bfloat16)
    grad_query = (
        (
            jnp.einsum("npq,nqc->npc", grad_scores, key_block, preferred_element_type=jnp.float32)
            * score_scale
        )
        .astype(jnp.bfloat16)
        .reshape(flat_rows, channels)
    )
    grad_keys = (
        (
            jnp.einsum("npq,npc->nqc", grad_scores, query_block, preferred_element_type=jnp.float32)
            * score_scale
        )
        .astype(jnp.bfloat16)
        .reshape(flat_rows, channels)
    )
    grad_values = grad_values.reshape(flat_rows, channels)
    grad_query_weight = contract_rows(normed_low, grad_query)
    grad_key_weight = contract_rows(normed_low, grad_keys)
    grad_value_weight = contract_rows(normed_low, grad_values)
    grad_query_bias = jnp.sum(grad_query.astype(jnp.float32), axis=0)
    grad_value_bias = jnp.sum(grad_values.astype(jnp.float32), axis=0)
    grad_normed = against(grad_query, query_weight) + against(grad_keys, key_weight)
    grad_normed = grad_normed + against(grad_values, value_weight)
    grad_middle, grad_gain_three, grad_shift_three = back_three(
        grad_normed.reshape(images_here, pixels, channels)
    )
    grad_middle = grad_middle + upstream.astype(jnp.float32)
    grad_branch = grad_middle.astype(jnp.bfloat16).reshape(flat_rows, channels)
    grad_bias_two = jnp.sum(grad_branch.astype(jnp.float32), axis=0)
    grad_conv_two = contract_rows(cols_two, grad_branch)
    grad_act_two = unpatch(against(grad_branch, conv_two), images_here)
    grad_hidden, grad_gain_two, grad_shift_two = back_two(grad_act_two)
    grad_hidden_low = grad_hidden.astype(jnp.bfloat16)
    hidden_rows = grad_hidden_low.reshape(flat_rows, channels)
    grad_bias_one = jnp.sum(hidden_rows.astype(jnp.float32), axis=0)
    grad_conv_one = contract_rows(cols_one, hidden_rows)
    grad_shift = jnp.sum(grad_hidden_low.astype(jnp.float32), axis=1)
    grad_embed_bias = jnp.sum(grad_shift, axis=0)
    grad_embed_weight = jnp.dot(embedded.astype(jnp.float32).T, grad_shift, precision=highest)
    embed_float = embed_weight.astype(jnp.float32)
    grad_act_one = unpatch(against(hidden_rows, conv_one), images_here)
    grad_input_part, grad_gain_one, grad_shift_one = back_one(grad_act_one)
    grad_input = grad_middle + grad_input_part
    output_back, input_back = (
        lax.all_to_all(
            result.reshape(images_here, pixels, channels).astype(jnp.bfloat16),
            "wide",
            split_axis=1,
            concat_axis=0,
            tiled=True,
        ),
        lax.all_to_all(
            grad_input.astype(jnp.bfloat16), "wide", split_axis=1, concat_axis=0, tiled=True
        ),
    )
    wide_count = lax.axis_size("wide")
    rep_count = lax.axis_size("rep")
    device_count = wide_count * rep_count
    weight_grads = (
        grad_conv_one,
        grad_conv_two,
        grad_embed_weight,
        grad_query_weight,
        grad_key_weight,
        grad_value_weight,
        grad_out_weight,
    )
    grad_embedded = jnp.dot(grad_shift, embed_float.T, precision=highest)
    grad_table = jnp.dot(selector.astype(jnp.float32).T, grad_embedded, precision=highest)
    members = (grad_table,) + weight_grads
    widths = [member.size // device_count for member in members]
    packed = jnp.concatenate([member.reshape(device_count, -1) for member in members], axis=1)
    packed = lax.psum_scatter(packed, ("wide", "rep"), scatter_dimension=0, tiled=True)
    packed = packed.reshape(-1)
    large_grads = []
    start_at = 0
    for width in widths:
        large_grads.append(packed[start_at : start_at + width])
        start_at = start_at + width
    large_grads = tuple(large_grads)
    small_grads = lax.psum(
        (
            grad_gain_one,
            grad_shift_one,
            grad_bias_one,
            grad_embed_bias,
            grad_gain_two,
            grad_shift_two,
            grad_bias_two,
            grad_gain_three,
            grad_shift_three,
            grad_query_bias,
            grad_value_bias,
            grad_out_bias,
        ),
        ("wide", "rep"),
    )
    return (output_back, input_back) + large_grads + tuple(small_grads)


def by_rows(left, right):
    return lax.dot_general(
        left, right, (((0,), (0,)), ((), ())), preferred_element_type=jnp.float32
    )


def group_sum(rows):
    channels = rows.shape[1]
    lane = lax.broadcasted_iota(jnp.int32, rows.shape, 1)
    reach = 1
    while reach < channels // GROUPS:
        odd = (lane // reach) % 2
        rows = rows + jnp.where(
            odd == 0, pltpu.roll(rows, channels - reach, 1), pltpu.roll(rows, reach, 1)
        )
        reach = reach * 2
    return rows


def stack_rows(members):
    shape = (8, members[0].shape[1])
    place = lax.broadcasted_iota(jnp.int32, shape, 0)
    stacked = jnp.zeros(shape, jnp.float32)
    for index, member in enumerate(members):
        stacked = jnp.where(place == index, jnp.broadcast_to(member, shape), stacked)
    return stacked


def sigmoid(field):
    return 0.5 + 0.5 * jnp.tanh(0.5 * field)


INPUTS = ("images", "cotangent", "noise_table", "conv_one", "conv_two", "embed_weight", "query_weight", "key_weight", "value_weight", "out_weight", "levels", "gain_one", "shift_one", "bias_one", "embed_bias", "gain_two", "shift_two", "bias_two", "gain_three", "shift_three", "query_bias", "value_bias", "out_bias")
SUMS = ("gain_one", "shift_one", "bias_one", "gain_two", "shift_two", "bias_two", "gain_three", "shift_three", "query_bias", "value_bias", "out_bias")


class Reduce:
    def __init__(self, place, blocks, bits, landing, kept, send, recv, parts, last):
        self.place, self.blocks, self.bits, self.last = place, blocks, bits, last
        self.landing, self.kept, self.send, self.recv = landing, kept, send, recv
        self.rows = blocks.shape[2]
        self.parts = parts

    def cut(self, part):
        size = self.rows // self.parts
        return pl.ds(part * size, size)

    def copy(self, stage, part):
        place, rows = self.place, self.cut(part)
        if stage == 0:
            source = self.blocks.at[:, 1 - place.core, rows, :]
            target = place.other_core
        else:
            count = self.blocks.shape[0] >> stage
            bit = self.bits[stage - 1]
            source = self.kept[stage - 1].at[
                pl.ds((1 - place.bit(bit)) * count, count), rows, :
            ]
            target = place.across(bit)
        return pltpu.make_async_remote_copy(
            src_ref=source,
            dst_ref=self.landing[stage].at[:, rows, :],
            send_sem=self.send.at[stage, part],
            recv_sem=self.recv.at[stage, part],
            device_id=target,
            device_id_type=MESH,
        )

    def start(self, stage, part):
        self.copy(stage, part).start()

    def finish(self, stage, part):
        place, rows = self.place, self.cut(part)
        self.copy(stage, part).wait_recv()
        count = self.blocks.shape[0] >> stage
        final = stage == len(self.bits)

        def add(index, carry):
            if stage == 0:
                own = self.blocks[index, place.core, rows, :]
            else:
                own = self.kept[stage - 1][
                    place.bit(self.bits[stage - 1]) * count + index, rows, :
                ]
            total = own.astype(jnp.float32) + self.landing[stage][index, rows, :].astype(
                jnp.float32
            )
            if final:
                self.last(index, rows, total)
            else:
                self.kept[stage][index, rows, :] = total.astype(jnp.bfloat16)
            return carry

        lax.fori_loop(0, count, add, 0)

    def drain(self):
        for stage in range(len(self.bits) + 1):
            for part in range(self.parts):
                self.copy(stage, part).wait_send()


class Place:
    def __init__(self, ranks):
        self.ranks = ranks
        self.rank = lax.axis_index("wide")
        self.core = lax.axis_index("rep")
        self.other_core = (self.rank, 1 - self.core)

    def bit(self, index):
        return (self.rank // (1 << index)) % 2

    def across(self, index):
        step = 1 << index
        return (self.rank + step - 2 * step * self.bit(index), self.core)


def block_order(ranks, order):
    places = []
    for rank in range(ranks):
        spot = 0
        for bit in order:
            spot = spot * 2 + (rank >> bit) % 2
        places.append(spot)
    return places


def fused_kernel(names, ranks, table_rows, *refs):
    s = types.SimpleNamespace(**dict(zip(names, refs, strict=True)))
    place = Place(ranks)
    bits = (ranks - 1).bit_length()
    far = list(range(2, bits))
    images_here, pixels, channels = s.arrived.shape
    flat_rows = images_here * pixels
    piece = pixels // ranks
    half = channels // 2
    steps = pixels // CHUNK
    score_scale = channels ** (-0.5)
    count_inverse = 1.0 / (pixels * (channels // GROUPS))
    col = lax.broadcasted_iota(jnp.int32, (CHUNK, 1), 0) % SIDE

    loads = []
    for index, name in enumerate(
        ("noise_table", "embed_weight", "conv_one", "conv_two", "query_weight", "key_weight", "value_weight", "out_weight")
    ):
        source = getattr(s, name)
        target = getattr(s, name + "_here")
        if name == "noise_table":
            target = target.at[pl.ds(0, table_rows), :]
        loads.append(pltpu.make_async_copy(source, target, s.load_sem.at[index]))
        loads[-1].start()

    barrier = pltpu.get_barrier_semaphore()

    def greet(offset, carry):
        pl.semaphore_signal(
            barrier,
            inc=1,
            device_id=((place.rank + offset) % ranks, place.core),
            device_id_type=MESH,
        )
        return carry

    lax.fori_loop(1, ranks, greet, 0)
    pl.semaphore_signal(barrier, inc=1, device_id=place.other_core, device_id_type=MESH)
    pl.semaphore_wait(barrier, ranks)

    def gather_copy(which, source, target, offset):
        peer = (place.rank + offset) % ranks
        return pltpu.make_async_remote_copy(
            src_ref=source.at[pl.ds(peer * images_here, images_here)],
            dst_ref=target.at[:, pl.ds(pl.multiple_of(place.rank * piece, 16), piece)],
            send_sem=s.swap_send.at[which, offset],
            recv_sem=s.swap_recv.at[which, offset],
            device_id=(peer, place.core),
            device_id_type=MESH,
        )

    def gather_own(which, source, target):
        return pltpu.make_async_copy(
            source.at[pl.ds(place.rank * images_here, images_here)],
            target.at[:, pl.ds(pl.multiple_of(place.rank * piece, 16), piece)],
            s.swap_own.at[which],
        )

    def scatter_copy(which, source, target, offset):
        peer = (place.rank + offset) % ranks
        return pltpu.make_async_remote_copy(
            src_ref=source.at[:, pl.ds(pl.multiple_of(peer * piece, 16), piece)],
            dst_ref=target.at[pl.ds(place.rank * images_here, images_here)],
            send_sem=s.swap_send.at[which, offset],
            recv_sem=s.swap_recv.at[which, offset],
            device_id=(peer, place.core),
            device_id_type=MESH,
        )

    def scatter_own(which, source, target):
        return pltpu.make_async_copy(
            source.at[:, pl.ds(pl.multiple_of(place.rank * piece, 16), piece)],
            target.at[pl.ds(place.rank * images_here, images_here)],
            s.swap_own.at[which],
        )

    def swap_start(copy, own, which, source, target):
        def go(offset, carry):
            copy(which, source, target, offset).start()
            return carry

        lax.fori_loop(1, ranks, go, 0)
        own(which, source, target).start()

    def swap_arrive(copy, own, which, source, target):
        def go(offset, carry):
            copy(which, source, target, offset).wait_recv()
            return carry

        lax.fori_loop(1, ranks, go, 0)
        own(which, source, target).wait()

    def swap_drain(copy, which, source, target):
        def go(offset, carry):
            copy(which, source, target, offset).wait_send()
            return carry

        lax.fori_loop(1, ranks, go, 0)

    swap_start(gather_copy, gather_own, 0, s.images, s.arrived)

    for padded in (s.spread_act, s.spread_two, s.spread_one, s.spread_far):
        for image in range(images_here):
            edge = jnp.zeros((SIDE, padded.shape[2]), jnp.bfloat16)
            padded[image, 0:SIDE, :] = edge
            padded[image, pixels + SIDE : pixels + 2 * SIDE, :] = edge
    tail = s.noise_table_here.shape[0] - table_rows
    if tail:
        s.noise_table_here[table_rows:, :] = jnp.zeros((tail, channels), jnp.bfloat16)
    own_levels = [s.levels[place.rank * images_here + image] for image in range(images_here)]
    entry = lax.broadcasted_iota(jnp.int32, (8, s.noise_table_here.shape[0]), 1)
    line = lax.broadcasted_iota(jnp.int32, entry.shape, 0)
    selected = jnp.zeros(entry.shape, jnp.float32)
    for image in range(images_here):
        hit = jnp.where(entry == own_levels[image], 1.0, 0.0)
        selected = jnp.where(line == image, hit, selected)
    loads[0].wait()
    loads[1].wait()
    embedded = matmul(selected.astype(jnp.bfloat16), s.noise_table_here[...])
    embed_shift = matmul(embedded.astype(jnp.bfloat16), s.embed_weight_here[...])
    embed_shift = embed_shift + s.embed_bias[...] + s.bias_one[...]

    def over(image, body, start):
        return lax.fori_loop(0, steps, functools.partial(body, image), start)

    def at(step):
        return pl.ds(pl.multiple_of(step * CHUNK, CHUNK), CHUNK)

    def flat_at(image, step):
        return pl.ds(pl.multiple_of(image * pixels + step * CHUNK, CHUNK), CHUNK)

    def fold(chunk):
        return jnp.sum(chunk.reshape(CHUNK // 8, 8, channels), axis=0)

    none = jnp.zeros((8, channels), jnp.float32)

    def whole(part):
        return jnp.sum(part, axis=0, keepdims=True)

    def statistics(load):
        def first(image, step, total):
            return total + fold(load(image, step))

        sums = [whole(over(image, first, none)) for image in range(images_here)]
        center = group_sum(stack_rows(sums)) * count_inverse

        def second(image, step, total):
            spread = load(image, step) - center[image : image + 1]
            return total + fold(spread * spread)

        sums = [whole(over(image, second, none)) for image in range(images_here)]
        variance = group_sum(stack_rows(sums)) * count_inverse
        return center, lax.rsqrt(variance + epsilon)

    def spread_out(target, image, step, chunk, before, after):
        width = chunk.shape[1]
        rows = pl.ds(pl.multiple_of(step * CHUNK + SIDE, SIDE), CHUNK)
        target[image, rows, before * width : (before + 1) * width] = jnp.where(
            col > 0, pltpu.roll(chunk, 1, 0), 0.0
        ).astype(jnp.bfloat16)
        target[image, rows, width : 2 * width] = chunk.astype(jnp.bfloat16)
        target[image, rows, after * width : (after + 1) * width] = jnp.where(
            col < SIDE - 1, pltpu.roll(chunk, CHUNK - 1, 0), 0.0
        ).astype(jnp.bfloat16)

    def activate(load, center, rate, gain, shift, keep):
        for image in range(images_here):
            slope = rate[image : image + 1] * gain

            def apply(image, step, carry, slope=slope):
                field = (load(image, step) - center[image : image + 1]) * slope + shift
                act = field * sigmoid(field)
                spread_out(s.spread_act, image, step, act, 0, 2)
                keep[flat_at(image, step), :] = act.astype(jnp.bfloat16)
                return carry

            over(image, apply, 0)

    def convolve(weight):
        total = None
        for row_tap in range(3):
            window = s.spread_act[:, SIDE * row_tap : SIDE * row_tap + pixels, :]
            term = matmul(
                window.reshape(flat_rows, 3 * channels),
                weight[3 * channels * row_tap : 3 * channels * (row_tap + 1), :],
            )
            total = term if total is None else total + term
        return total

    def tap_rows(row_tap):
        return slice(SIDE * (2 - row_tap), SIDE * (2 - row_tap) + pixels)

    def convolve_back(source, weight):
        total = None
        for tap in range(9):
            window = source[
                :, tap_rows(tap // 3), (tap % 3) * channels : (tap % 3 + 1) * channels
            ]
            term = against(
                window.reshape(flat_rows, channels),
                weight[channels * tap : channels * (tap + 1), :],
            )
            total = term if total is None else total + term
        return total

    def share_copy(slot, source, target, bit):
        return pltpu.make_async_remote_copy(
            src_ref=source,
            dst_ref=target,
            send_sem=s.share_send.at[slot],
            recv_sem=s.share_recv.at[slot],
            device_id=place.across(bit),
            device_id_type=MESH,
        )

    bit_one, bit_two = 1, 0
    half_one, half_two = place.bit(bit_one), place.bit(bit_two)

    def other_half(ref, mine):
        return ref.at[:, pl.ds(pl.multiple_of((1 - mine) * half, half), half)]

    share_act_one = share_copy(0, s.act_one, s.act_one_far, bit_one)
    share_act_two = share_copy(1, s.act_two, s.act_two_far, bit_two)
    share_grad_two = share_copy(2, other_half(s.grad_two, half_two), s.grad_two_far, bit_two)
    share_grad_one = share_copy(3, other_half(s.grad_one, half_one), s.grad_one_far, bit_one)

    def weigh(spread, mine, act, act_far, grad_far, blocks, spots):
        def unfold(image, step, carry):
            chunk = grad_far[flat_at(image, step), :].astype(jnp.float32)
            spread_out(s.spread_far, image, step, chunk, 2, 0)
            return carry

        for image in range(images_here):
            over(image, unfold, 0)
        rows_block = blocks.shape[2]
        for tap in range(9):
            rows, side_tap = tap_rows(tap // 3), tap % 3
            near = spread[
                :, rows, pl.ds(pl.multiple_of(side_tap * channels + mine * half, half), half)
            ]
            beyond = s.spread_far[:, rows, side_tap * half : (side_tap + 1) * half]
            product = by_rows(act[...], near.reshape(flat_rows, half)) + by_rows(
                act_far[...], beyond.reshape(flat_rows, half)
            )
            product = product.astype(jnp.bfloat16)
            done = 0
            while done < channels:
                block, inside = divmod(tap * channels + done, rows_block)
                size = min(rows_block - inside, channels - done)
                blocks[spots[block // 2], block % 2, inside : inside + size, :] = product[
                    done : done + size
                ]
                done = done + size

    def last_conv(share, kept):
        def put(index, rows, total):
            kept[index, rows, :] = total

        return put

    order_one = [1 - bit_one] + far
    order_two = [1 - bit_two] + far
    order_mix = [0, 1] + far
    spots_one = block_order(ranks, order_one + [bit_one])
    spots_two = block_order(ranks, order_two + [bit_two])
    spots_mix = block_order(ranks, order_mix)

    def put_one(index, rows, total):
        s.sum_one[index, rows, :] = total
        s.fin_one[index, rows, :] = total.astype(jnp.bfloat16)

    def put_two(index, rows, total):
        s.sum_two[index, rows, :] = total
        s.fin_two[index, rows, :] = total.astype(jnp.bfloat16)

    def put_mix(index, rows, total):
        s.share_mix[rows, :] = total

    def gathered(name, count):
        return [getattr(s, f"{name}_{index}") for index in range(count)]

    parts = s.reduce_send_one.shape[1]
    reduce_one = Reduce(
        place,
        s.blocks_one,
        order_one,
        gathered("land_one", bits),
        gathered("kept_one", bits - 1),
        s.reduce_send_one,
        s.reduce_recv_one,
        parts,
        put_one,
    )
    reduce_two = Reduce(
        place,
        s.blocks_two,
        order_two,
        gathered("land_two", bits),
        gathered("kept_two", bits - 1),
        s.reduce_send_two,
        s.reduce_recv_two,
        parts,
        put_two,
    )
    reduce_mix = Reduce(
        place,
        s.blocks_mix,
        order_mix,
        gathered("land_mix", bits + 1),
        gathered("kept_mix", bits),
        s.reduce_send_mix,
        s.reduce_recv_mix,
        1,
        put_mix,
    )

    def last_copy(slot, fin, target, mine, bit):
        return share_copy(slot, fin.at[1 - mine], target, bit)

    def settle(copy, sums, target, mine, share):
        copy.wait_recv()
        own = sums[mine]
        other = target[...].astype(jnp.float32)
        share[:, 0:half] = jnp.where(mine == 0, own, other)
        share[:, half:channels] = jnp.where(mine == 0, other, own)

    def small_copy(stage):
        return pltpu.make_async_remote_copy(
            src_ref=s.small_sum.at[stage],
            dst_ref=s.small_land.at[stage],
            send_sem=s.small_send.at[stage],
            recv_sem=s.small_recv.at[stage],
            device_id=place.other_core if stage == 0 else place.across(stage - 1),
            device_id_type=MESH,
        )

    def small_finish(stage):
        small_copy(stage).wait_recv()
        s.small_sum[stage + 1] = s.small_sum[stage] + s.small_land[stage]

    slot_rows = 16
    device = place.rank * 2 + place.core

    def slots_copy(stage):
        count = 1 << stage
        first = pl.multiple_of((device // count) * count * slot_rows, slot_rows)
        window = s.slots.at[pl.ds(first, count * slot_rows), :]
        return pltpu.make_async_remote_copy(
            src_ref=window,
            dst_ref=window,
            send_sem=s.slots_send.at[stage],
            recv_sem=s.slots_recv.at[stage],
            device_id=place.other_core if stage == 0 else place.across(stage - 1),
            device_id_type=MESH,
        )

    swap_arrive(gather_copy, gather_own, 0, s.images, s.arrived)
    swap_start(gather_copy, gather_own, 1, s.cotangent, s.upstream)

    def load_input(image, step):
        return s.arrived[image, at(step), :].astype(jnp.float32)

    def load_hidden(image, step):
        return s.hidden[flat_at(image, step), :]

    def load_middle(image, step):
        return s.middle[flat_at(image, step), :]

    gain_one, shift_one = s.gain_one[...], s.shift_one[...]
    gain_two, shift_two = s.gain_two[...], s.shift_two[...]
    gain_three, shift_three = s.gain_three[...], s.shift_three[...]
    center_one, rate_one = statistics(load_input)
    activate(load_input, center_one, rate_one, gain_one, shift_one, s.act_one)
    share_act_one.start()
    loads[2].wait()
    conv = convolve(s.conv_one_here)
    for image in range(images_here):
        rows = slice(image * pixels, (image + 1) * pixels)
        s.hidden[rows, :] = conv[rows] + embed_shift[image : image + 1]
    center_two, rate_two = statistics(load_hidden)
    activate(load_hidden, center_two, rate_two, gain_two, shift_two, s.act_two)
    share_act_two.start()
    loads[3].wait()
    s.middle[...] = (
        convolve(s.conv_two_here)
        + s.bias_two[...]
        + s.arrived[...].reshape(flat_rows, channels).astype(jnp.float32)
    )
    center_three, rate_three = statistics(load_middle)
    for image in range(images_here):
        slope = rate_three[image : image + 1] * gain_three

        def normalize(image, step, carry, slope=slope):
            spread = load_middle(image, step) - center_three[image : image + 1]
            s.normed[flat_at(image, step), :] = (spread * slope + shift_three).astype(jnp.bfloat16)
            return carry

        over(image, normalize, 0)
    for load in loads[4:]:
        load.wait()
    normed = s.normed[...]
    s.query[...] = (matmul(normed, s.query_weight_here[...]) + s.query_bias[...]).astype(
        jnp.bfloat16
    )
    s.key[...] = matmul(normed, s.key_weight_here[...]).astype(jnp.bfloat16)
    s.value[...] = (matmul(normed, s.value_weight_here[...]) + s.value_bias[...]).astype(
        jnp.bfloat16
    )
    for image in range(images_here):
        rows = slice(image * pixels, (image + 1) * pixels)
        scores = against(s.query[rows, :], s.key[rows, :]) * score_scale
        exponent = jnp.exp(scores - jnp.max(scores, axis=1, keepdims=True))
        probs = exponent / jnp.sum(exponent, axis=1, keepdims=True)
        s.probs[rows, :] = probs
        s.mixed[rows, :] = matmul(probs.astype(jnp.bfloat16), s.value[rows, :]).astype(
            jnp.bfloat16
        )
    result = s.middle[...] + matmul(s.mixed[...], s.out_weight_here[...]) + s.out_bias[...]
    s.leaving[...] = result.astype(jnp.bfloat16).reshape(images_here, pixels, channels)

    swap_arrive(gather_copy, gather_own, 1, s.cotangent, s.upstream)
    swap_start(scatter_copy, scatter_own, 2, s.leaving, s.output)

    def load_upstream(image, step):
        return s.upstream[image, at(step), :].astype(jnp.float32)

    def column_sums(load):
        def body(image, step, total):
            return total + fold(load(image, step))

        total = none
        for image in range(images_here):
            total = over(image, body, total)
        return whole(total)

    grad_out_bias = column_sums(load_upstream)
    upstream = s.upstream[...].reshape(flat_rows, channels)
    mix_rows = s.blocks_mix.shape[2] // 4

    def store_mix(which, product):
        product = product.astype(jnp.bfloat16)
        for rank in range(ranks):
            for core in range(2):
                block = rank * 2 + core
                s.blocks_mix[
                    spots_mix[rank], core, which * mix_rows : (which + 1) * mix_rows, :
                ] = product[block * mix_rows : (block + 1) * mix_rows]

    store_mix(3, by_rows(s.mixed[...], upstream))
    s.grad_mixed[...] = against(upstream, s.out_weight_here[...]).astype(jnp.bfloat16)
    for image in range(images_here):
        rows = slice(image * pixels, (image + 1) * pixels)
        probs = s.probs[rows, :]
        grad_mixed = s.grad_mixed[rows, :]
        grad_probs = against(grad_mixed, s.value[rows, :])
        s.grad_value[rows, :] = by_rows(probs.astype(jnp.bfloat16), grad_mixed).astype(
            jnp.bfloat16
        )
        inner = jnp.sum(grad_probs * probs, axis=1, keepdims=True)
        grad_scores = (probs * (grad_probs - inner)).astype(jnp.bfloat16)
        s.grad_query[rows, :] = (matmul(grad_scores, s.key[rows, :]) * score_scale).astype(
            jnp.bfloat16
        )
        s.grad_key[rows, :] = (by_rows(grad_scores, s.query[rows, :]) * score_scale).astype(
            jnp.bfloat16
        )

    s.delta[...] = (
        against(s.grad_query[...], s.query_weight_here[...])
        + against(s.grad_key[...], s.key_weight_here[...])
        + against(s.grad_value[...], s.value_weight_here[...])
    )

    def delta_at(image, step):
        return s.delta[flat_at(image, step), :]

    def norm_back_terms(gain, shift_sums, gain_sums):
        rows = [gain * total for total in shift_sums] + [gain * total for total in gain_sums]
        return group_sum(stack_rows(rows)) * count_inverse

    shift_sums, gain_sums = [], []
    for image in range(images_here):

        def sums_three(image, step, totals):
            grad = delta_at(image, step)
            unit = (load_middle(image, step) - center_three[image : image + 1]) * rate_three[
                image : image + 1
            ]
            return totals[0] + fold(grad), totals[1] + fold(grad * unit)

        totals = over(image, sums_three, (none, none))
        shift_sums.append(whole(totals[0]))
        gain_sums.append(whole(totals[1]))
    means = norm_back_terms(gain_three, shift_sums, gain_sums)
    grad_gain_three = functools.reduce(jnp.add, gain_sums)
    grad_shift_three = functools.reduce(jnp.add, shift_sums)
    total_two = none
    for image in range(images_here):
        mean_shift = means[image : image + 1]
        mean_gain = means[images_here + image : images_here + image + 1]

        def back_three(image, step, total, mean_shift=mean_shift, mean_gain=mean_gain):
            rate = rate_three[image : image + 1]
            unit = (load_middle(image, step) - center_three[image : image + 1]) * rate
            grad = rate * (delta_at(image, step) * gain_three - mean_shift - unit * mean_gain)
            grad = grad + load_upstream(image, step)
            s.grad_middle[flat_at(image, step), :] = grad
            low = grad.astype(jnp.bfloat16)
            s.grad_two[flat_at(image, step), :] = low
            low = low.astype(jnp.float32)
            spread_out(s.spread_two, image, step, low, 2, 0)
            return total + fold(low)

        total_two = over(image, back_three, total_two)
    grad_bias_two = whole(total_two)
    share_grad_two.start()

    store_mix(0, by_rows(normed, s.grad_query[...]))
    store_mix(1, by_rows(normed, s.grad_key[...]))
    store_mix(2, by_rows(normed, s.grad_value[...]))
    reduce_mix.start(0, 0)

    def load_grad(ref):
        return lambda image, step: ref[flat_at(image, step), :].astype(jnp.float32)

    grad_query_bias = column_sums(load_grad(s.grad_query))
    grad_value_bias = column_sums(load_grad(s.grad_value))

    def swish_norm_back(load, center, rate, gain, shift, put, start):
        shift_sums, gain_sums = [], []
        for image in range(images_here):

            def sums(image, step, totals):
                unit = (load(image, step) - center[image : image + 1]) * rate[image : image + 1]
                field = unit * gain + shift
                gate = sigmoid(field)
                grad = delta_at(image, step) * (gate * (1.0 + field * (1.0 - gate)))
                s.delta[flat_at(image, step), :] = grad
                return totals[0] + fold(grad), totals[1] + fold(grad * unit)

            totals = over(image, sums, (none, none))
            shift_sums.append(whole(totals[0]))
            gain_sums.append(whole(totals[1]))
        means = norm_back_terms(gain, shift_sums, gain_sums)
        carries = []
        for image in range(images_here):
            mean_shift = means[image : image + 1]
            mean_gain = means[images_here + image : images_here + image + 1]

            def back(image, step, carry, mean_shift=mean_shift, mean_gain=mean_gain):
                slope = rate[image : image + 1]
                unit = (load(image, step) - center[image : image + 1]) * slope
                grad = slope * (delta_at(image, step) * gain - mean_shift - unit * mean_gain)
                return put(image, step, grad, carry)

            carries.append(over(image, back, start))
        return (
            functools.reduce(jnp.add, gain_sums),
            functools.reduce(jnp.add, shift_sums),
            carries,
        )

    s.delta[...] = convolve_back(s.spread_two, s.conv_two_here)

    def put_hidden(image, step, grad, total):
        low = grad.astype(jnp.bfloat16)
        s.grad_one[flat_at(image, step), :] = low
        low = low.astype(jnp.float32)
        spread_out(s.spread_one, image, step, low, 2, 0)
        return total + fold(low)

    grad_gain_two, grad_shift_two, totals = swish_norm_back(
        load_hidden, center_two, rate_two, gain_two, shift_two, put_hidden, none
    )
    share_grad_one.start()
    grad_shift = [whole(total) for total in totals]
    grad_bias_one = functools.reduce(jnp.add, grad_shift)

    lanes = s.slots.shape[1]
    slot_place = lax.broadcasted_iota(jnp.int32, (slot_rows, lanes), 0)
    slot = jnp.zeros((slot_rows, lanes), jnp.float32)
    per_image = channels // lanes
    for image in range(images_here):
        for index in range(per_image):
            row = grad_shift[image][:, index * lanes : (index + 1) * lanes]
            slot = jnp.where(
                slot_place == image * per_image + index, jnp.broadcast_to(row, slot.shape), slot
            )
        slot = jnp.where(
            slot_place == images_here * per_image + image,
            own_levels[image].astype(jnp.float32),
            slot,
        )
    s.slots[pl.ds(pl.multiple_of(device * slot_rows, slot_rows), slot_rows), :] = slot
    slots_copy(0).start()

    reduce_mix.finish(0, 0)
    reduce_mix.start(1, 0)
    slots_copy(0).wait_recv()
    slots_copy(1).start()

    share_act_two.wait_recv()
    share_grad_two.wait_recv()
    weigh(
        s.spread_two, half_two, s.act_two, s.act_two_far, s.grad_two_far, s.blocks_two, spots_two
    )
    for part in range(parts):
        reduce_two.start(0, part)

    s.delta[...] = convolve_back(s.spread_one, s.conv_one_here)

    def put_input(image, step, grad, carry):
        total = grad + s.grad_middle[flat_at(image, step), :]
        s.leaving_grad[image, at(step), :] = total.astype(jnp.bfloat16)
        return carry

    grad_gain_one, grad_shift_one, _ = swish_norm_back(
        load_input, center_one, rate_one, gain_one, shift_one, put_input, 0
    )
    swap_start(scatter_copy, scatter_own, 3, s.leaving_grad, s.input_grad)

    sums = dict(
        gain_one=grad_gain_one,
        shift_one=grad_shift_one,
        bias_one=grad_bias_one,
        gain_two=grad_gain_two,
        shift_two=grad_shift_two,
        bias_two=grad_bias_two,
        gain_three=grad_gain_three,
        shift_three=grad_shift_three,
        query_bias=grad_query_bias,
        value_bias=grad_value_bias,
        out_bias=grad_out_bias,
    )
    rows = [sums[name] for name in SUMS]
    s.small_sum[0, 0:8, :] = stack_rows(rows[:8])
    s.small_sum[0, 8:16, :] = stack_rows(rows[8:])
    small_copy(0).start()

    for part in range(parts):
        reduce_two.finish(0, part)
        reduce_two.start(1, part)
    share_act_one.wait_recv()
    share_grad_one.wait_recv()
    weigh(
        s.spread_one, half_one, s.act_one, s.act_one_far, s.grad_one_far, s.blocks_one, spots_one
    )
    for part in range(parts):
        reduce_one.start(0, part)

    reduce_mix.finish(1, 0)
    reduce_mix.start(2, 0)
    slots_copy(1).wait_recv()
    slots_copy(2).start()
    small_finish(0)
    small_copy(1).start()
    for part in range(parts):
        reduce_one.finish(0, part)
        reduce_one.start(1, part)
    for stage in range(1, bits):
        for part in range(parts):
            reduce_two.finish(stage, part)
            if stage + 1 < bits:
                reduce_two.start(stage + 1, part)
        if stage + 1 <= bits:
            reduce_mix.finish(stage + 1, 0)
            if stage + 2 <= bits:
                reduce_mix.start(stage + 2, 0)
        slots_copy(stage + 1).wait_recv()
        if stage + 2 <= bits:
            slots_copy(stage + 2).start()
        small_finish(stage)
        small_copy(stage + 1).start()
        for part in range(parts):
            reduce_one.finish(stage, part)
            if stage + 1 < bits:
                reduce_one.start(stage + 1, part)
    small_finish(bits)
    end_two = last_copy(4, s.fin_two, s.last_two, half_two, bit_two)
    end_one = last_copy(5, s.fin_one, s.last_one, half_one, bit_one)
    end_two.start()
    end_one.start()
    s.sums[...] = s.small_sum[bits + 1]
    s.slots_out[...] = s.slots[...]
    settle(end_two, s.sum_two, s.last_two, half_two, s.share_two)
    settle(end_one, s.sum_one, s.last_one, half_one, s.share_one)
    swap_arrive(scatter_copy, scatter_own, 2, s.leaving, s.output)
    swap_arrive(scatter_copy, scatter_own, 3, s.leaving_grad, s.input_grad)

    swap_drain(gather_copy, 0, s.images, s.arrived)
    swap_drain(gather_copy, 1, s.cotangent, s.upstream)
    swap_drain(scatter_copy, 2, s.leaving, s.output)
    swap_drain(scatter_copy, 3, s.leaving_grad, s.input_grad)
    for copy in (share_act_one, share_act_two, share_grad_two, share_grad_one, end_two, end_one):
        copy.wait_send()
    for reduction in (reduce_mix, reduce_two, reduce_one):
        reduction.drain()
    for stage in range(bits + 1):
        small_copy(stage).wait_send()
        slots_copy(stage).wait_send()


def last_kernel(names, table_rows, *refs):
    s = types.SimpleNamespace(**dict(zip(names, refs, strict=True)))
    device = lax.axis_index("wide") * lax.axis_size("rep") + lax.axis_index("rep")
    moves = [
        pltpu.make_async_copy(s.output_in, s.output, s.sems.at[0]),
        pltpu.make_async_copy(s.input_grad_in, s.input_grad, s.sems.at[1]),
    ]
    for move in moves:
        move.start()
    lanes = s.slots.shape[1]
    channels = s.embed_weight.shape[0]
    per_image = channels // lanes

    def flat(target, rows, first=0):
        count = rows.shape[0]
        width = rows.shape[1] // lanes
        for index in range(width):
            target[pl.ds(first + index, count, stride=width), :] = rows[
                :, index * lanes : (index + 1) * lanes
            ]

    flat(s.conv_one, s.share_one[...])
    flat(s.conv_two, s.share_two[...])
    mix_rows = s.share_mix.shape[0] // 4
    for index, target in enumerate((s.query, s.key, s.value, s.out)):
        flat(target, s.share_mix[index * mix_rows : (index + 1) * mix_rows, :])
    for index, name in enumerate(SUMS):
        getattr(s, "sum_" + name)[...] = s.sums[index : index + 1, :]
    s.sum_embed_bias[...] = s.sums[SUMS.index("bias_one") : SUMS.index("bias_one") + 1, :]

    slot_rows = 16
    devices = s.slots.shape[0] // slot_rows
    images_here = 2

    def every(index):
        return s.slots[pl.ds(index, devices, stride=slot_rows), :]

    de = jnp.concatenate(
        [
            jnp.concatenate([every(image * per_image + j) for j in range(per_image)], axis=1)
            for image in range(images_here)
        ],
        axis=0,
    )
    levels = jnp.concatenate(
        [every(images_here * per_image + image) for image in range(images_here)], axis=0
    ).astype(jnp.int32)
    padded_rows = s.noise_table.shape[0]
    entry = lax.broadcasted_iota(jnp.int32, (levels.shape[0], padded_rows), 1)
    hit = jnp.where(entry == levels[:, 0:1], 1.0, 0.0).astype(jnp.bfloat16)
    embedded = matmul(hit, s.noise_table[...])
    exact = dict(preferred_element_type=jnp.float32, precision=lax.Precision.HIGHEST)
    own_rows = s.embed.shape[0] * lanes // channels
    s.product[...] = lax.dot_general(embedded, de, (((0,), (0,)), ((), ())), **exact)
    flat(s.embed, s.product[pl.ds(pl.multiple_of(device * own_rows, own_rows), own_rows), :])
    grad_rows = lax.dot_general(
        de, s.embed_weight[...].astype(jnp.float32), (((1,), (1,)), ((), ())), **exact
    )
    half = channels // 2
    halves = s.table.shape[0] * lanes // half
    wide = -(-halves // 128) * 128
    spot = lax.broadcasted_iota(jnp.int32, (levels.shape[0], wide), 1) + device * halves
    total = jnp.zeros((wide, half), jnp.float32)
    for side in range(2):
        pick = jnp.where(2 * levels[:, 0:1] + side == spot, 1.0, 0.0)
        total = total + lax.dot_general(
            pick, grad_rows[:, side * half : (side + 1) * half], (((0,), (0,)), ((), ())), **exact
        )
    flat(s.table, total[:halves])
    for move in moves:
        move.wait()


def fused_device(*operands):
    given = dict(zip(ARGUMENTS, operands, strict=True))
    ranks = lax.axis_size("wide")
    bits = (ranks - 1).bit_length()
    images = given["images"]
    images_rep, piece, channels = images.shape
    images_here, pixels = images_rep // ranks, piece * ranks
    flat_rows = images_here * pixels
    half = channels // 2
    devices = ranks * 2
    table_rows = given["noise_table"].shape[0]
    padded_rows = -(-table_rows // 128) * 128
    conv_rows = given["conv_one"].shape[0] // devices
    mix_rows = 4 * channels // devices
    low, full = jnp.bfloat16, jnp.float32
    parts = 3 if conv_rows % 48 == 0 else 1

    def struct(shape, kind):
        return jax.ShapeDtypeStruct(shape, kind)

    outputs = dict(
        output=struct(images.shape, low),
        input_grad=struct(images.shape, low),
        share_one=struct((conv_rows, channels), full),
        share_two=struct((conv_rows, channels), full),
        share_mix=struct((mix_rows, channels), full),
        sums=struct((16, channels), full),
        slots_out=struct((devices * 16, 128), full),
    )
    flat_low, flat_full = (flat_rows, channels), (flat_rows, channels)
    padded = pixels + 2 * SIDE
    scratch = dict(
        noise_table_here=pltpu.VMEM((padded_rows, channels), low),
        embed_weight_here=pltpu.VMEM((channels, channels), low),
        conv_one_here=pltpu.VMEM(given["conv_one"].shape, low),
        conv_two_here=pltpu.VMEM(given["conv_two"].shape, low),
        query_weight_here=pltpu.VMEM((channels, channels), low),
        key_weight_here=pltpu.VMEM((channels, channels), low),
        value_weight_here=pltpu.VMEM((channels, channels), low),
        out_weight_here=pltpu.VMEM((channels, channels), low),
        arrived=pltpu.VMEM((images_here, pixels, channels), low),
        upstream=pltpu.VMEM((images_here, pixels, channels), low),
        leaving=pltpu.VMEM((images_here, pixels, channels), low),
        leaving_grad=pltpu.VMEM((images_here, pixels, channels), low),
        spread_act=pltpu.VMEM((images_here, padded, 3 * channels), low),
        spread_two=pltpu.VMEM((images_here, padded, 3 * channels), low),
        spread_one=pltpu.VMEM((images_here, padded, 3 * channels), low),
        spread_far=pltpu.VMEM((images_here, padded, 3 * half), low),
        hidden=pltpu.VMEM(flat_full, full),
        middle=pltpu.VMEM(flat_full, full),
        delta=pltpu.VMEM(flat_full, full),
        grad_middle=pltpu.VMEM(flat_full, full),
        probs=pltpu.VMEM((flat_rows, pixels), full),
        grad_one_far=pltpu.VMEM((flat_rows, half), low),
        grad_two_far=pltpu.VMEM((flat_rows, half), low),
        small_sum=pltpu.VMEM((bits + 2, 16, channels), full),
        small_land=pltpu.VMEM((bits + 1, 16, channels), full),
        slots=pltpu.VMEM((devices * 16, 128), full),
        load_sem=pltpu.SemaphoreType.DMA((8,)),
        swap_send=pltpu.SemaphoreType.DMA((4, ranks)),
        swap_recv=pltpu.SemaphoreType.DMA((4, ranks)),
        swap_own=pltpu.SemaphoreType.DMA((4,)),
        share_send=pltpu.SemaphoreType.DMA((6,)),
        share_recv=pltpu.SemaphoreType.DMA((6,)),
        small_send=pltpu.SemaphoreType.DMA((bits + 1,)),
        small_recv=pltpu.SemaphoreType.DMA((bits + 1,)),
        slots_send=pltpu.SemaphoreType.DMA((bits + 1,)),
        slots_recv=pltpu.SemaphoreType.DMA((bits + 1,)),
    )
    for name in ("act_one", "act_two", "act_one_far", "act_two_far", "normed", "query", "key", "value", "mixed", "grad_mixed", "grad_query", "grad_key", "grad_value", "grad_one", "grad_two"):
        scratch[name] = pltpu.VMEM(flat_low, low)
    for name in ("one", "two"):
        scratch["blocks_" + name] = pltpu.VMEM((ranks, 2, conv_rows, half), low)
        for stage in range(bits):
            scratch[f"land_{name}_{stage}"] = pltpu.VMEM((ranks >> stage, conv_rows, half), low)
        for stage in range(bits - 1):
            scratch[f"kept_{name}_{stage}"] = pltpu.VMEM((ranks >> stage, conv_rows, half), low)
        scratch["sum_" + name] = pltpu.VMEM((2, conv_rows, half), full)
        scratch["fin_" + name] = pltpu.VMEM((2, conv_rows, half), low)
        scratch["last_" + name] = pltpu.VMEM((conv_rows, half), low)
        scratch["reduce_send_" + name] = pltpu.SemaphoreType.DMA((bits, parts))
        scratch["reduce_recv_" + name] = pltpu.SemaphoreType.DMA((bits, parts))
    scratch["blocks_mix"] = pltpu.VMEM((ranks, 2, mix_rows, channels), low)
    for stage in range(bits + 1):
        scratch[f"land_mix_{stage}"] = pltpu.VMEM((ranks >> stage, mix_rows, channels), low)
    for stage in range(bits):
        scratch[f"kept_mix_{stage}"] = pltpu.VMEM((ranks >> stage, mix_rows, channels), low)
    scratch["reduce_send_mix"] = pltpu.SemaphoreType.DMA((bits + 1, 1))
    scratch["reduce_recv_mix"] = pltpu.SemaphoreType.DMA((bits + 1, 1))

    in_hbm = INPUTS[:10]
    in_specs = [pl.BlockSpec(memory_space=pl.ANY)] * len(in_hbm)
    in_specs.append(pl.BlockSpec(memory_space=pltpu.SMEM))
    in_specs.extend([pl.BlockSpec(memory_space=pltpu.VMEM)] * (len(INPUTS) - len(in_hbm) - 1))
    in_vmem = pl.BlockSpec(memory_space=pltpu.VMEM)
    anywhere = pl.BlockSpec(memory_space=pl.ANY)
    names = tuple(INPUTS) + tuple(outputs) + tuple(scratch)
    arrays = [given[name] for name in INPUTS[:11]] + [
        given[name].reshape(1, channels) for name in INPUTS[11:]
    ]
    made = pl.pallas_call(
        functools.partial(fused_kernel, names, ranks, table_rows),
        out_shape=tuple(outputs.values()),
        in_specs=in_specs,
        out_specs=(anywhere, anywhere) + (in_vmem,) * (len(outputs) - 2),
        scratch_shapes=list(scratch.values()),
        compiler_params=pltpu.CompilerParams(
            collective_id=0, has_side_effects=True, vmem_limit_bytes=63 << 20
        ),
        name="block",
    )(*arrays)
    made = dict(zip(outputs, made, strict=True))

    share = given["embed_weight"].size // devices // 128
    finals = dict(
        output=struct(images.shape, low),
        input_grad=struct(images.shape, low),
        table=struct((given["noise_table"].size // devices // 128, 128), full),
        conv_one=struct((conv_rows * channels // 128, 128), full),
        conv_two=struct((conv_rows * channels // 128, 128), full),
        embed=struct((share, 128), full),
        query=struct((share, 128), full),
        key=struct((share, 128), full),
        value=struct((share, 128), full),
        out=struct((share, 128), full),
    )
    for name in ("gain_one", "shift_one", "bias_one", "embed_bias", "gain_two", "shift_two", "bias_two", "gain_three", "shift_three", "query_bias", "value_bias", "out_bias"):
        finals["sum_" + name] = struct((1, channels), full)
    sources = dict(
        output_in=made["output"],
        input_grad_in=made["input_grad"],
        share_one=made["share_one"],
        share_two=made["share_two"],
        share_mix=made["share_mix"],
        sums=made["sums"],
        slots=made["slots_out"],
        noise_table=given["noise_table"],
        embed_weight=given["embed_weight"],
    )
    names = tuple(sources) + tuple(finals) + ("product", "sems")
    results = pl.pallas_call(
        functools.partial(last_kernel, names, table_rows),
        out_shape=tuple(finals.values()),
        in_specs=[anywhere, anywhere] + [in_vmem] * (len(sources) - 2),
        out_specs=(anywhere, anywhere) + (in_vmem,) * (len(finals) - 2),
        scratch_shapes=[
            pltpu.VMEM((channels, channels), full),
            pltpu.SemaphoreType.DMA((2,)),
        ],
        compiler_params=pltpu.CompilerParams(vmem_limit_bytes=32 << 20),
        name="finish",
    )(*sources.values())
    return tuple(results[:2]) + tuple(member.reshape(-1) for member in results[2:])


ARGUMENTS = ("images", "cotangent", "levels", "noise_table", "gain_one", "shift_one", "conv_one", "bias_one", "embed_weight", "embed_bias", "gain_two", "shift_two", "conv_two", "bias_two", "gain_three", "shift_three", "query_weight", "query_bias", "key_weight", "value_weight", "value_bias", "out_weight", "out_bias")


def per_device(*operands):
    given = dict(zip(ARGUMENTS, operands, strict=True))
    ranks, cores = lax.axis_size("wide"), lax.axis_size("rep")
    images_rep, piece, channels = given["images"].shape
    devices = ranks * cores
    conv_rows = given["conv_one"].shape[0]
    fits = (
        cores == 2
        and ranks >= 8
        and ranks & (ranks - 1) == 0
        and images_rep == 2 * ranks
        and piece % 16 == 0
        and conv_rows % (devices * 16) == 0
        and channels % (devices * 16) == 0
        and given["noise_table"].size % (devices * channels // 2) == 0
    )
    return fused_device(*operands) if fits else plain_device(*operands)


def solution(mesh):
    in_specs = (
        P("rep", "wide", None),
        P("rep", "wide", None),
        P("rep"),
        P(),
        P(),
        P(),
        P(),
        P(),
        P(),
        P(),
        P(),
        P(),
        P(),
        P(),
        P(),
        P(),
        P(),
        P(),
        P(),
        P(),
        P(),
        P(),
        P(),
    )
    out_specs = (
        P("rep", "wide", None),
        P("rep", "wide", None),
        P(("wide", "rep")),
        P(("wide", "rep")),
        P(("wide", "rep")),
        P(("wide", "rep")),
        P(("wide", "rep")),
        P(("wide", "rep")),
        P(("wide", "rep")),
        P(("wide", "rep")),
        P(),
        P(),
        P(),
        P(),
        P(),
        P(),
        P(),
        P(),
        P(),
        P(),
        P(),
        P(),
    )
    return jax.shard_map(
        per_device, mesh=mesh, in_specs=in_specs, out_specs=out_specs, check_vma=False
    )
```

```python
import functools
import types

import jax
import jax.numpy as jnp
from jax import lax
from jax.experimental import pallas as pl
from jax.experimental.pallas import tpu as pltpu
from jax.sharding import PartitionSpec as P

GROUPS = 32
SIDE = 16
MESH = pl.DeviceIdType.MESH
CHUNK = 64


epsilon = 1e-05
highest = lax.Precision.HIGHEST


def swish(field):
    return field * jax.nn.sigmoid(field)


def group_norm(field, norm_gain, norm_shift):
    images_here = field.shape[0]
    channels = field.shape[2]
    grouped = field.reshape(images_here, field.shape[1], GROUPS, channels // GROUPS)
    center = jnp.mean(grouped, axis=(1, 3), keepdims=True)
    spread = grouped - center
    variance = jnp.mean(spread * spread, axis=(1, 3), keepdims=True)
    return (spread * lax.rsqrt(variance + epsilon)).reshape(field.shape) * norm_gain + norm_shift


def norm_swish(field, norm_gain, norm_shift):
    return swish(group_norm(field, norm_gain, norm_shift))


def matmul(left, right):
    return jnp.dot(left, right, preferred_element_type=jnp.float32)


def contract_rows(left, right):
    return lax.dot_general(
        left, right, (((0,), (0,)), ((), ())), preferred_element_type=jnp.float32
    )


def against(left, right):
    return lax.dot_general(
        left, right, (((1,), (1,)), ((), ())), preferred_element_type=jnp.float32
    )


def patches(activation):
    images_here = activation.shape[0]
    grid = activation.reshape(images_here, SIDE, SIDE, activation.shape[2])
    padded = jnp.pad(grid, ((0, 0), (1, 1), (1, 1), (0, 0)))
    pieces = [
        padded[
            :, kernel_tap // 3 : kernel_tap // 3 + SIDE, kernel_tap % 3 : kernel_tap % 3 + SIDE, :
        ]
        for kernel_tap in range(9)
    ]
    return jnp.concatenate(pieces, axis=-1).reshape(images_here * SIDE * SIDE, -1)


def unpatch(columns, images_here):
    channels = columns.shape[1] // 9
    grid = columns.reshape(images_here, SIDE, SIDE, 9, channels)
    summed = jnp.zeros((images_here, SIDE + 2, SIDE + 2, channels), jnp.float32)
    for kernel_tap in range(9):
        row_off = kernel_tap // 3
        col_off = kernel_tap % 3
        summed = summed + jnp.pad(
            grid[:, :, :, kernel_tap, :],
            ((0, 0), (row_off, 2 - row_off), (col_off, 2 - col_off), (0, 0)),
        )
    return summed[:, 1 : SIDE + 1, 1 : SIDE + 1, :].reshape(images_here, SIDE * SIDE, channels)


def plain_device(
    images,
    cotangent,
    levels,
    noise_table,
    gain_one,
    shift_one,
    conv_one,
    bias_one,
    embed_weight,
    embed_bias,
    gain_two,
    shift_two,
    conv_two,
    bias_two,
    gain_three,
    shift_three,
    query_weight,
    query_bias,
    key_weight,
    value_weight,
    value_bias,
    out_weight,
    out_bias,
):
    arrived, upstream = (
        lax.all_to_all(images, "wide", split_axis=0, concat_axis=1, tiled=True),
        lax.all_to_all(cotangent, "wide", split_axis=0, concat_axis=1, tiled=True),
    )
    images_here = arrived.shape[0]
    pixels = arrived.shape[1]
    channels = arrived.shape[2]
    flat_rows = images_here * pixels
    score_scale = channels ** (-0.5)
    table_rows = noise_table.shape[0]
    offset = lax.axis_index("wide") * images_here
    own_levels = lax.dynamic_slice_in_dim(levels, offset, images_here)
    selector = own_levels[:, None] == jnp.arange(table_rows, dtype=jnp.int32)[None, :]
    embedded = matmul(selector.astype(jnp.bfloat16), noise_table).astype(jnp.bfloat16)
    embed_shift = matmul(embedded, embed_weight) + embed_bias
    inputs = arrived.astype(jnp.float32)
    act_one, back_one = jax.vjp(norm_swish, inputs, gain_one, shift_one)
    cols_one = patches(act_one.astype(jnp.bfloat16))
    hidden_one = (matmul(cols_one, conv_one) + bias_one).reshape(images_here, pixels, channels)
    hidden_one = hidden_one + embed_shift[:, None, :]
    act_two, back_two = jax.vjp(norm_swish, hidden_one, gain_two, shift_two)
    cols_two = patches(act_two.astype(jnp.bfloat16))
    branch_out = matmul(cols_two, conv_two) + bias_two
    middle = inputs + branch_out.reshape(images_here, pixels, channels)
    normed, back_three = jax.vjp(group_norm, middle, gain_three, shift_three)
    normed_low = normed.astype(jnp.bfloat16).reshape(flat_rows, channels)
    query_block = (matmul(normed_low, query_weight) + query_bias).astype(jnp.bfloat16)
    key_block = matmul(normed_low, key_weight).astype(jnp.bfloat16)
    value_block = (matmul(normed_low, value_weight) + value_bias).astype(jnp.bfloat16)
    query_block = query_block.reshape(images_here, pixels, channels)
    key_block = key_block.reshape(images_here, pixels, channels)
    value_block = value_block.reshape(images_here, pixels, channels)
    scores = (
        jnp.einsum("npc,nqc->npq", query_block, key_block, preferred_element_type=jnp.float32)
        * score_scale
    )
    row_top = jnp.max(scores, axis=-1, keepdims=True)
    exponent = jnp.exp(scores - row_top)
    row_total = jnp.sum(exponent, axis=-1, keepdims=True)
    probs_low = (exponent / row_total).astype(jnp.bfloat16)
    log_total = row_top + jnp.log(row_total)
    mixed = jnp.einsum("npq,nqc->npc", probs_low, value_block, preferred_element_type=jnp.float32)
    mixed_low = mixed.astype(jnp.bfloat16).reshape(flat_rows, channels)
    result = middle.reshape(flat_rows, channels) + matmul(mixed_low, out_weight) + out_bias
    grad_out = upstream.reshape(flat_rows, channels)
    grad_out_bias = jnp.sum(grad_out.astype(jnp.float32), axis=0)
    grad_out_weight = contract_rows(mixed_low, grad_out)
    grad_mixed = (
        against(grad_out, out_weight).astype(jnp.bfloat16).reshape(images_here, pixels, channels)
    )
    scores_again = (
        jnp.einsum("npc,nqc->npq", query_block, key_block, preferred_element_type=jnp.float32)
        * score_scale
    )
    probs = jnp.exp(scores_again - log_total)
    probs_again = probs.astype(jnp.bfloat16)
    grad_probs = jnp.einsum(
        "npc,nqc->npq", grad_mixed, value_block, preferred_element_type=jnp.float32
    )
    grad_values = jnp.einsum(
        "npq,npc->nqc", probs_again, grad_mixed, preferred_element_type=jnp.float32
    ).astype(jnp.bfloat16)
    grad_scores = probs * (grad_probs - jnp.sum(grad_probs * probs, axis=-1, keepdims=True))
    grad_scores = grad_scores.astype(jnp.bfloat16)
    grad_query = (
        (
            jnp.einsum("npq,nqc->npc", grad_scores, key_block, preferred_element_type=jnp.float32)
            * score_scale
        )
        .astype(jnp.bfloat16)
        .reshape(flat_rows, channels)
    )
    grad_keys = (
        (
            jnp.einsum("npq,npc->nqc", grad_scores, query_block, preferred_element_type=jnp.float32)
            * score_scale
        )
        .astype(jnp.bfloat16)
        .reshape(flat_rows, channels)
    )
    grad_values = grad_values.reshape(flat_rows, channels)
    grad_query_weight = contract_rows(normed_low, grad_query)
    grad_key_weight = contract_rows(normed_low, grad_keys)
    grad_value_weight = contract_rows(normed_low, grad_values)
    grad_query_bias = jnp.sum(grad_query.astype(jnp.float32), axis=0)
    grad_value_bias = jnp.sum(grad_values.astype(jnp.float32), axis=0)
    grad_normed = against(grad_query, query_weight) + against(grad_keys, key_weight)
    grad_normed = grad_normed + against(grad_values, value_weight)
    grad_middle, grad_gain_three, grad_shift_three = back_three(
        grad_normed.reshape(images_here, pixels, channels)
    )
    grad_middle = grad_middle + upstream.astype(jnp.float32)
    grad_branch = grad_middle.astype(jnp.bfloat16).reshape(flat_rows, channels)
    grad_bias_two = jnp.sum(grad_branch.astype(jnp.float32), axis=0)
    grad_conv_two = contract_rows(cols_two, grad_branch)
    grad_act_two = unpatch(against(grad_branch, conv_two), images_here)
    grad_hidden, grad_gain_two, grad_shift_two = back_two(grad_act_two)
    grad_hidden_low = grad_hidden.astype(jnp.bfloat16)
    hidden_rows = grad_hidden_low.reshape(flat_rows, channels)
    grad_bias_one = jnp.sum(hidden_rows.astype(jnp.float32), axis=0)
    grad_conv_one = contract_rows(cols_one, hidden_rows)
    grad_shift = jnp.sum(grad_hidden_low.astype(jnp.float32), axis=1)
    grad_embed_bias = jnp.sum(grad_shift, axis=0)
    grad_embed_weight = jnp.dot(embedded.astype(jnp.float32).T, grad_shift, precision=highest)
    embed_float = embed_weight.astype(jnp.float32)
    grad_act_one = unpatch(against(hidden_rows, conv_one), images_here)
    grad_input_part, grad_gain_one, grad_shift_one = back_one(grad_act_one)
    grad_input = grad_middle + grad_input_part
    output_back, input_back = (
        lax.all_to_all(
            result.reshape(images_here, pixels, channels).astype(jnp.bfloat16),
            "wide",
            split_axis=1,
            concat_axis=0,
            tiled=True,
        ),
        lax.all_to_all(
            grad_input.astype(jnp.bfloat16), "wide", split_axis=1, concat_axis=0, tiled=True
        ),
    )
    wide_count = lax.axis_size("wide")
    rep_count = lax.axis_size("rep")
    device_count = wide_count * rep_count
    weight_grads = (
        grad_conv_one,
        grad_conv_two,
        grad_embed_weight,
        grad_query_weight,
        grad_key_weight,
        grad_value_weight,
        grad_out_weight,
    )
    grad_embedded = jnp.dot(grad_shift, embed_float.T, precision=highest)
    grad_table = jnp.dot(selector.astype(jnp.float32).T, grad_embedded, precision=highest)
    members = (grad_table,) + weight_grads
    widths = [member.size // device_count for member in members]
    packed = jnp.concatenate([member.reshape(device_count, -1) for member in members], axis=1)
    packed = lax.psum_scatter(packed, ("wide", "rep"), scatter_dimension=0, tiled=True)
    packed = packed.reshape(-1)
    large_grads = []
    start_at = 0
    for width in widths:
        large_grads.append(packed[start_at : start_at + width])
        start_at = start_at + width
    large_grads = tuple(large_grads)
    small_grads = lax.psum(
        (
            grad_gain_one,
            grad_shift_one,
            grad_bias_one,
            grad_embed_bias,
            grad_gain_two,
            grad_shift_two,
            grad_bias_two,
            grad_gain_three,
            grad_shift_three,
            grad_query_bias,
            grad_value_bias,
            grad_out_bias,
        ),
        ("wide", "rep"),
    )
    return (output_back, input_back) + large_grads + tuple(small_grads)


def by_rows(left, right):
    return lax.dot_general(
        left, right, (((0,), (0,)), ((), ())), preferred_element_type=jnp.float32
    )


def group_sum(rows, same_group):
    width = same_group.shape[0]
    first = rows.astype(jnp.bfloat16).astype(jnp.float32)
    rest = rows - first
    second = rest.astype(jnp.bfloat16).astype(jnp.float32)
    terms = (first, second, rest - second)
    spans = [slice(start, start + width) for start in range(0, rows.shape[1], width)]
    stacked = jnp.concatenate([term[:, span] for span in spans for term in terms], axis=0)
    summed = matmul(stacked.astype(jnp.bfloat16), same_group)
    parts = [summed[24 * k : 24 * k + 24] for k in range(len(spans))]
    return jnp.concatenate([part[0:8] + part[8:16] + part[16:24] for part in parts], axis=1)


def stack_rows(members):
    shape = (8, members[0].shape[1])
    place = lax.broadcasted_iota(jnp.int32, shape, 0)
    stacked = jnp.zeros(shape, jnp.float32)
    for index, member in enumerate(members):
        stacked = jnp.where(place == index, jnp.broadcast_to(member, shape), stacked)
    return stacked


def sigmoid(field):
    return 0.5 + 0.5 * jnp.tanh(0.5 * field)


SUMS = tuple(
    dict(
        gain_one=0,
        shift_one=0,
        bias_one=0,
        gain_two=0,
        shift_two=0,
        bias_two=0,
        gain_three=0,
        shift_three=0,
        query_bias=0,
        value_bias=0,
        out_bias=0,
    )
)
GIVEN_BACK = SUMS[:3] + SUMS[2:]


class Flight:
    def __init__(self, flights, make, offsets=None, whole=None, own=None):
        self.flights, self.make, self.offsets, self.own = flights, make, offsets, own
        self.whole = make if whole is None else whole
        self.arrived = self.left = False

    def start(self):
        if self.offsets is None:
            self.make().start()
        else:

            def go(offset, carry):
                self.make(offset).start()
                return carry

            lax.fori_loop(*self.offsets, go, 0)
        if self.own is not None:
            self.own().start()
        self.flights.append(self)
        return self

    def arrive(self):
        self.whole().wait_recv()
        if self.own is not None:
            self.own().wait()
        self.arrived = True

    def leave(self):
        self.whole().wait_send()
        self.left = True

    def land(self):
        if not self.arrived:
            self.arrive()
        if not self.left:
            self.leave()


class Reduce:
    def __init__(self, flights, place, blocks, bits, landing, kept, send, recv, last):
        self.flights, self.place = flights, place
        self.blocks, self.bits, self.last = blocks, bits, last
        self.landing, self.kept, self.send, self.recv = landing, kept, send, recv
        self.rows = blocks.shape[2]
        self.parts = send.shape[1]
        self.under_way = {}

    def cut(self, part):
        size = self.rows // self.parts
        return pl.ds(part * size, size)

    def copy(self, stage, part):
        place, rows = self.place, self.cut(part)
        if stage == 0:
            source = self.blocks.at[:, 1 - place.core, rows, :]
            target = place.other_core
        else:
            count = self.blocks.shape[0] >> stage
            bit = self.bits[stage - 1]
            source = self.kept[stage - 1].at[
                pl.ds((1 - place.bit(bit)) * count, count), rows, :
            ]
            target = place.across(bit)
        return pltpu.make_async_remote_copy(
            src_ref=source,
            dst_ref=self.landing[stage].at[:, rows, :],
            send_sem=self.send.at[stage, part],
            recv_sem=self.recv.at[stage, part],
            device_id=target,
            device_id_type=MESH,
        )

    def start(self, stage, part):
        copy = functools.partial(self.copy, stage, part)
        self.under_way[stage, part] = Flight(self.flights, copy).start()

    def step(self, stage, part):
        self.finish(stage, part)
        if stage < len(self.bits):
            self.start(stage + 1, part)

    def finish(self, stage, part):
        place, rows = self.place, self.cut(part)
        self.under_way[stage, part].arrive()
        count = self.blocks.shape[0] >> stage
        if stage == 0:
            own = self.blocks[:, place.core, rows, :]
        else:
            first = place.bit(self.bits[stage - 1]) * count
            own = self.kept[stage - 1][pl.ds(first, count), rows, :]
        landed = self.landing[stage][:, rows, :]
        if stage < len(self.bits):
            self.kept[stage][:, rows, :] = own + landed
        else:
            self.last(rows, own.astype(jnp.float32) + landed.astype(jnp.float32))


class Place:
    def __init__(self, ranks):
        self.ranks = ranks
        self.rank = lax.axis_index("wide")
        self.core = lax.axis_index("rep")
        self.other_core = (self.rank, 1 - self.core)

    def bit(self, index):
        return (self.rank // (1 << index)) % 2

    def across(self, index):
        step = 1 << index
        return (self.rank + step - 2 * step * self.bit(index), self.core)


def block_order(ranks, order):
    places = []
    for rank in range(ranks):
        spot = 0
        for bit in order:
            spot = spot * 2 + (rank >> bit) % 2
        places.append(spot)
    return places


def fused_kernel(names, spans, ranks, table_rows, *refs):
    s = types.SimpleNamespace(**dict(zip(names, refs, strict=True)))
    place = Place(ranks)
    bits = (ranks - 1).bit_length()
    far = list(range(2, bits))
    images_here, pixels, channels = s.arrived.shape
    every_image = range(images_here)
    flat_rows = images_here * pixels
    piece = pixels // ranks
    half = channels // 2
    steps = pixels // CHUNK
    score_scale = channels ** (-0.5)
    count_inverse = 1.0 / (pixels * (channels // GROUPS))
    col = lax.broadcasted_iota(jnp.int32, (CHUNK, 1), 0) % SIDE
    flights = []

    def image_rows(image):
        return slice(image * pixels, (image + 1) * pixels)

    barrier = pltpu.get_barrier_semaphore()

    def greet(offset, carry):
        pl.semaphore_signal(
            barrier,
            inc=1,
            device_id=((place.rank + offset) % ranks, place.core),
            device_id_type=MESH,
        )
        return carry

    lax.fori_loop(1, ranks, greet, 0)
    pl.semaphore_signal(barrier, inc=1, device_id=place.other_core, device_id_type=MESH)

    pairs = (
        (s.noise_table, s.noise_table_here.at[pl.ds(0, table_rows), :]),
        (s.embed_weight, s.embed_weight_here),
        (s.conv_one, s.conv_one_here),
        (s.conv_two, s.conv_two_here),
        (s.query_weight, s.query_weight_here),
        (s.key_weight, s.key_weight_here),
        (s.value_weight, s.value_weight_here),
        (s.out_weight, s.out_weight_here),
    )
    loads = []
    for index, (source, target) in enumerate(pairs):
        loads.append(pltpu.make_async_copy(source, target, s.load_sem.at[index]))
        loads[-1].start()
    pl.semaphore_wait(barrier, ranks)

    def gather_copy(slot, source, target, image, offset):
        peer = (place.rank + offset) % ranks
        return pltpu.make_async_remote_copy(
            src_ref=source.at[peer * images_here + image],
            dst_ref=target.at[image, pl.ds(pl.multiple_of(place.rank * piece, 16), piece)],
            send_sem=s.swap_send.at[slot],
            recv_sem=s.swap_recv.at[slot],
            device_id=(peer, place.core),
            device_id_type=MESH,
        )

    def gather_own(slot, source, target, image):
        return pltpu.make_async_copy(
            source.at[place.rank * images_here + image],
            target.at[image, pl.ds(pl.multiple_of(place.rank * piece, 16), piece)],
            s.swap_own.at[slot],
        )

    def scatter_copy(slot, source, target, image, offset):
        peer = (place.rank + offset) % ranks
        return pltpu.make_async_remote_copy(
            src_ref=source.at[image, pl.ds(pl.multiple_of(peer * piece, 16), piece)],
            dst_ref=target.at[place.rank * images_here + image],
            send_sem=s.swap_send.at[slot],
            recv_sem=s.swap_recv.at[slot],
            device_id=(peer, place.core),
            device_id_type=MESH,
        )

    def scatter_own(slot, source, target, image):
        return pltpu.make_async_copy(
            source.at[image, pl.ds(pl.multiple_of(place.rank * piece, 16), piece)],
            target.at[place.rank * images_here + image],
            s.swap_own.at[slot],
        )

    def swap_whole(slot, held, image):
        others = held.at[image, pl.ds(0, pixels - piece)]
        return pltpu.make_async_remote_copy(
            src_ref=others,
            dst_ref=others,
            send_sem=s.swap_send.at[slot],
            recv_sem=s.swap_recv.at[slot],
            device_id=place.across(0),
            device_id_type=MESH,
        )

    def swaps(copy, own, which, source, target, held):
        return [
            Flight(
                flights,
                functools.partial(copy, which * images_here + image, source, target, image),
                (1, ranks),
                functools.partial(swap_whole, which * images_here + image, held, image),
                functools.partial(own, which * images_here + image, source, target, image),
            )
            for image in every_image
        ]

    swap_images = swaps(gather_copy, gather_own, 0, s.images, s.arrived, s.arrived)
    swap_upstream = swaps(gather_copy, gather_own, 1, s.cotangent, s.upstream, s.upstream)
    swap_output = swaps(scatter_copy, scatter_own, 2, s.leaving, s.output, s.leaving)
    swap_grad = swaps(scatter_copy, scatter_own, 3, s.leaving_grad, s.input_grad, s.leaving_grad)
    for image in every_image:
        swap_images[image].start()

    for padded in (s.spread_act, s.spread_two, s.spread_one, s.spread_far):
        for image in every_image:
            edge = jnp.zeros((SIDE, padded.shape[2]), jnp.bfloat16)
            padded[image, 0:SIDE, :] = edge
            padded[image, pixels + SIDE : pixels + 2 * SIDE, :] = edge
    tail = s.noise_table_here.shape[0] - table_rows
    if tail:
        s.noise_table_here[table_rows:, :] = jnp.zeros((tail, channels), jnp.bfloat16)
    own_levels = [s.levels[place.rank * images_here + image] for image in every_image]
    entry = lax.broadcasted_iota(jnp.int32, (8, s.noise_table_here.shape[0]), 1)
    line = lax.broadcasted_iota(jnp.int32, entry.shape, 0)
    selected = jnp.zeros(entry.shape, jnp.float32)
    for image in every_image:
        hit = jnp.where(entry == own_levels[image], 1.0, 0.0)
        selected = jnp.where(line == image, hit, selected)
    loads[0].wait()
    loads[1].wait()
    embedded = matmul(selected.astype(jnp.bfloat16), s.noise_table_here[...])
    embed_shift = matmul(embedded.astype(jnp.bfloat16), s.embed_weight_here[...])
    embed_shift = embed_shift + s.embed_bias[...] + s.bias_one[...]

    def over(image, body, start):
        return lax.fori_loop(0, steps, functools.partial(body, image), start)

    def at(step):
        return pl.ds(pl.multiple_of(step * CHUNK, CHUNK), CHUNK)

    def flat_at(image, step):
        return pl.ds(pl.multiple_of(image * pixels + step * CHUNK, CHUNK), CHUNK)

    def fold(chunk):
        return jnp.sum(chunk.reshape(CHUNK // 8, 8, channels), axis=0)

    none = jnp.zeros((8, channels), jnp.float32)

    def whole(part):
        return jnp.sum(part, axis=0, keepdims=True)

    group_width = s.same_group.shape[0]
    same_group = [
        lax.broadcasted_iota(jnp.int32, (group_width, group_width), axis)
        // (channels // GROUPS)
        for axis in range(2)
    ]
    s.same_group[...] = jnp.where(same_group[0] == same_group[1], 1.0, 0.0).astype(jnp.bfloat16)

    def group_total(row):
        rows = jnp.broadcast_to(row, (8, channels))
        return group_sum(rows, s.same_group[...])[0:1] * count_inverse

    def statistics(load, image):
        def first(image, step, total):
            return total + fold(load(image, step))

        center = group_total(whole(over(image, first, none)))

        def second(image, step, total):
            spread = load(image, step) - center
            return total + fold(spread * spread)

        variance = group_total(whole(over(image, second, none)))
        return center, lax.rsqrt(variance + epsilon)

    def spread_out(target, image, step, chunk, before, after):
        width = chunk.shape[1]
        rows = pl.ds(pl.multiple_of(step * CHUNK + SIDE, SIDE), CHUNK)
        target[image, rows, before * width : (before + 1) * width] = jnp.where(
            col > 0, pltpu.roll(chunk, 1, 0), 0.0
        ).astype(jnp.bfloat16)
        target[image, rows, width : 2 * width] = chunk.astype(jnp.bfloat16)
        target[image, rows, after * width : (after + 1) * width] = jnp.where(
            col < SIDE - 1, pltpu.roll(chunk, CHUNK - 1, 0), 0.0
        ).astype(jnp.bfloat16)

    def activate(load, image, moments, gain, shift, keep):
        center, rate = moments
        slope = rate * gain

        def apply(image, step, carry):
            field = (load(image, step) - center) * slope + shift
            act = field * sigmoid(field)
            spread_out(s.spread_act, image, step, act, 0, 2)
            keep[flat_at(image, step), :] = act.astype(jnp.bfloat16)
            return carry

        over(image, apply, 0)

    def convolve(weight, image):
        total = None
        for row_tap in range(3):
            term = matmul(
                s.spread_act[image, SIDE * row_tap : SIDE * row_tap + pixels, :],
                weight[3 * channels * row_tap : 3 * channels * (row_tap + 1), :],
            )
            total = term if total is None else total + term
        return total

    def tap_rows(row_tap):
        return slice(SIDE * (2 - row_tap), SIDE * (2 - row_tap) + pixels)

    def convolve_back(source, weight, images):
        total = None
        for tap in range(9):
            window = source[
                images, tap_rows(tap // 3), (tap % 3) * channels : (tap % 3 + 1) * channels
            ]
            term = against(
                window.reshape(-1, channels), weight[channels * tap : channels * (tap + 1), :]
            )
            total = term if total is None else total + term
        return total

    def share_copy(slot, source, target, bit):
        def make():
            return pltpu.make_async_remote_copy(
                src_ref=source,
                dst_ref=target,
                send_sem=s.share_send.at[slot],
                recv_sem=s.share_recv.at[slot],
                device_id=place.across(bit),
                device_id_type=MESH,
            )

        return Flight(flights, make)

    bit_one, bit_two = 1, 0
    half_one, half_two = place.bit(bit_one), place.bit(bit_two)

    def shares(which, source, target, bit, mine=None):
        made = []
        for image in every_image:
            rows = pl.ds(image * pixels, pixels)
            lanes_sent = pl.ds(0, channels)
            if mine is not None:
                lanes_sent = pl.ds(pl.multiple_of((1 - mine) * half, half), half)
            made.append(
                share_copy(
                    which * images_here + image,
                    source.at[rows, lanes_sent],
                    target.at[rows, :],
                    bit,
                )
            )
        return made

    share_act_one = shares(0, s.act_one, s.act_one_far, bit_one)
    share_act_two = shares(1, s.act_two, s.act_two_far, bit_two)
    share_grad_two = shares(2, s.grad_two, s.grad_two_far, bit_two, half_two)
    share_grad_one = shares(3, s.grad_one, s.grad_one_far, bit_one, half_one)

    def weigh(spread, mine, act, act_far, grad_far, blocks, spots):
        def unfold(image, step, carry):
            chunk = grad_far[flat_at(image, step), :].astype(jnp.float32)
            spread_out(s.spread_far, image, step, chunk, 2, 0)
            return carry

        for image in every_image:
            over(image, unfold, 0)
        rows_block = blocks.shape[2]
        for tap in range(9):
            rows, side_tap = tap_rows(tap // 3), tap % 3
            near = spread[
                :, rows, pl.ds(pl.multiple_of(side_tap * channels + mine * half, half), half)
            ]
            beyond = s.spread_far[:, rows, side_tap * half : (side_tap + 1) * half]
            product = by_rows(act[...], near.reshape(flat_rows, half)) + by_rows(
                act_far[...], beyond.reshape(flat_rows, half)
            )
            product = product.astype(jnp.bfloat16)
            done = 0
            while done < channels:
                block, inside = divmod(tap * channels + done, rows_block)
                size = min(rows_block - inside, channels - done)
                blocks[spots[block // 2], block % 2, inside : inside + size, :] = product[
                    done : done + size
                ]
                done = done + size

    order_one = [1 - bit_one] + far
    order_two = [1 - bit_two] + far
    order_mix = [0, 1] + far
    spots_one = block_order(ranks, order_one + [bit_one])
    spots_two = block_order(ranks, order_two + [bit_two])
    spots_mix = block_order(ranks, order_mix)

    def put_one(rows, total):
        s.sum_one[:, rows, :] = total
        s.fin_one[:, rows, :] = total.astype(jnp.bfloat16)

    def put_two(rows, total):
        s.sum_two[:, rows, :] = total
        s.fin_two[:, rows, :] = total.astype(jnp.bfloat16)

    def put_mix(rows, total):
        s.share_mix[rows, :] = total[0]

    def staged(ref, first, stages):
        views, start = [], 0
        for stage in range(stages):
            views.append(ref.at[pl.ds(start, first >> stage)])
            start = start + (first >> stage)
        return views

    def reduction(blocks, order, landing, kept, send, recv, put):
        stages = len(order)
        return Reduce(
            flights,
            place,
            blocks,
            order,
            staged(landing, ranks, stages + 1),
            staged(kept, ranks, stages),
            send,
            recv,
            put,
        )

    reduce_one = reduction(
        s.blocks_one,
        order_one,
        s.land_one,
        s.kept_one,
        s.reduce_send_one,
        s.reduce_recv_one,
        put_one,
    )
    reduce_two = reduction(
        s.blocks_two,
        order_two,
        s.land_two,
        s.kept_two,
        s.reduce_send_two,
        s.reduce_recv_two,
        put_two,
    )
    reduce_mix = reduction(
        s.blocks_mix,
        order_mix,
        s.land_mix,
        s.kept_mix,
        s.reduce_send_mix,
        s.reduce_recv_mix,
        put_mix,
    )
    parts = reduce_one.parts

    def settle(flight, sums, target, mine):
        flight.arrive()
        own = sums[mine]
        other = target[...].astype(jnp.float32)
        left = jnp.where(mine == 0, own, other)
        right = jnp.where(mine == 0, other, own)
        return jnp.concatenate([left, right], axis=1)

    def small_copy(stage):
        return pltpu.make_async_remote_copy(
            src_ref=s.small_sum.at[stage],
            dst_ref=s.small_land.at[stage],
            send_sem=s.small_send.at[stage],
            recv_sem=s.small_recv.at[stage],
            device_id=place.other_core if stage == 0 else place.across(stage - 1),
            device_id_type=MESH,
        )

    small = [Flight(flights, functools.partial(small_copy, k)) for k in range(bits + 1)]

    def small_step(stage):
        small[stage].arrive()
        s.small_sum[stage + 1] = s.small_sum[stage] + s.small_land[stage]
        if stage < bits:
            small[stage + 1].start()

    slot_rows = 16
    lanes = s.slots.shape[1]

    def pair_window():
        return s.slots.at[pl.ds(pl.multiple_of(place.rank * 2 * slot_rows, 16), 2 * slot_rows), :]

    def slot_copy():
        first = pl.multiple_of((place.rank * 2 + place.core) * slot_rows, slot_rows)
        window = s.slots.at[pl.ds(first, slot_rows), :]
        return pltpu.make_async_remote_copy(
            src_ref=window,
            dst_ref=window,
            send_sem=s.slots_send.at[0],
            recv_sem=s.slots_recv.at[0],
            device_id=place.other_core,
            device_id_type=MESH,
        )

    def pair_copy(offset):
        return pltpu.make_async_remote_copy(
            src_ref=pair_window(),
            dst_ref=pair_window(),
            send_sem=s.slots_send.at[1],
            recv_sem=s.slots_recv.at[1],
            device_id=((place.rank + offset) % ranks, place.core),
            device_id_type=MESH,
        )

    slots_pair = Flight(flights, slot_copy)
    def pairs_whole():
        others = s.slots.at[pl.ds(0, (ranks - 1) * 2 * slot_rows), :]
        return pltpu.make_async_remote_copy(
            src_ref=others,
            dst_ref=others,
            send_sem=s.slots_send.at[1],
            recv_sem=s.slots_recv.at[1],
            device_id=place.across(0),
            device_id_type=MESH,
        )

    slots_all = Flight(flights, pair_copy, (1, ranks), pairs_whole)

    def load_input(image, step):
        return s.arrived[image, at(step), :].astype(jnp.float32)

    def load_hidden(image, step):
        return s.hidden[flat_at(image, step), :]

    def load_middle(image, step):
        return s.middle[flat_at(image, step), :]

    def load_upstream(image, step):
        return s.upstream[image, at(step), :].astype(jnp.float32)

    def delta_at(image, step):
        return s.delta[flat_at(image, step), :]

    def load_low(ref):
        return lambda image, step: ref[flat_at(image, step), :].astype(jnp.float32)

    gain_one, shift_one = s.gain_one[...], s.shift_one[...]
    gain_two, shift_two = s.gain_two[...], s.shift_two[...]
    gain_three, shift_three = s.gain_three[...], s.shift_three[...]
    moments_one, moments_two, moments_three = [], [], []
    sums = {name: [] for name in SUMS}

    def forward(image):
        rows = image_rows(image)
        swap_images[image].arrive()
        if image == images_here - 1:
            for later in every_image:
                swap_upstream[later].start()
        moments_one.append(statistics(load_input, image))
        activate(load_input, image, moments_one[image], gain_one, shift_one, s.act_one)
        share_act_one[image].start()
        if image == 0:
            loads[2].wait()
        s.hidden[rows, :] = convolve(s.conv_one_here, image) + embed_shift[image : image + 1]
        moments_two.append(statistics(load_hidden, image))
        activate(load_hidden, image, moments_two[image], gain_two, shift_two, s.act_two)
        share_act_two[image].start()
        if image == 0:
            loads[3].wait()
        s.middle[rows, :] = (
            convolve(s.conv_two_here, image)
            + s.bias_two[...]
            + s.arrived[image].astype(jnp.float32)
        )
        moments_three.append(statistics(load_middle, image))
        center, rate = moments_three[image]
        slope = rate * gain_three

        def normalize(image, step, carry):
            field = (load_middle(image, step) - center) * slope + shift_three
            s.normed[flat_at(image, step), :] = field.astype(jnp.bfloat16)
            return carry

        over(image, normalize, 0)
        if image == 0:
            for load in loads[4:]:
                load.wait()
        normed = s.normed[rows, :]
        query = (matmul(normed, s.query_weight_here[...]) + s.query_bias[...]).astype(jnp.bfloat16)
        key = matmul(normed, s.key_weight_here[...]).astype(jnp.bfloat16)
        value = (matmul(normed, s.value_weight_here[...]) + s.value_bias[...]).astype(jnp.bfloat16)
        s.query[rows, :] = query
        s.key[rows, :] = key
        s.value[rows, :] = value
        scores = against(query, key) * score_scale
        exponent = jnp.exp(scores - jnp.max(scores, axis=1, keepdims=True))
        probs = exponent / jnp.sum(exponent, axis=1, keepdims=True)
        s.probs[rows, :] = probs
        mixed = matmul(probs.astype(jnp.bfloat16), value).astype(jnp.bfloat16)
        s.mixed[rows, :] = mixed
        result = s.middle[rows, :] + matmul(mixed, s.out_weight_here[...]) + s.out_bias[...]
        s.leaving[image] = result.astype(jnp.bfloat16)

    def norm_back_terms(gain, shift_sum, gain_sum):
        rows = stack_rows([gain * shift_sum, gain * gain_sum])
        means = group_sum(rows, s.same_group[...]) * count_inverse
        return means[0:1], means[1:2]

    def backward(image):
        rows = image_rows(image)
        swap_upstream[image].arrive()
        probs = s.probs[rows, :]
        query, key, value = s.query[rows, :], s.key[rows, :], s.value[rows, :]
        grad_mixed = against(s.upstream[image], s.out_weight_here[...]).astype(jnp.bfloat16)
        grad_probs = against(grad_mixed, value)
        grad_value = by_rows(probs.astype(jnp.bfloat16), grad_mixed).astype(jnp.bfloat16)
        inner = jnp.sum(grad_probs * probs, axis=1, keepdims=True)
        grad_scores = (probs * (grad_probs - inner)).astype(jnp.bfloat16)
        grad_query = (matmul(grad_scores, key) * score_scale).astype(jnp.bfloat16)
        grad_key = (by_rows(grad_scores, query) * score_scale).astype(jnp.bfloat16)
        s.grad_value[rows, :] = grad_value
        s.grad_query[rows, :] = grad_query
        s.grad_key[rows, :] = grad_key
        s.delta[rows, :] = (
            against(grad_query, s.query_weight_here[...])
            + against(grad_key, s.key_weight_here[...])
            + against(grad_value, s.value_weight_here[...])
        )

        center, rate = moments_three[image]

        def sums_three(image, step, totals):
            grad = delta_at(image, step)
            unit = (load_middle(image, step) - center) * rate
            return totals[0] + fold(grad), totals[1] + fold(grad * unit)

        shift_sum, gain_sum = map(whole, over(image, sums_three, (none, none)))
        sums["gain_three"].append(gain_sum)
        sums["shift_three"].append(shift_sum)
        mean_shift, mean_gain = norm_back_terms(gain_three, shift_sum, gain_sum)

        def back_three(image, step, total):
            unit = (load_middle(image, step) - center) * rate
            grad = rate * (delta_at(image, step) * gain_three - mean_shift - unit * mean_gain)
            grad = grad + load_upstream(image, step)
            s.grad_middle[flat_at(image, step), :] = grad
            low = grad.astype(jnp.bfloat16)
            s.grad_two[flat_at(image, step), :] = low
            low = low.astype(jnp.float32)
            spread_out(s.spread_two, image, step, low, 2, 0)
            return total + fold(low)

        sums["bias_two"].append(whole(over(image, back_three, none)))
        share_grad_two[image].start()

        s.delta[rows, :] = convolve_back(s.spread_two, s.conv_two_here, slice(image, image + 1))

        def put_hidden(image, step, grad, total):
            low = grad.astype(jnp.bfloat16)
            s.grad_one[flat_at(image, step), :] = low
            low = low.astype(jnp.float32)
            spread_out(s.spread_one, image, step, low, 2, 0)
            return total + fold(low)

        gain_sum, shift_sum, total = swish_norm_back(
            load_hidden, image, moments_two[image], gain_two, shift_two, put_hidden, none
        )
        share_grad_one[image].start()
        sums["gain_two"].append(gain_sum)
        sums["shift_two"].append(shift_sum)
        sums["bias_one"].append(whole(total))

    def swish_norm_back(load, image, moments, gain, shift, put, start):
        center, rate = moments

        def totals(image, step, carry):
            unit = (load(image, step) - center) * rate
            field = unit * gain + shift
            gate = sigmoid(field)
            grad = delta_at(image, step) * (gate * (1.0 + field * (1.0 - gate)))
            s.delta[flat_at(image, step), :] = grad
            return carry[0] + fold(grad), carry[1] + fold(grad * unit)

        shift_sum, gain_sum = map(whole, over(image, totals, (none, none)))
        mean_shift, mean_gain = norm_back_terms(gain, shift_sum, gain_sum)

        def back(image, step, carry):
            unit = (load(image, step) - center) * rate
            grad = rate * (delta_at(image, step) * gain - mean_shift - unit * mean_gain)
            return put(image, step, grad, carry)

        return gain_sum, shift_sum, over(image, back, start)

    def backward_input(image):
        def put_input(image, step, grad, carry):
            total = grad + s.grad_middle[flat_at(image, step), :]
            s.leaving_grad[image, at(step), :] = total.astype(jnp.bfloat16)
            return carry

        gain_sum, shift_sum, _ = swish_norm_back(
            load_input, image, moments_one[image], gain_one, shift_one, put_input, 0
        )
        swap_grad[image].start()
        sums["gain_one"].append(gain_sum)
        sums["shift_one"].append(shift_sum)

    mix_rows = s.blocks_mix.shape[2] // 4

    def store_mix(which, product):
        product = product.astype(jnp.bfloat16)
        for rank in range(ranks):
            for core in range(2):
                block = rank * 2 + core
                s.blocks_mix[
                    spots_mix[rank], core, which * mix_rows : (which + 1) * mix_rows, :
                ] = product[block * mix_rows : (block + 1) * mix_rows]

    def weigh_mix():
        upstream = s.upstream[...].reshape(flat_rows, channels)
        normed = s.normed[...]
        store_mix(3, by_rows(s.mixed[...], upstream))
        store_mix(0, by_rows(normed, s.grad_query[...]))
        store_mix(1, by_rows(normed, s.grad_key[...]))
        store_mix(2, by_rows(normed, s.grad_value[...]))

    def column_sums(load):
        def body(image, step, total):
            return total + fold(load(image, step))

        total = none
        for image in every_image:
            total = over(image, body, total)
        return whole(total)

    def fill_slot():
        slot_place = lax.broadcasted_iota(jnp.int32, (slot_rows, lanes), 0)
        slot = jnp.zeros((slot_rows, lanes), jnp.float32)
        for image in every_image:
            for index in range(per_image):
                row = sums["bias_one"][image][:, index * lanes : (index + 1) * lanes]
                slot = jnp.where(
                    slot_place == image * per_image + index,
                    jnp.broadcast_to(row, slot.shape),
                    slot,
                )
            slot = jnp.where(
                slot_place == images_here * per_image + image,
                own_levels[image].astype(jnp.float32),
                slot,
            )
        device = place.rank * 2 + place.core
        s.slots[pl.ds(pl.multiple_of(device * slot_rows, slot_rows), slot_rows), :] = slot

    per_image = channels // lanes

    def flat(first, rows):
        count, width = rows.shape[0], rows.shape[1] // lanes
        for index in range(width):
            s.flat[pl.ds(first + index, count, stride=width), :] = rows[
                :, index * lanes : (index + 1) * lanes
            ]

    def embedding_gradients():
        def every(index):
            return s.slots[pl.ds(index, ranks * 2, stride=slot_rows), :]

        device = place.rank * 2 + place.core
        de = jnp.concatenate(
            [
                jnp.concatenate([every(image * per_image + j) for j in range(per_image)], axis=1)
                for image in every_image
            ],
            axis=0,
        )
        levels = jnp.concatenate(
            [every(images_here * per_image + image) for image in every_image], axis=0
        ).astype(jnp.int32)[:, 0:1]
        entry = lax.broadcasted_iota(
            jnp.int32, (levels.shape[0], s.noise_table_here.shape[0]), 1
        )
        hit = jnp.where(entry == levels, 1.0, 0.0).astype(jnp.bfloat16)
        everywhere = matmul(hit, s.noise_table_here[...])
        exact = dict(preferred_element_type=jnp.float32, precision=lax.Precision.HIGHEST)
        own_rows = channels // (ranks * 2)
        s.product[...] = lax.dot_general(everywhere, de, (((0,), (0,)), ((), ())), **exact)
        first = pl.multiple_of(device * own_rows, own_rows)
        flat(spans["embed"], s.product[pl.ds(first, own_rows), :])
        grad_rows = lax.dot_general(
            de, s.embed_weight_here[...].astype(jnp.float32), (((1,), (1,)), ((), ())), **exact
        )
        halves = table_rows * 2 // (ranks * 2)
        wide = -(-halves // 128) * 128
        spot = lax.broadcasted_iota(jnp.int32, (levels.shape[0], wide), 1) + device * halves
        total = jnp.zeros((wide, half), jnp.float32)
        for side in range(2):
            pick = jnp.where(2 * levels + side == spot, 1.0, 0.0)
            total = total + lax.dot_general(
                pick,
                grad_rows[:, side * half : (side + 1) * half],
                (((0,), (0,)), ((), ())),
                **exact,
            )
        flat(spans["table"], total)

    def start_small():
        sums["query_bias"].append(column_sums(load_low(s.grad_query)))
        sums["value_bias"].append(column_sums(load_low(s.grad_value)))
        sums["out_bias"].append(column_sums(load_upstream))
        rows = [functools.reduce(jnp.add, sums[name]) for name in SUMS]
        s.small_sum[0, 0:8, :] = stack_rows(rows[:8])
        s.small_sum[0, 8:16, :] = stack_rows(rows[8:])
        small[0].start()

    def step_all(reduction, stage):
        for part in range(reduction.parts):
            reduction.step(stage, part)

    for image in every_image:
        forward(image)
    backward(0)
    for image in every_image[1:]:
        backward(image)
    for image in every_image:
        swap_output[image].start()
    fill_slot()
    slots_pair.start()
    weigh_mix()
    reduce_mix.start(0, 0)
    slots_pair.arrive()
    slots_all.start()
    for image in every_image:
        share_act_two[image].arrive()
        share_grad_two[image].arrive()
    weigh(
        s.spread_two, half_two, s.act_two, s.act_two_far, s.grad_two_far, s.blocks_two, spots_two
    )
    for part in range(parts):
        reduce_two.start(0, part)
    reduce_mix.step(0, 0)
    s.delta[...] = convolve_back(s.spread_one, s.conv_one_here, slice(None))
    for image in every_image:
        backward_input(image)
    start_small()
    step_all(reduce_two, 0)
    for image in every_image:
        share_act_one[image].arrive()
        share_grad_one[image].arrive()
    weigh(
        s.spread_one, half_one, s.act_one, s.act_one_far, s.grad_one_far, s.blocks_one, spots_one
    )
    for part in range(parts):
        reduce_one.start(0, part)
    small_step(0)
    step_all(reduce_one, 0)
    slots_all.arrive()
    embedding_gradients()
    reduce_mix.step(1, 0)
    small_step(1)

    reduce_two.step(1, 0)
    reduce_one.step(1, 0)
    reduce_two.step(1, 1)
    reduce_two.step(2, 0)
    reduce_mix.step(2, 0)
    small_step(2)
    reduce_one.step(1, 1)
    reduce_one.step(2, 0)
    reduce_two.step(1, 2)
    reduce_two.step(2, 1)
    reduce_two.step(3, 0)
    reduce_mix.step(3, 0)
    small_step(3)
    reduce_one.step(1, 2)
    reduce_one.step(2, 1)
    reduce_one.step(3, 0)
    reduce_two.step(2, 2)
    reduce_two.step(3, 1)
    reduce_mix.step(4, 0)
    small_step(4)
    s.sums[...] = s.small_sum[bits + 1]
    for index, name in enumerate(dict(query=0, key=0, value=0, out=0)):
        flat(spans[name], s.share_mix[index * mix_rows : (index + 1) * mix_rows, :])
    reduce_one.step(2, 2)
    reduce_one.step(3, 1)
    reduce_two.step(3, 2)
    end_two = share_copy(4 * images_here, s.fin_two.at[1 - half_two], s.last_two, bit_two).start()
    reduce_one.step(3, 2)
    end_one = share_copy(
        4 * images_here + 1, s.fin_one.at[1 - half_one], s.last_one, bit_one
    ).start()
    flat(spans["conv_two"], settle(end_two, s.sum_two, s.last_two, half_two))
    flat(spans["conv_one"], settle(end_one, s.sum_one, s.last_one, half_one))

    for flight in flights:
        flight.land()


def last_kernel(starts, rows, *refs):
    output_in, grad_in, flat_in, sums_in, output, grad = refs[:6]
    flats, sums = refs[6 : 6 + len(starts)], refs[6 + len(starts) : -4]
    output_here, grad_here, flat_here, sems = refs[-4:]
    arrive = [
        pltpu.make_async_copy(output_in, output_here, sems.at[0]),
        pltpu.make_async_copy(grad_in, grad_here, sems.at[1]),
        pltpu.make_async_copy(flat_in, flat_here, sems.at[2]),
    ]
    for move in arrive:
        move.start()
    for row, target in zip(rows, sums, strict=True):
        target[...] = sums_in[row : row + 1, :]
    leave = [
        pltpu.make_async_copy(output_here, output, sems.at[3]),
        pltpu.make_async_copy(grad_here, grad, sems.at[4]),
    ]
    for index, (start, target) in enumerate(zip(starts, flats, strict=True)):
        span = flat_here.at[pl.ds(start, target.shape[0]), :]
        leave.append(pltpu.make_async_copy(span, target, sems.at[5 + index]))
    for index, move in enumerate(arrive):
        move.wait()
        for out in leave[index : index + 1] if index < 2 else leave[2:]:
            out.start()
    for move in leave:
        move.wait()


def fused_device(given):
    ranks = lax.axis_size("wide")
    bits = (ranks - 1).bit_length()
    images = given["images"]
    images_rep, piece, channels = images.shape
    images_here, pixels = images_rep // ranks, piece * ranks
    flat_rows = images_here * pixels
    half = channels // 2
    devices = ranks * 2
    table_rows = given["noise_table"].shape[0]
    padded_rows = -(-table_rows // 128) * 128
    conv_rows = given["conv_one"].shape[0] // devices
    mix_rows = 4 * channels // devices
    low, full = jnp.bfloat16, jnp.float32
    parts = 3
    lanes = 128

    def struct(shape, kind):
        return jax.ShapeDtypeStruct(shape, kind)

    def hold(*shape, kind=low):
        return pltpu.VMEM(shape, kind)

    def semaphores(*shape):
        return pltpu.SemaphoreType.DMA(shape)

    def activations():
        return hold(flat_rows, channels)

    def fields():
        return hold(flat_rows, channels, kind=full)

    def square():
        return hold(channels, channels)

    def images_low():
        return hold(images_here, pixels, channels)

    def flat_span(size, pad=False):
        rows = size // lanes
        return -(-rows // 128) * 128 if pad else rows

    share = channels * channels // devices
    sizes = dict(
        conv_one=flat_span(conv_rows * channels),
        conv_two=flat_span(conv_rows * channels),
        query=flat_span(share),
        key=flat_span(share),
        value=flat_span(share),
        out=flat_span(share),
        embed=flat_span(share),
        table=flat_span(table_rows * channels // devices, True),
    )
    spans, start = {}, 0
    for name, size in sizes.items():
        spans[name] = start
        start = start + size

    outputs = dict(
        output=struct(images.shape, low),
        input_grad=struct(images.shape, low),
        flat=struct((start, lanes), full),
        sums=struct((16, channels), full),
    )
    padded = pixels + 2 * SIDE
    halvings = sum(ranks >> stage for stage in range(bits + 1))
    scratch = dict(
        noise_table_here=hold(padded_rows, channels),
        embed_weight_here=square(),
        conv_one_here=hold(*given["conv_one"].shape),
        conv_two_here=hold(*given["conv_two"].shape),
        query_weight_here=square(),
        key_weight_here=square(),
        value_weight_here=square(),
        out_weight_here=square(),
        arrived=images_low(),
        upstream=images_low(),
        leaving=images_low(),
        leaving_grad=images_low(),
        spread_act=hold(images_here, padded, 3 * channels),
        spread_two=hold(images_here, padded, 3 * channels),
        spread_one=hold(images_here, padded, 3 * channels),
        spread_far=hold(images_here, padded, 3 * half),
        hidden=fields(),
        middle=fields(),
        delta=fields(),
        grad_middle=fields(),
        probs=hold(flat_rows, pixels, kind=full),
        act_one=activations(),
        act_two=activations(),
        act_one_far=activations(),
        act_two_far=activations(),
        normed=activations(),
        query=activations(),
        key=activations(),
        value=activations(),
        mixed=activations(),
        grad_mixed=activations(),
        grad_query=activations(),
        grad_key=activations(),
        grad_value=activations(),
        grad_one=activations(),
        grad_two=activations(),
        grad_one_far=hold(flat_rows, half),
        grad_two_far=hold(flat_rows, half),
        blocks_one=hold(ranks, 2, conv_rows, half),
        blocks_two=hold(ranks, 2, conv_rows, half),
        blocks_mix=hold(ranks, 2, mix_rows, channels),
        land_one=hold(halvings - 1, conv_rows, half),
        land_two=hold(halvings - 1, conv_rows, half),
        land_mix=hold(halvings, mix_rows, channels),
        kept_one=hold(halvings - 3, conv_rows, half),
        kept_two=hold(halvings - 3, conv_rows, half),
        kept_mix=hold(halvings - 1, mix_rows, channels),
        sum_one=hold(2, conv_rows, half, kind=full),
        sum_two=hold(2, conv_rows, half, kind=full),
        fin_one=hold(2, conv_rows, half),
        fin_two=hold(2, conv_rows, half),
        last_one=hold(conv_rows, half),
        last_two=hold(conv_rows, half),
        share_mix=hold(mix_rows, channels, kind=full),
        small_sum=hold(bits + 2, 16, channels, kind=full),
        small_land=hold(bits + 1, 16, channels, kind=full),
        slots=hold(devices * 16, lanes, kind=full),
        product=hold(channels, channels, kind=full),
        same_group=hold(half, half),
        load_sem=semaphores(8),
        swap_send=semaphores(4 * images_here),
        swap_recv=semaphores(4 * images_here),
        swap_own=semaphores(4 * images_here),
        share_send=semaphores(4 * images_here + 2),
        share_recv=semaphores(4 * images_here + 2),
        small_send=semaphores(bits + 1),
        small_recv=semaphores(bits + 1),
        slots_send=semaphores(2),
        slots_recv=semaphores(2),
        reduce_send_one=semaphores(bits, parts),
        reduce_recv_one=semaphores(bits, parts),
        reduce_send_two=semaphores(bits, parts),
        reduce_recv_two=semaphores(bits, parts),
        reduce_send_mix=semaphores(bits + 1, 1),
        reduce_recv_mix=semaphores(bits + 1, 1),
    )

    in_vmem = pl.BlockSpec(memory_space=pltpu.VMEM)
    anywhere = pl.BlockSpec(memory_space=pl.ANY)
    in_smem = pl.BlockSpec(memory_space=pltpu.SMEM)
    arrays, in_specs = {}, []
    for name, value in given.items():
        if value.ndim == 1 and value.dtype == full:
            value = value.reshape(1, channels)
            in_specs.append(in_vmem)
        else:
            in_specs.append(in_smem if value.ndim == 1 else anywhere)
        arrays[name] = value
    names = tuple(arrays) + tuple(outputs) + tuple(scratch)
    output, input_grad, flat, sums = pl.pallas_call(
        functools.partial(fused_kernel, names, spans, ranks, table_rows),
        out_shape=tuple(outputs.values()),
        in_specs=in_specs,
        out_specs=(anywhere, anywhere, in_vmem, in_vmem),
        scratch_shapes=list(scratch.values()),
        compiler_params=pltpu.CompilerParams(
            collective_id=0, has_side_effects=True, vmem_limit_bytes=63 << 20
        ),
        name="block",
    )(*arrays.values())

    order = dict(table=0, conv_one=0, conv_two=0, embed=0, query=0, key=0, value=0, out=0)
    sizes["table"] = table_rows * channels // devices // lanes
    finals = [struct((sizes[name], lanes), full) for name in order]
    rows = [SUMS.index(name) for name in GIVEN_BACK]
    results = pl.pallas_call(
        functools.partial(last_kernel, [spans[name] for name in order], rows),
        out_shape=(outputs["output"], outputs["input_grad"], *finals)
        + (struct((1, channels), full),) * len(rows),
        in_specs=[anywhere, anywhere, anywhere, in_vmem],
        out_specs=(anywhere,) * (2 + len(finals)) + (in_vmem,) * len(rows),
        scratch_shapes=[
            hold(*images.shape),
            hold(*images.shape),
            hold(start, lanes, kind=full),
            semaphores(5 + len(finals)),
        ],
        compiler_params=pltpu.CompilerParams(vmem_limit_bytes=63 << 20),
        name="finish",
    )(output, input_grad, flat, sums)
    return tuple(results[:2]) + tuple(member.reshape(-1) for member in results[2:])


def per_device(
    images,
    cotangent,
    levels,
    noise_table,
    gain_one,
    shift_one,
    conv_one,
    bias_one,
    embed_weight,
    embed_bias,
    gain_two,
    shift_two,
    conv_two,
    bias_two,
    gain_three,
    shift_three,
    query_weight,
    query_bias,
    key_weight,
    value_weight,
    value_bias,
    out_weight,
    out_bias,
):
    given = dict(
        images=images,
        cotangent=cotangent,
        levels=levels,
        noise_table=noise_table,
        gain_one=gain_one,
        shift_one=shift_one,
        conv_one=conv_one,
        bias_one=bias_one,
        embed_weight=embed_weight,
        embed_bias=embed_bias,
        gain_two=gain_two,
        shift_two=shift_two,
        conv_two=conv_two,
        bias_two=bias_two,
        gain_three=gain_three,
        shift_three=shift_three,
        query_weight=query_weight,
        query_bias=query_bias,
        key_weight=key_weight,
        value_weight=value_weight,
        value_bias=value_bias,
        out_weight=out_weight,
        out_bias=out_bias,
    )
    ranks, cores = lax.axis_size("wide"), lax.axis_size("rep")
    images_rep, piece, channels = images.shape
    devices = ranks * cores
    fits = (
        cores == 2
        and ranks >= 8
        and ranks & (ranks - 1) == 0
        and images_rep == 2 * ranks
        and piece % 16 == 0
        and conv_one.shape[0] % (devices * 48) == 0
        and channels % (devices * 16) == 0
        and noise_table.size % (devices * channels // 2) == 0
    )
    return fused_device(given) if fits else plain_device(*given.values())


def solution(mesh):
    in_specs = (
        P("rep", "wide", None),
        P("rep", "wide", None),
        P("rep"),
        P(),
        P(),
        P(),
        P(),
        P(),
        P(),
        P(),
        P(),
        P(),
        P(),
        P(),
        P(),
        P(),
        P(),
        P(),
        P(),
        P(),
        P(),
        P(),
        P(),
    )
    out_specs = (
        P("rep", "wide", None),
        P("rep", "wide", None),
        P(("wide", "rep")),
        P(("wide", "rep")),
        P(("wide", "rep")),
        P(("wide", "rep")),
        P(("wide", "rep")),
        P(("wide", "rep")),
        P(("wide", "rep")),
        P(("wide", "rep")),
        P(),
        P(),
        P(),
        P(),
        P(),
        P(),
        P(),
        P(),
        P(),
        P(),
        P(),
        P(),
    )
    return jax.shard_map(
        per_device, mesh=mesh, in_specs=in_specs, out_specs=out_specs, check_vma=False
    )
```

```python
import functools
import types

import jax
import jax.numpy as jnp
from jax import lax
from jax.experimental import pallas as pl
from jax.experimental.pallas import tpu as pltpu
from jax.sharding import PartitionSpec as P

GROUPS = 32
SIDE = 16
MESH = pl.DeviceIdType.MESH
CHUNK = 64


epsilon = 1e-05
highest = lax.Precision.HIGHEST


def swish(field):
    return field * jax.nn.sigmoid(field)


def group_norm(field, norm_gain, norm_shift):
    images_here = field.shape[0]
    channels = field.shape[2]
    grouped = field.reshape(images_here, field.shape[1], GROUPS, channels // GROUPS)
    center = jnp.mean(grouped, axis=(1, 3), keepdims=True)
    spread = grouped - center
    variance = jnp.mean(spread * spread, axis=(1, 3), keepdims=True)
    return (spread * lax.rsqrt(variance + epsilon)).reshape(field.shape) * norm_gain + norm_shift


def norm_swish(field, norm_gain, norm_shift):
    return swish(group_norm(field, norm_gain, norm_shift))


def matmul(left, right):
    return jnp.dot(left, right, preferred_element_type=jnp.float32)


def contract_rows(left, right):
    return lax.dot_general(
        left, right, (((0,), (0,)), ((), ())), preferred_element_type=jnp.float32
    )


def against(left, right):
    return lax.dot_general(
        left, right, (((1,), (1,)), ((), ())), preferred_element_type=jnp.float32
    )


def patches(activation):
    images_here = activation.shape[0]
    grid = activation.reshape(images_here, SIDE, SIDE, activation.shape[2])
    padded = jnp.pad(grid, ((0, 0), (1, 1), (1, 1), (0, 0)))
    pieces = [
        padded[
            :, kernel_tap // 3 : kernel_tap // 3 + SIDE, kernel_tap % 3 : kernel_tap % 3 + SIDE, :
        ]
        for kernel_tap in range(9)
    ]
    return jnp.concatenate(pieces, axis=-1).reshape(images_here * SIDE * SIDE, -1)


def unpatch(columns, images_here):
    channels = columns.shape[1] // 9
    grid = columns.reshape(images_here, SIDE, SIDE, 9, channels)
    summed = jnp.zeros((images_here, SIDE + 2, SIDE + 2, channels), jnp.float32)
    for kernel_tap in range(9):
        row_off = kernel_tap // 3
        col_off = kernel_tap % 3
        summed = summed + jnp.pad(
            grid[:, :, :, kernel_tap, :],
            ((0, 0), (row_off, 2 - row_off), (col_off, 2 - col_off), (0, 0)),
        )
    return summed[:, 1 : SIDE + 1, 1 : SIDE + 1, :].reshape(images_here, SIDE * SIDE, channels)


def plain_device(
    images,
    cotangent,
    levels,
    noise_table,
    gain_one,
    shift_one,
    conv_one,
    bias_one,
    embed_weight,
    embed_bias,
    gain_two,
    shift_two,
    conv_two,
    bias_two,
    gain_three,
    shift_three,
    query_weight,
    query_bias,
    key_weight,
    value_weight,
    value_bias,
    out_weight,
    out_bias,
):
    arrived, upstream = (
        lax.all_to_all(images, "wide", split_axis=0, concat_axis=1, tiled=True),
        lax.all_to_all(cotangent, "wide", split_axis=0, concat_axis=1, tiled=True),
    )
    images_here = arrived.shape[0]
    pixels = arrived.shape[1]
    channels = arrived.shape[2]
    flat_rows = images_here * pixels
    score_scale = channels ** (-0.5)
    table_rows = noise_table.shape[0]
    offset = lax.axis_index("wide") * images_here
    own_levels = lax.dynamic_slice_in_dim(levels, offset, images_here)
    selector = own_levels[:, None] == jnp.arange(table_rows, dtype=jnp.int32)[None, :]
    embedded = matmul(selector.astype(jnp.bfloat16), noise_table).astype(jnp.bfloat16)
    embed_shift = matmul(embedded, embed_weight) + embed_bias
    inputs = arrived.astype(jnp.float32)
    act_one, back_one = jax.vjp(norm_swish, inputs, gain_one, shift_one)
    cols_one = patches(act_one.astype(jnp.bfloat16))
    hidden_one = (matmul(cols_one, conv_one) + bias_one).reshape(images_here, pixels, channels)
    hidden_one = hidden_one + embed_shift[:, None, :]
    act_two, back_two = jax.vjp(norm_swish, hidden_one, gain_two, shift_two)
    cols_two = patches(act_two.astype(jnp.bfloat16))
    branch_out = matmul(cols_two, conv_two) + bias_two
    middle = inputs + branch_out.reshape(images_here, pixels, channels)
    normed, back_three = jax.vjp(group_norm, middle, gain_three, shift_three)
    normed_low = normed.astype(jnp.bfloat16).reshape(flat_rows, channels)
    query_block = (matmul(normed_low, query_weight) + query_bias).astype(jnp.bfloat16)
    key_block = matmul(normed_low, key_weight).astype(jnp.bfloat16)
    value_block = (matmul(normed_low, value_weight) + value_bias).astype(jnp.bfloat16)
    query_block = query_block.reshape(images_here, pixels, channels)
    key_block = key_block.reshape(images_here, pixels, channels)
    value_block = value_block.reshape(images_here, pixels, channels)
    scores = (
        jnp.einsum("npc,nqc->npq", query_block, key_block, preferred_element_type=jnp.float32)
        * score_scale
    )
    row_top = jnp.max(scores, axis=-1, keepdims=True)
    exponent = jnp.exp(scores - row_top)
    row_total = jnp.sum(exponent, axis=-1, keepdims=True)
    probs_low = (exponent / row_total).astype(jnp.bfloat16)
    log_total = row_top + jnp.log(row_total)
    mixed = jnp.einsum("npq,nqc->npc", probs_low, value_block, preferred_element_type=jnp.float32)
    mixed_low = mixed.astype(jnp.bfloat16).reshape(flat_rows, channels)
    result = middle.reshape(flat_rows, channels) + matmul(mixed_low, out_weight) + out_bias
    grad_out = upstream.reshape(flat_rows, channels)
    grad_out_bias = jnp.sum(grad_out.astype(jnp.float32), axis=0)
    grad_out_weight = contract_rows(mixed_low, grad_out)
    grad_mixed = (
        against(grad_out, out_weight).astype(jnp.bfloat16).reshape(images_here, pixels, channels)
    )
    scores_again = (
        jnp.einsum("npc,nqc->npq", query_block, key_block, preferred_element_type=jnp.float32)
        * score_scale
    )
    probs = jnp.exp(scores_again - log_total)
    probs_again = probs.astype(jnp.bfloat16)
    grad_probs = jnp.einsum(
        "npc,nqc->npq", grad_mixed, value_block, preferred_element_type=jnp.float32
    )
    grad_values = jnp.einsum(
        "npq,npc->nqc", probs_again, grad_mixed, preferred_element_type=jnp.float32
    ).astype(jnp.bfloat16)
    grad_scores = probs * (grad_probs - jnp.sum(grad_probs * probs, axis=-1, keepdims=True))
    grad_scores = grad_scores.astype(jnp.bfloat16)
    grad_query = (
        (
            jnp.einsum("npq,nqc->npc", grad_scores, key_block, preferred_element_type=jnp.float32)
            * score_scale
        )
        .astype(jnp.bfloat16)
        .reshape(flat_rows, channels)
    )
    grad_keys = (
        (
            jnp.einsum("npq,npc->nqc", grad_scores, query_block, preferred_element_type=jnp.float32)
            * score_scale
        )
        .astype(jnp.bfloat16)
        .reshape(flat_rows, channels)
    )
    grad_values = grad_values.reshape(flat_rows, channels)
    grad_query_weight = contract_rows(normed_low, grad_query)
    grad_key_weight = contract_rows(normed_low, grad_keys)
    grad_value_weight = contract_rows(normed_low, grad_values)
    grad_query_bias = jnp.sum(grad_query.astype(jnp.float32), axis=0)
    grad_value_bias = jnp.sum(grad_values.astype(jnp.float32), axis=0)
    grad_normed = against(grad_query, query_weight) + against(grad_keys, key_weight)
    grad_normed = grad_normed + against(grad_values, value_weight)
    grad_middle, grad_gain_three, grad_shift_three = back_three(
        grad_normed.reshape(images_here, pixels, channels)
    )
    grad_middle = grad_middle + upstream.astype(jnp.float32)
    grad_branch = grad_middle.astype(jnp.bfloat16).reshape(flat_rows, channels)
    grad_bias_two = jnp.sum(grad_branch.astype(jnp.float32), axis=0)
    grad_conv_two = contract_rows(cols_two, grad_branch)
    grad_act_two = unpatch(against(grad_branch, conv_two), images_here)
    grad_hidden, grad_gain_two, grad_shift_two = back_two(grad_act_two)
    grad_hidden_low = grad_hidden.astype(jnp.bfloat16)
    hidden_rows = grad_hidden_low.reshape(flat_rows, channels)
    grad_bias_one = jnp.sum(hidden_rows.astype(jnp.float32), axis=0)
    grad_conv_one = contract_rows(cols_one, hidden_rows)
    grad_shift = jnp.sum(grad_hidden_low.astype(jnp.float32), axis=1)
    grad_embed_bias = jnp.sum(grad_shift, axis=0)
    grad_embed_weight = jnp.dot(embedded.astype(jnp.float32).T, grad_shift, precision=highest)
    embed_float = embed_weight.astype(jnp.float32)
    grad_act_one = unpatch(against(hidden_rows, conv_one), images_here)
    grad_input_part, grad_gain_one, grad_shift_one = back_one(grad_act_one)
    grad_input = grad_middle + grad_input_part
    output_back, input_back = (
        lax.all_to_all(
            result.reshape(images_here, pixels, channels).astype(jnp.bfloat16),
            "wide",
            split_axis=1,
            concat_axis=0,
            tiled=True,
        ),
        lax.all_to_all(
            grad_input.astype(jnp.bfloat16), "wide", split_axis=1, concat_axis=0, tiled=True
        ),
    )
    wide_count = lax.axis_size("wide")
    rep_count = lax.axis_size("rep")
    device_count = wide_count * rep_count
    weight_grads = (
        grad_conv_one,
        grad_conv_two,
        grad_embed_weight,
        grad_query_weight,
        grad_key_weight,
        grad_value_weight,
        grad_out_weight,
    )
    grad_embedded = jnp.dot(grad_shift, embed_float.T, precision=highest)
    grad_table = jnp.dot(selector.astype(jnp.float32).T, grad_embedded, precision=highest)
    members = (grad_table,) + weight_grads
    widths = [member.size // device_count for member in members]
    packed = jnp.concatenate([member.reshape(device_count, -1) for member in members], axis=1)
    packed = lax.psum_scatter(packed, ("wide", "rep"), scatter_dimension=0, tiled=True)
    packed = packed.reshape(-1)
    large_grads = []
    start_at = 0
    for width in widths:
        large_grads.append(packed[start_at : start_at + width])
        start_at = start_at + width
    large_grads = tuple(large_grads)
    small_grads = lax.psum(
        (
            grad_gain_one,
            grad_shift_one,
            grad_bias_one,
            grad_embed_bias,
            grad_gain_two,
            grad_shift_two,
            grad_bias_two,
            grad_gain_three,
            grad_shift_three,
            grad_query_bias,
            grad_value_bias,
            grad_out_bias,
        ),
        ("wide", "rep"),
    )
    return (output_back, input_back) + large_grads + tuple(small_grads)


def by_rows(left, right):
    return lax.dot_general(
        left, right, (((0,), (0,)), ((), ())), preferred_element_type=jnp.float32
    )


def group_sum(rows, same_group):
    width = same_group.shape[0]
    first = rows.astype(jnp.bfloat16).astype(jnp.float32)
    rest = rows - first
    second = rest.astype(jnp.bfloat16).astype(jnp.float32)
    terms = (first, second, rest - second)
    spans = [slice(start, start + width) for start in range(0, rows.shape[1], width)]
    stacked = jnp.concatenate([term[:, span] for span in spans for term in terms], axis=0)
    summed = matmul(stacked.astype(jnp.bfloat16), same_group)
    parts = [summed[24 * k : 24 * k + 24] for k in range(len(spans))]
    return jnp.concatenate([part[0:8] + part[8:16] + part[16:24] for part in parts], axis=1)


def stack_rows(members):
    shape = (8, members[0].shape[1])
    place = lax.broadcasted_iota(jnp.int32, shape, 0)
    stacked = jnp.zeros(shape, jnp.float32)
    for index, member in enumerate(members):
        stacked = jnp.where(place == index, jnp.broadcast_to(member, shape), stacked)
    return stacked


def sigmoid(field):
    return 0.5 + 0.5 * jnp.tanh(0.5 * field)


SUMS = tuple(
    dict(
        gain_one=0,
        shift_one=0,
        bias_one=0,
        gain_two=0,
        shift_two=0,
        bias_two=0,
        gain_three=0,
        shift_three=0,
        query_bias=0,
        value_bias=0,
        out_bias=0,
    )
)
GIVEN_BACK = SUMS[:3] + SUMS[2:]


class Flight:
    def __init__(self, flights, make, offsets=None, whole=None, own=None):
        self.flights, self.make, self.offsets, self.own = flights, make, offsets, own
        self.whole = make if whole is None else whole
        self.arrived = self.left = False

    def start(self):
        if self.offsets is None:
            self.make().start()
        else:

            def go(offset, carry):
                self.make(offset).start()
                return carry

            lax.fori_loop(*self.offsets, go, 0)
        if self.own is not None:
            self.own().start()
        self.flights.append(self)
        return self

    def arrive(self):
        self.whole().wait_recv()
        if self.own is not None:
            self.own().wait()
        self.arrived = True

    def leave(self):
        self.whole().wait_send()
        self.left = True

    def land(self):
        if not self.arrived:
            self.arrive()
        if not self.left:
            self.leave()


class Reduce:
    def __init__(self, flights, place, blocks, orders, landing, kept, send, recv, last):
        self.flights, self.place = flights, place
        self.blocks, self.orders, self.last = blocks, orders, last
        self.landing, self.kept, self.send, self.recv = landing, kept, send, recv
        self.rows = blocks.shape[2]
        self.parts = send.shape[1]
        self.under_way = {}

    def cut(self, part):
        size = self.rows // self.parts
        return pl.ds(part * size, size)

    def copy(self, stage, part):
        place, rows = self.place, self.cut(part)
        if stage == 0:
            source = self.blocks.at[:, 1 - place.core, rows, :]
            target = place.other_core
        else:
            count = self.blocks.shape[0] >> stage
            bit = self.orders[part][stage - 1]
            source = self.kept[stage - 1].at[
                pl.ds((1 - place.bit(bit)) * count, count), rows, :
            ]
            target = place.across(bit)
        return pltpu.make_async_remote_copy(
            src_ref=source,
            dst_ref=self.landing[stage].at[:, rows, :],
            send_sem=self.send.at[stage, part],
            recv_sem=self.recv.at[stage, part],
            device_id=target,
            device_id_type=MESH,
        )

    def start(self, stage, part):
        copy = functools.partial(self.copy, stage, part)
        self.under_way[stage, part] = Flight(self.flights, copy).start()

    def step(self, stage, part):
        self.finish(stage, part)
        if stage < len(self.orders[part]):
            self.start(stage + 1, part)

    def finish(self, stage, part):
        place, rows = self.place, self.cut(part)
        self.under_way[stage, part].arrive()
        count = self.blocks.shape[0] >> stage
        if stage == 0:
            own = self.blocks[:, place.core, rows, :]
        else:
            first = place.bit(self.orders[part][stage - 1]) * count
            own = self.kept[stage - 1][pl.ds(first, count), rows, :]
        landed = self.landing[stage][:, rows, :]
        if stage < len(self.orders[part]):
            self.kept[stage][:, rows, :] = own + landed
        else:
            self.last(rows, own.astype(jnp.float32) + landed.astype(jnp.float32))


class Place:
    def __init__(self, ranks):
        self.ranks = ranks
        self.rank = lax.axis_index("wide")
        self.core = lax.axis_index("rep")
        self.other_core = (self.rank, 1 - self.core)

    def bit(self, index):
        return (self.rank // (1 << index)) % 2

    def across(self, index):
        step = 1 << index
        return (self.rank + step - 2 * step * self.bit(index), self.core)


def block_order(ranks, order):
    places = []
    for rank in range(ranks):
        spot = 0
        for bit in order:
            spot = spot * 2 + (rank >> bit) % 2
        places.append(spot)
    return places


def fused_kernel(names, spans, ranks, table_rows, *refs):
    s = types.SimpleNamespace(**dict(zip(names, refs, strict=True)))
    place = Place(ranks)
    bits = (ranks - 1).bit_length()
    far = list(range(2, bits))
    images_here, pixels, channels = s.arrived.shape
    every_image = range(images_here)
    flat_rows = images_here * pixels
    piece = pixels // ranks
    half = channels // 2
    steps = pixels // CHUNK
    score_scale = channels ** (-0.5)
    count_inverse = 1.0 / (pixels * (channels // GROUPS))
    col = lax.broadcasted_iota(jnp.int32, (CHUNK, 1), 0) % SIDE
    flights = []

    def image_rows(image):
        return slice(image * pixels, (image + 1) * pixels)

    barrier = pltpu.get_barrier_semaphore()

    def greet(offset, carry):
        pl.semaphore_signal(
            barrier,
            inc=1,
            device_id=((place.rank + offset) % ranks, place.core),
            device_id_type=MESH,
        )
        return carry

    lax.fori_loop(1, ranks, greet, 0)
    pl.semaphore_signal(barrier, inc=1, device_id=place.other_core, device_id_type=MESH)

    pairs = (
        (s.noise_table, s.noise_table_here.at[pl.ds(0, table_rows), :]),
        (s.embed_weight, s.embed_weight_here),
        (s.conv_one, s.conv_one_here),
        (s.conv_two, s.conv_two_here),
        (s.query_weight, s.query_weight_here),
        (s.key_weight, s.key_weight_here),
        (s.value_weight, s.value_weight_here),
        (s.out_weight, s.out_weight_here),
    )
    loads = []
    for index, (source, target) in enumerate(pairs):
        loads.append(pltpu.make_async_copy(source, target, s.load_sem.at[index]))
        loads[-1].start()
    pl.semaphore_wait(barrier, ranks)

    def gather_copy(slot, source, target, image, offset):
        peer = (place.rank + offset) % ranks
        return pltpu.make_async_remote_copy(
            src_ref=source.at[peer * images_here + image],
            dst_ref=target.at[image, pl.ds(pl.multiple_of(place.rank * piece, 16), piece)],
            send_sem=s.swap_send.at[slot],
            recv_sem=s.swap_recv.at[slot],
            device_id=(peer, place.core),
            device_id_type=MESH,
        )

    def gather_own(slot, source, target, image):
        return pltpu.make_async_copy(
            source.at[place.rank * images_here + image],
            target.at[image, pl.ds(pl.multiple_of(place.rank * piece, 16), piece)],
            s.swap_own.at[slot],
        )

    def scatter_copy(slot, source, target, image, offset):
        peer = (place.rank + offset) % ranks
        return pltpu.make_async_remote_copy(
            src_ref=source.at[image, pl.ds(pl.multiple_of(peer * piece, 16), piece)],
            dst_ref=target.at[place.rank * images_here + image],
            send_sem=s.swap_send.at[slot],
            recv_sem=s.swap_recv.at[slot],
            device_id=(peer, place.core),
            device_id_type=MESH,
        )

    def scatter_own(slot, source, target, image):
        return pltpu.make_async_copy(
            source.at[image, pl.ds(pl.multiple_of(place.rank * piece, 16), piece)],
            target.at[place.rank * images_here + image],
            s.swap_own.at[slot],
        )

    def swap_whole(slot, held, image):
        others = held.at[image, pl.ds(0, pixels - piece)]
        return pltpu.make_async_remote_copy(
            src_ref=others,
            dst_ref=others,
            send_sem=s.swap_send.at[slot],
            recv_sem=s.swap_recv.at[slot],
            device_id=place.across(0),
            device_id_type=MESH,
        )

    def swaps(copy, own, which, source, target, held):
        return [
            Flight(
                flights,
                functools.partial(copy, which * images_here + image, source, target, image),
                (1, ranks),
                functools.partial(swap_whole, which * images_here + image, held, image),
                functools.partial(own, which * images_here + image, source, target, image),
            )
            for image in every_image
        ]

    swap_images = swaps(gather_copy, gather_own, 0, s.images, s.arrived, s.arrived)
    swap_upstream = swaps(gather_copy, gather_own, 1, s.cotangent, s.upstream, s.upstream)
    swap_output = swaps(scatter_copy, scatter_own, 2, s.leaving, s.output, s.leaving)
    swap_grad = swaps(scatter_copy, scatter_own, 3, s.leaving_grad, s.input_grad, s.leaving_grad)
    for image in every_image:
        swap_images[image].start()
    for image in every_image:
        swap_upstream[image].start()

    for padded in (s.spread_act, s.spread_two, s.spread_one, s.spread_far):
        for image in every_image:
            edge = jnp.zeros((SIDE, padded.shape[2]), jnp.bfloat16)
            padded[image, 0:SIDE, :] = edge
            padded[image, pixels + SIDE : pixels + 2 * SIDE, :] = edge
    tail = s.noise_table_here.shape[0] - table_rows
    if tail:
        s.noise_table_here[table_rows:, :] = jnp.zeros((tail, channels), jnp.bfloat16)
    own_levels = [s.levels[place.rank * images_here + image] for image in every_image]
    lane = lax.broadcasted_iota(jnp.int32, s.levels_all.shape[1:], 1)
    tile = jnp.zeros(lane.shape, jnp.float32)
    for index in range(ranks * images_here):
        tile = jnp.where(lane == index, s.levels[index].astype(jnp.float32), tile)
    s.levels_all[place.core] = tile

    def levels_copy():
        return pltpu.make_async_remote_copy(
            src_ref=s.levels_all.at[place.core],
            dst_ref=s.levels_all.at[place.core],
            send_sem=s.slots_send.at[2],
            recv_sem=s.slots_recv.at[2],
            device_id=place.other_core,
            device_id_type=MESH,
        )

    levels_pair = Flight(flights, levels_copy).start()
    entry = lax.broadcasted_iota(jnp.int32, (8, s.noise_table_here.shape[0]), 1)
    line = lax.broadcasted_iota(jnp.int32, entry.shape, 0)
    selected = jnp.zeros(entry.shape, jnp.float32)
    for image in every_image:
        hit = jnp.where(entry == own_levels[image], 1.0, 0.0)
        selected = jnp.where(line == image, hit, selected)
    loads[0].wait()
    loads[1].wait()
    embedded = matmul(selected.astype(jnp.bfloat16), s.noise_table_here[...])
    embed_shift = matmul(embedded.astype(jnp.bfloat16), s.embed_weight_here[...])
    embed_shift = embed_shift + s.embed_bias[...] + s.bias_one[...]

    def over(image, body, start):
        return lax.fori_loop(0, steps, functools.partial(body, image), start)

    def at(step):
        return pl.ds(pl.multiple_of(step * CHUNK, CHUNK), CHUNK)

    def flat_at(image, step):
        return pl.ds(pl.multiple_of(image * pixels + step * CHUNK, CHUNK), CHUNK)

    def fold(chunk):
        return jnp.sum(chunk.reshape(CHUNK // 8, 8, channels), axis=0)

    none = jnp.zeros((8, channels), jnp.float32)

    def whole(part):
        return jnp.sum(part, axis=0, keepdims=True)

    group_width = s.same_group.shape[0]
    same_group = [
        lax.broadcasted_iota(jnp.int32, (group_width, group_width), axis)
        // (channels // GROUPS)
        for axis in range(2)
    ]
    s.same_group[...] = jnp.where(same_group[0] == same_group[1], 1.0, 0.0).astype(jnp.bfloat16)

    def group_total(row):
        rows = jnp.broadcast_to(row, (8, channels))
        return group_sum(rows, s.same_group[...])[0:1] * count_inverse

    def statistics(load, image):
        def first(image, step, total):
            return total + fold(load(image, step))

        center = group_total(whole(over(image, first, none)))

        def second(image, step, total):
            spread = load(image, step) - center
            return total + fold(spread * spread)

        variance = group_total(whole(over(image, second, none)))
        return center, lax.rsqrt(variance + epsilon)

    def spread_out(target, image, step, chunk, before, after):
        width = chunk.shape[1]
        rows = pl.ds(pl.multiple_of(step * CHUNK + SIDE, SIDE), CHUNK)
        target[image, rows, before * width : (before + 1) * width] = jnp.where(
            col > 0, pltpu.roll(chunk, 1, 0), 0.0
        ).astype(jnp.bfloat16)
        target[image, rows, width : 2 * width] = chunk.astype(jnp.bfloat16)
        target[image, rows, after * width : (after + 1) * width] = jnp.where(
            col < SIDE - 1, pltpu.roll(chunk, CHUNK - 1, 0), 0.0
        ).astype(jnp.bfloat16)

    def activate(load, image, moments, gain, shift, keep):
        center, rate = moments
        slope = rate * gain

        def apply(image, step, carry):
            field = (load(image, step) - center) * slope + shift
            act = field * sigmoid(field)
            spread_out(s.spread_act, image, step, act, 0, 2)
            keep[flat_at(image, step), :] = act.astype(jnp.bfloat16)
            return carry

        over(image, apply, 0)

    def convolve(weight, image):
        total = None
        for row_tap in range(3):
            term = matmul(
                s.spread_act[image, SIDE * row_tap : SIDE * row_tap + pixels, :],
                weight[3 * channels * row_tap : 3 * channels * (row_tap + 1), :],
            )
            total = term if total is None else total + term
        return total

    def tap_rows(row_tap):
        return slice(SIDE * (2 - row_tap), SIDE * (2 - row_tap) + pixels)

    def convolve_back(source, weight, images):
        total = None
        for tap in range(9):
            window = source[
                images, tap_rows(tap // 3), (tap % 3) * channels : (tap % 3 + 1) * channels
            ]
            term = against(
                window.reshape(-1, channels), weight[channels * tap : channels * (tap + 1), :]
            )
            total = term if total is None else total + term
        return total

    def share_copy(slot, source, target, bit):
        def make():
            return pltpu.make_async_remote_copy(
                src_ref=source,
                dst_ref=target,
                send_sem=s.share_send.at[slot],
                recv_sem=s.share_recv.at[slot],
                device_id=place.across(bit),
                device_id_type=MESH,
            )

        return Flight(flights, make)

    bit_one, bit_two = 1, 0
    half_one, half_two = place.bit(bit_one), place.bit(bit_two)

    def shares(which, source, target, bit, mine=None):
        made = []
        for image in every_image:
            rows = pl.ds(image * pixels, pixels)
            lanes_sent = pl.ds(0, channels)
            if mine is not None:
                lanes_sent = pl.ds(pl.multiple_of((1 - mine) * half, half), half)
            made.append(
                share_copy(
                    which * images_here + image,
                    source.at[rows, lanes_sent],
                    target.at[rows, :],
                    bit,
                )
            )
        return made

    share_act_one = shares(0, s.act_one, s.act_one_far, bit_one)
    share_act_two = shares(1, s.act_two, s.act_two_far, bit_two)
    share_grad_two = shares(2, s.grad_two, s.grad_two_far, bit_two, half_two)
    share_grad_one = shares(3, s.grad_one, s.grad_one_far, bit_one, half_one)

    def weigh(spread, mine, act, act_far, grad_far, blocks, spots):
        def unfold(image, step, carry):
            chunk = grad_far[flat_at(image, step), :].astype(jnp.float32)
            spread_out(s.spread_far, image, step, chunk, 2, 0)
            return carry

        for image in every_image:
            over(image, unfold, 0)
        rows_block = blocks.shape[2]
        rows_part = rows_block // len(spots)
        for tap in range(9):
            rows, side_tap = tap_rows(tap // 3), tap % 3
            near = spread[
                :, rows, pl.ds(pl.multiple_of(side_tap * channels + mine * half, half), half)
            ]
            beyond = s.spread_far[:, rows, side_tap * half : (side_tap + 1) * half]
            product = by_rows(act[...], near.reshape(flat_rows, half)) + by_rows(
                act_far[...], beyond.reshape(flat_rows, half)
            )
            product = product.astype(jnp.bfloat16)
            done = 0
            while done < channels:
                block, inside = divmod(tap * channels + done, rows_block)
                part = inside // rows_part
                size = min(rows_part * (part + 1) - inside, channels - done)
                blocks[spots[part][block // 2], block % 2, inside : inside + size, :] = product[
                    done : done + size
                ]
                done = done + size

    orders_one = [[1 - bit_one] + far] * 2 + [far + [1 - bit_one]]
    orders_two = [[1 - bit_two] + far] * 2 + [far + [1 - bit_two]]
    orders_mix = [[0, 1] + far, [1, 0] + far]
    spots_one = [block_order(ranks, order + [bit_one]) for order in orders_one]
    spots_two = [block_order(ranks, order + [bit_two]) for order in orders_two]
    spots_mix = [block_order(ranks, order) for order in orders_mix]

    def put_one(rows, total):
        s.sum_one[:, rows, :] = total
        s.fin_one[:, rows, :] = total.astype(jnp.bfloat16)

    def put_two(rows, total):
        s.sum_two[:, rows, :] = total
        s.fin_two[:, rows, :] = total.astype(jnp.bfloat16)

    def put_mix(rows, total):
        s.share_mix[rows, :] = total[0]

    def staged(ref, first, stages):
        views, start = [], 0
        for stage in range(stages):
            views.append(ref.at[pl.ds(start, first >> stage)])
            start = start + (first >> stage)
        return views

    def reduction(blocks, order, landing, kept, send, recv, put):
        stages = len(order[0])
        return Reduce(
            flights,
            place,
            blocks,
            order,
            staged(landing, ranks, stages + 1),
            staged(kept, ranks, stages),
            send,
            recv,
            put,
        )

    reduce_one = reduction(
        s.blocks_one,
        orders_one,
        s.land_one,
        s.kept_one,
        s.reduce_send_one,
        s.reduce_recv_one,
        put_one,
    )
    reduce_two = reduction(
        s.blocks_two,
        orders_two,
        s.land_two,
        s.kept_two,
        s.reduce_send_two,
        s.reduce_recv_two,
        put_two,
    )
    reduce_mix = reduction(
        s.blocks_mix,
        orders_mix,
        s.land_mix,
        s.kept_mix,
        s.reduce_send_mix,
        s.reduce_recv_mix,
        put_mix,
    )
    parts = reduce_one.parts

    def settle(flight, sums, target, mine):
        flight.arrive()
        own = sums[mine]
        other = target[...].astype(jnp.float32)
        left = jnp.where(mine == 0, own, other)
        right = jnp.where(mine == 0, other, own)
        return jnp.concatenate([left, right], axis=1)

    def small_copy(stage):
        return pltpu.make_async_remote_copy(
            src_ref=s.small_sum.at[stage],
            dst_ref=s.small_land.at[stage],
            send_sem=s.small_send.at[stage],
            recv_sem=s.small_recv.at[stage],
            device_id=place.other_core if stage == 0 else place.across(stage - 1),
            device_id_type=MESH,
        )

    small = [Flight(flights, functools.partial(small_copy, k)) for k in range(bits + 1)]

    def small_step(stage):
        small[stage].arrive()
        s.small_sum[stage + 1] = s.small_sum[stage] + s.small_land[stage]
        if stage < bits:
            small[stage + 1].start()

    slot_rows = 8
    lanes = s.slots.shape[1]

    def pair_window():
        return s.slots.at[pl.ds(pl.multiple_of(place.rank * 2 * slot_rows, 16), 2 * slot_rows), :]

    def slot_copy():
        first = pl.multiple_of((place.rank * 2 + place.core) * slot_rows, slot_rows)
        window = s.slots.at[pl.ds(first, slot_rows), :]
        return pltpu.make_async_remote_copy(
            src_ref=window,
            dst_ref=window,
            send_sem=s.slots_send.at[0],
            recv_sem=s.slots_recv.at[0],
            device_id=place.other_core,
            device_id_type=MESH,
        )

    def pair_copy(offset):
        return pltpu.make_async_remote_copy(
            src_ref=pair_window(),
            dst_ref=pair_window(),
            send_sem=s.slots_send.at[1],
            recv_sem=s.slots_recv.at[1],
            device_id=((place.rank + offset) % ranks, place.core),
            device_id_type=MESH,
        )

    slots_pair = Flight(flights, slot_copy)
    def pairs_whole():
        others = s.slots.at[pl.ds(0, (ranks - 1) * 2 * slot_rows), :]
        return pltpu.make_async_remote_copy(
            src_ref=others,
            dst_ref=others,
            send_sem=s.slots_send.at[1],
            recv_sem=s.slots_recv.at[1],
            device_id=place.across(0),
            device_id_type=MESH,
        )

    slots_all = Flight(flights, pair_copy, (1, ranks), pairs_whole)

    def load_input(image, step):
        return s.arrived[image, at(step), :].astype(jnp.float32)

    def load_hidden(image, step):
        return s.hidden[flat_at(image, step), :]

    def load_middle(image, step):
        return s.middle[flat_at(image, step), :]

    def load_upstream(image, step):
        return s.upstream[image, at(step), :].astype(jnp.float32)

    def delta_at(image, step):
        return s.delta[flat_at(image, step), :]

    def load_low(ref):
        return lambda image, step: ref[flat_at(image, step), :].astype(jnp.float32)

    gain_one, shift_one = s.gain_one[...], s.shift_one[...]
    gain_two, shift_two = s.gain_two[...], s.shift_two[...]
    gain_three, shift_three = s.gain_three[...], s.shift_three[...]
    moments_one, moments_two, moments_three = [], [], []
    sums = {name: [] for name in SUMS}

    def forward(image):
        rows = image_rows(image)
        swap_images[image].arrive()
        moments_one.append(statistics(load_input, image))
        activate(load_input, image, moments_one[image], gain_one, shift_one, s.act_one)
        share_act_one[image].start()
        if image == 0:
            loads[2].wait()
        s.hidden[rows, :] = convolve(s.conv_one_here, image) + embed_shift[image : image + 1]
        moments_two.append(statistics(load_hidden, image))
        activate(load_hidden, image, moments_two[image], gain_two, shift_two, s.act_two)
        share_act_two[image].start()
        if image == 0:
            loads[3].wait()
        s.middle[rows, :] = (
            convolve(s.conv_two_here, image)
            + s.bias_two[...]
            + s.arrived[image].astype(jnp.float32)
        )
        moments_three.append(statistics(load_middle, image))
        center, rate = moments_three[image]
        slope = rate * gain_three

        def normalize(image, step, carry):
            field = (load_middle(image, step) - center) * slope + shift_three
            s.normed[flat_at(image, step), :] = field.astype(jnp.bfloat16)
            return carry

        over(image, normalize, 0)
        if image == 0:
            for load in loads[4:]:
                load.wait()
        normed = s.normed[rows, :]
        query = (matmul(normed, s.query_weight_here[...]) + s.query_bias[...]).astype(jnp.bfloat16)
        key = matmul(normed, s.key_weight_here[...]).astype(jnp.bfloat16)
        value = (matmul(normed, s.value_weight_here[...]) + s.value_bias[...]).astype(jnp.bfloat16)
        s.query[rows, :] = query
        s.key[rows, :] = key
        s.value[rows, :] = value
        scores = against(query, key) * score_scale
        exponent = jnp.exp(scores - jnp.max(scores, axis=1, keepdims=True))
        probs = exponent / jnp.sum(exponent, axis=1, keepdims=True)
        s.probs[rows, :] = probs
        mixed = matmul(probs.astype(jnp.bfloat16), value).astype(jnp.bfloat16)
        s.mixed[rows, :] = mixed
        result = s.middle[rows, :] + matmul(mixed, s.out_weight_here[...]) + s.out_bias[...]
        s.leaving[image] = result.astype(jnp.bfloat16)

    def norm_back_terms(gain, shift_sum, gain_sum):
        rows = stack_rows([gain * shift_sum, gain * gain_sum])
        means = group_sum(rows, s.same_group[...]) * count_inverse
        return means[0:1], means[1:2]

    def backward(image):
        rows = image_rows(image)
        swap_upstream[image].arrive()
        probs = s.probs[rows, :]
        query, key, value = s.query[rows, :], s.key[rows, :], s.value[rows, :]
        grad_mixed = against(s.upstream[image], s.out_weight_here[...]).astype(jnp.bfloat16)
        grad_probs = against(grad_mixed, value)
        grad_value = by_rows(probs.astype(jnp.bfloat16), grad_mixed).astype(jnp.bfloat16)
        inner = jnp.sum(grad_probs * probs, axis=1, keepdims=True)
        grad_scores = (probs * (grad_probs - inner)).astype(jnp.bfloat16)
        grad_query = (matmul(grad_scores, key) * score_scale).astype(jnp.bfloat16)
        grad_key = (by_rows(grad_scores, query) * score_scale).astype(jnp.bfloat16)
        s.grad_value[rows, :] = grad_value
        s.grad_query[rows, :] = grad_query
        s.grad_key[rows, :] = grad_key
        s.delta[rows, :] = (
            against(grad_query, s.query_weight_here[...])
            + against(grad_key, s.key_weight_here[...])
            + against(grad_value, s.value_weight_here[...])
        )

    def backward_rest(image, between=None):
        rows = image_rows(image)
        center, rate = moments_three[image]

        def sums_three(image, step, totals):
            grad = delta_at(image, step)
            unit = (load_middle(image, step) - center) * rate
            return totals[0] + fold(grad), totals[1] + fold(grad * unit)

        shift_sum, gain_sum = map(whole, over(image, sums_three, (none, none)))
        sums["gain_three"].append(gain_sum)
        sums["shift_three"].append(shift_sum)
        mean_shift, mean_gain = norm_back_terms(gain_three, shift_sum, gain_sum)

        def back_three(image, step, total):
            unit = (load_middle(image, step) - center) * rate
            grad = rate * (delta_at(image, step) * gain_three - mean_shift - unit * mean_gain)
            grad = grad + load_upstream(image, step)
            s.grad_middle[flat_at(image, step), :] = grad
            low = grad.astype(jnp.bfloat16)
            s.grad_two[flat_at(image, step), :] = low
            low = low.astype(jnp.float32)
            spread_out(s.spread_two, image, step, low, 2, 0)
            return total + fold(low)

        sums["bias_two"].append(whole(over(image, back_three, none)))
        share_grad_two[image].start()
        if between is not None:
            between()

        s.delta[rows, :] = convolve_back(s.spread_two, s.conv_two_here, slice(image, image + 1))

        def put_hidden(image, step, grad, total):
            low = grad.astype(jnp.bfloat16)
            s.grad_one[flat_at(image, step), :] = low
            low = low.astype(jnp.float32)
            spread_out(s.spread_one, image, step, low, 2, 0)
            return total + fold(low)

        gain_sum, shift_sum, total = swish_norm_back(
            load_hidden, image, moments_two[image], gain_two, shift_two, put_hidden, none
        )
        share_grad_one[image].start()
        sums["gain_two"].append(gain_sum)
        sums["shift_two"].append(shift_sum)
        sums["bias_one"].append(whole(total))

    def swish_norm_back(load, image, moments, gain, shift, put, start):
        center, rate = moments

        def totals(image, step, carry):
            unit = (load(image, step) - center) * rate
            field = unit * gain + shift
            gate = sigmoid(field)
            grad = delta_at(image, step) * (gate * (1.0 + field * (1.0 - gate)))
            s.delta[flat_at(image, step), :] = grad
            return carry[0] + fold(grad), carry[1] + fold(grad * unit)

        shift_sum, gain_sum = map(whole, over(image, totals, (none, none)))
        mean_shift, mean_gain = norm_back_terms(gain, shift_sum, gain_sum)

        def back(image, step, carry):
            unit = (load(image, step) - center) * rate
            grad = rate * (delta_at(image, step) * gain - mean_shift - unit * mean_gain)
            return put(image, step, grad, carry)

        return gain_sum, shift_sum, over(image, back, start)

    def backward_input(image):
        s.delta[image_rows(image), :] = convolve_back(
            s.spread_one, s.conv_one_here, slice(image, image + 1)
        )
        def put_input(image, step, grad, carry):
            total = grad + s.grad_middle[flat_at(image, step), :]
            s.leaving_grad[image, at(step), :] = total.astype(jnp.bfloat16)
            return carry

        gain_sum, shift_sum, _ = swish_norm_back(
            load_input, image, moments_one[image], gain_one, shift_one, put_input, 0
        )
        swap_grad[image].start()
        sums["gain_one"].append(gain_sum)
        sums["shift_one"].append(shift_sum)

    mix_rows = s.blocks_mix.shape[2] // 4

    def store_mix(which, product):
        product = product.astype(jnp.bfloat16)
        for rank in range(ranks):
            for core in range(2):
                block = rank * 2 + core
                spot = spots_mix[which // 2][rank]
                s.blocks_mix[spot, core, which * mix_rows : (which + 1) * mix_rows, :] = product[
                    block * mix_rows : (block + 1) * mix_rows
                ]

    def weigh_mix():
        upstream = s.upstream[...].reshape(flat_rows, channels)
        normed = s.normed[...]
        store_mix(3, by_rows(s.mixed[...], upstream))
        store_mix(0, by_rows(normed, s.grad_query[...]))
        store_mix(1, by_rows(normed, s.grad_key[...]))
        store_mix(2, by_rows(normed, s.grad_value[...]))

    def column_sums(load):
        def body(image, step, total):
            return total + fold(load(image, step))

        total = none
        for image in every_image:
            total = over(image, body, total)
        return whole(total)

    def fill_slot():
        slot_place = lax.broadcasted_iota(jnp.int32, (slot_rows, lanes), 0)
        slot = jnp.zeros((slot_rows, lanes), jnp.float32)
        for image in every_image:
            for index in range(per_image):
                row = sums["bias_one"][image][:, index * lanes : (index + 1) * lanes]
                slot = jnp.where(
                    slot_place == image * per_image + index,
                    jnp.broadcast_to(row, slot.shape),
                    slot,
                )
        device = place.rank * 2 + place.core
        s.slots[pl.ds(pl.multiple_of(device * slot_rows, slot_rows), slot_rows), :] = slot

    per_image = channels // lanes

    def flat(first, rows):
        count, width = rows.shape[0], rows.shape[1] // lanes
        for index in range(width):
            s.flat[pl.ds(first + index, count, stride=width), :] = rows[
                :, index * lanes : (index + 1) * lanes
            ]

    def embedding_gradients():
        def every(index):
            return s.slots[pl.ds(index, ranks * 2, stride=slot_rows), :]

        device = place.rank * 2 + place.core
        de = jnp.concatenate(
            [
                jnp.concatenate([every(image * per_image + j) for j in range(per_image)], axis=1)
                for image in every_image
            ],
            axis=0,
        )
        place_of = lax.broadcasted_iota(jnp.int32, (images_here * ranks * 2, lanes), 0)
        lane = lax.broadcasted_iota(jnp.int32, place_of.shape, 1)
        wanted = (place_of % (ranks * 2)) // 2 * images_here + place_of // (ranks * 2)
        tiles = [jnp.broadcast_to(s.levels_all[core, 0:1, :], place_of.shape) for core in (0, 1)]
        chosen = jnp.where(place_of % 2 == 0, tiles[0], tiles[1])
        levels = jnp.sum(jnp.where(lane == wanted, chosen, 0.0), axis=1, keepdims=True)
        levels = levels.astype(jnp.int32)
        entry = lax.broadcasted_iota(
            jnp.int32, (levels.shape[0], s.noise_table_here.shape[0]), 1
        )
        hit = jnp.where(entry == levels, 1.0, 0.0).astype(jnp.bfloat16)
        everywhere = matmul(hit, s.noise_table_here[...])
        exact = dict(preferred_element_type=jnp.float32, precision=lax.Precision.HIGHEST)
        own_rows = channels // (ranks * 2)
        s.product[...] = lax.dot_general(everywhere, de, (((0,), (0,)), ((), ())), **exact)
        first = pl.multiple_of(device * own_rows, own_rows)
        flat(spans["embed"], s.product[pl.ds(first, own_rows), :])
        grad_rows = lax.dot_general(
            de, s.embed_weight_here[...].astype(jnp.float32), (((1,), (1,)), ((), ())), **exact
        )
        halves = table_rows * 2 // (ranks * 2)
        wide = -(-halves // 128) * 128
        spot = lax.broadcasted_iota(jnp.int32, (levels.shape[0], wide), 1) + device * halves
        total = jnp.zeros((wide, half), jnp.float32)
        for side in range(2):
            pick = jnp.where(2 * levels + side == spot, 1.0, 0.0)
            total = total + lax.dot_general(
                pick,
                grad_rows[:, side * half : (side + 1) * half],
                (((0,), (0,)), ((), ())),
                **exact,
            )
        flat(spans["table"], total)

    def sum_biases():
        sums["query_bias"].append(column_sums(load_low(s.grad_query)))
        sums["value_bias"].append(column_sums(load_low(s.grad_value)))
        sums["out_bias"].append(column_sums(load_upstream))

    def start_small():
        rows = [functools.reduce(jnp.add, sums[name]) for name in SUMS]
        s.small_sum[0, 0:8, :] = stack_rows(rows[:8])
        s.small_sum[0, 8:16, :] = stack_rows(rows[8:])
        small[0].start()

    def step_all(reduction, stage):
        for part in range(reduction.parts):
            reduction.step(stage, part)

    for image in every_image:
        forward(image)
    for image in every_image:
        swap_output[image].start()
    for image in every_image[:-1]:
        backward(image)
        backward_rest(image)
        backward_input(image)
    backward(images_here - 1)
    backward_rest(images_here - 1)
    fill_slot()
    slots_pair.start()
    weigh_mix()
    reduce_mix.start(0, 0)
    reduce_mix.start(0, 1)
    backward_input(images_here - 1)
    step_all(reduce_mix, 0)
    slots_pair.arrive()
    slots_all.start()
    for image in every_image:
        share_act_two[image].arrive()
        share_grad_two[image].arrive()
    weigh(
        s.spread_two, half_two, s.act_two, s.act_two_far, s.grad_two_far, s.blocks_two, spots_two
    )
    for part in range(parts):
        reduce_two.start(0, part)
    for image in every_image:
        share_act_one[image].arrive()
        share_grad_one[image].arrive()
    weigh(
        s.spread_one, half_one, s.act_one, s.act_one_far, s.grad_one_far, s.blocks_one, spots_one
    )
    for part in range(parts):
        reduce_one.start(0, part)
    step_all(reduce_two, 0)
    sum_biases()
    start_small()
    step_all(reduce_one, 0)
    reduce_two.step(1, 0)
    reduce_two.step(1, 2)
    reduce_one.step(1, 2)
    reduce_mix.step(1, 1)
    reduce_mix.step(1, 0)
    reduce_one.step(1, 0)
    reduce_two.step(1, 1)
    reduce_two.step(2, 0)
    reduce_two.step(2, 2)
    small_step(0)
    reduce_one.step(2, 2)
    reduce_one.step(1, 1)
    reduce_one.step(2, 0)
    reduce_two.step(2, 1)
    reduce_mix.step(2, 1)
    reduce_mix.step(2, 0)
    small_step(1)
    reduce_two.step(3, 0)
    reduce_two.step(3, 2)
    levels_pair.arrive()
    slots_all.arrive()
    embedding_gradients()
    reduce_one.step(3, 0)
    reduce_one.step(3, 2)
    small_step(2)
    reduce_mix.step(3, 1)
    reduce_mix.step(3, 0)
    reduce_one.step(2, 1)
    reduce_two.step(3, 1)
    end_two = share_copy(4 * images_here, s.fin_two.at[1 - half_two], s.last_two, bit_two).start()
    small_step(3)
    reduce_one.step(3, 1)
    end_one = share_copy(
        4 * images_here + 1, s.fin_one.at[1 - half_one], s.last_one, bit_one
    ).start()
    reduce_mix.step(4, 1)
    reduce_mix.step(4, 0)
    for index, name in enumerate(dict(query=0, key=0, value=0, out=0)):
        flat(spans[name], s.share_mix[index * mix_rows : (index + 1) * mix_rows, :])
    small_step(4)
    s.sums[...] = s.small_sum[bits + 1]
    flat(spans["conv_two"], settle(end_two, s.sum_two, s.last_two, half_two))
    flat(spans["conv_one"], settle(end_one, s.sum_one, s.last_one, half_one))

    for flight in flights:
        flight.land()


def last_kernel(starts, rows, *refs):
    output_in, grad_in, flat_in, sums_in, output, grad = refs[:6]
    flats, sums = refs[6 : 6 + len(starts)], refs[6 + len(starts) : -4]
    output_here, grad_here, flat_here, sems = refs[-4:]
    arrive = [
        pltpu.make_async_copy(output_in, output_here, sems.at[0]),
        pltpu.make_async_copy(grad_in, grad_here, sems.at[1]),
        pltpu.make_async_copy(flat_in, flat_here, sems.at[2]),
    ]
    for move in arrive:
        move.start()
    for row, target in zip(rows, sums, strict=True):
        target[...] = sums_in[row : row + 1, :]
    leave = [
        pltpu.make_async_copy(output_here, output, sems.at[3]),
        pltpu.make_async_copy(grad_here, grad, sems.at[4]),
    ]
    for index, (start, target) in enumerate(zip(starts, flats, strict=True)):
        span = flat_here.at[pl.ds(start, target.shape[0]), :]
        leave.append(pltpu.make_async_copy(span, target, sems.at[5 + index]))
    for index, move in enumerate(arrive):
        move.wait()
        for out in leave[index : index + 1] if index < 2 else leave[2:]:
            out.start()
    for move in leave:
        move.wait()


def fused_device(given):
    ranks = lax.axis_size("wide")
    bits = (ranks - 1).bit_length()
    images = given["images"]
    images_rep, piece, channels = images.shape
    images_here, pixels = images_rep // ranks, piece * ranks
    flat_rows = images_here * pixels
    half = channels // 2
    devices = ranks * 2
    table_rows = given["noise_table"].shape[0]
    padded_rows = -(-table_rows // 128) * 128
    conv_rows = given["conv_one"].shape[0] // devices
    mix_rows = 4 * channels // devices
    low, full = jnp.bfloat16, jnp.float32
    parts = 3
    lanes = 128

    def struct(shape, kind):
        return jax.ShapeDtypeStruct(shape, kind)

    def hold(*shape, kind=low):
        return pltpu.VMEM(shape, kind)

    def semaphores(*shape):
        return pltpu.SemaphoreType.DMA(shape)

    def activations():
        return hold(flat_rows, channels)

    def fields():
        return hold(flat_rows, channels, kind=full)

    def square():
        return hold(channels, channels)

    def images_low():
        return hold(images_here, pixels, channels)

    def flat_span(size, pad=False):
        rows = size // lanes
        return -(-rows // 128) * 128 if pad else rows

    share = channels * channels // devices
    sizes = dict(
        conv_one=flat_span(conv_rows * channels),
        conv_two=flat_span(conv_rows * channels),
        query=flat_span(share),
        key=flat_span(share),
        value=flat_span(share),
        out=flat_span(share),
        embed=flat_span(share),
        table=flat_span(table_rows * channels // devices, True),
    )
    spans, start = {}, 0
    for name, size in sizes.items():
        spans[name] = start
        start = start + size

    outputs = dict(
        output=struct(images.shape, low),
        input_grad=struct(images.shape, low),
        flat=struct((start, lanes), full),
        sums=struct((16, channels), full),
    )
    padded = pixels + 2 * SIDE
    halvings = sum(ranks >> stage for stage in range(bits + 1))
    scratch = dict(
        noise_table_here=hold(padded_rows, channels),
        embed_weight_here=square(),
        conv_one_here=hold(*given["conv_one"].shape),
        conv_two_here=hold(*given["conv_two"].shape),
        query_weight_here=square(),
        key_weight_here=square(),
        value_weight_here=square(),
        out_weight_here=square(),
        arrived=images_low(),
        upstream=images_low(),
        leaving=images_low(),
        leaving_grad=images_low(),
        spread_act=hold(images_here, padded, 3 * channels),
        spread_two=hold(images_here, padded, 3 * channels),
        spread_one=hold(images_here, padded, 3 * channels),
        spread_far=hold(images_here, padded, 3 * half),
        hidden=fields(),
        middle=fields(),
        delta=fields(),
        grad_middle=fields(),
        probs=hold(flat_rows, pixels, kind=full),
        act_one=activations(),
        act_two=activations(),
        act_one_far=activations(),
        act_two_far=activations(),
        normed=activations(),
        query=activations(),
        key=activations(),
        value=activations(),
        mixed=activations(),
        grad_mixed=activations(),
        grad_query=activations(),
        grad_key=activations(),
        grad_value=activations(),
        grad_one=activations(),
        grad_two=activations(),
        grad_one_far=hold(flat_rows, half),
        grad_two_far=hold(flat_rows, half),
        blocks_one=hold(ranks, 2, conv_rows, half),
        blocks_two=hold(ranks, 2, conv_rows, half),
        blocks_mix=hold(ranks, 2, mix_rows, channels),
        land_one=hold(halvings - 1, conv_rows, half),
        land_two=hold(halvings - 1, conv_rows, half),
        land_mix=hold(halvings, mix_rows, channels),
        kept_one=hold(halvings - 3, conv_rows, half),
        kept_two=hold(halvings - 3, conv_rows, half),
        kept_mix=hold(halvings - 1, mix_rows, channels),
        sum_one=hold(2, conv_rows, half, kind=full),
        sum_two=hold(2, conv_rows, half, kind=full),
        fin_one=hold(2, conv_rows, half),
        fin_two=hold(2, conv_rows, half),
        last_one=hold(conv_rows, half),
        last_two=hold(conv_rows, half),
        share_mix=hold(mix_rows, channels, kind=full),
        small_sum=hold(bits + 2, 16, channels, kind=full),
        small_land=hold(bits + 1, 16, channels, kind=full),
        slots=hold(devices * 8, lanes, kind=full),
        levels_all=hold(2, 8, lanes, kind=full),
        product=hold(channels, channels, kind=full),
        same_group=hold(half, half),
        load_sem=semaphores(8),
        swap_send=semaphores(4 * images_here),
        swap_recv=semaphores(4 * images_here),
        swap_own=semaphores(4 * images_here),
        share_send=semaphores(4 * images_here + 2),
        share_recv=semaphores(4 * images_here + 2),
        small_send=semaphores(bits + 1),
        small_recv=semaphores(bits + 1),
        slots_send=semaphores(3),
        slots_recv=semaphores(3),
        reduce_send_one=semaphores(bits, parts),
        reduce_recv_one=semaphores(bits, parts),
        reduce_send_two=semaphores(bits, parts),
        reduce_recv_two=semaphores(bits, parts),
        reduce_send_mix=semaphores(bits + 1, 2),
        reduce_recv_mix=semaphores(bits + 1, 2),
    )

    in_vmem = pl.BlockSpec(memory_space=pltpu.VMEM)
    anywhere = pl.BlockSpec(memory_space=pl.ANY)
    in_smem = pl.BlockSpec(memory_space=pltpu.SMEM)
    arrays, in_specs = {}, []
    for name, value in given.items():
        if value.ndim == 1 and value.dtype == full:
            value = value.reshape(1, channels)
            in_specs.append(in_vmem)
        else:
            in_specs.append(in_smem if value.ndim == 1 else anywhere)
        arrays[name] = value
    names = tuple(arrays) + tuple(outputs) + tuple(scratch)
    output, input_grad, flat, sums = pl.pallas_call(
        functools.partial(fused_kernel, names, spans, ranks, table_rows),
        out_shape=tuple(outputs.values()),
        in_specs=in_specs,
        out_specs=(anywhere, anywhere, in_vmem, in_vmem),
        scratch_shapes=list(scratch.values()),
        compiler_params=pltpu.CompilerParams(
            collective_id=0, has_side_effects=True, vmem_limit_bytes=63 << 20
        ),
        name="block",
    )(*arrays.values())

    order = dict(table=0, conv_one=0, conv_two=0, embed=0, query=0, key=0, value=0, out=0)
    sizes["table"] = table_rows * channels // devices // lanes
    finals = [struct((sizes[name], lanes), full) for name in order]
    rows = [SUMS.index(name) for name in GIVEN_BACK]
    results = pl.pallas_call(
        functools.partial(last_kernel, [spans[name] for name in order], rows),
        out_shape=(outputs["output"], outputs["input_grad"], *finals)
        + (struct((1, channels), full),) * len(rows),
        in_specs=[anywhere, anywhere, anywhere, in_vmem],
        out_specs=(anywhere,) * (2 + len(finals)) + (in_vmem,) * len(rows),
        scratch_shapes=[
            hold(*images.shape),
            hold(*images.shape),
            hold(start, lanes, kind=full),
            semaphores(5 + len(finals)),
        ],
        compiler_params=pltpu.CompilerParams(vmem_limit_bytes=63 << 20),
        name="finish",
    )(output, input_grad, flat, sums)
    return tuple(results[:2]) + tuple(member.reshape(-1) for member in results[2:])


def per_device(
    images,
    cotangent,
    levels,
    noise_table,
    gain_one,
    shift_one,
    conv_one,
    bias_one,
    embed_weight,
    embed_bias,
    gain_two,
    shift_two,
    conv_two,
    bias_two,
    gain_three,
    shift_three,
    query_weight,
    query_bias,
    key_weight,
    value_weight,
    value_bias,
    out_weight,
    out_bias,
):
    given = dict(
        images=images,
        cotangent=cotangent,
        levels=levels,
        noise_table=noise_table,
        gain_one=gain_one,
        shift_one=shift_one,
        conv_one=conv_one,
        bias_one=bias_one,
        embed_weight=embed_weight,
        embed_bias=embed_bias,
        gain_two=gain_two,
        shift_two=shift_two,
        conv_two=conv_two,
        bias_two=bias_two,
        gain_three=gain_three,
        shift_three=shift_three,
        query_weight=query_weight,
        query_bias=query_bias,
        key_weight=key_weight,
        value_weight=value_weight,
        value_bias=value_bias,
        out_weight=out_weight,
        out_bias=out_bias,
    )
    ranks, cores = lax.axis_size("wide"), lax.axis_size("rep")
    images_rep, piece, channels = images.shape
    devices = ranks * cores
    fits = (
        cores == 2
        and ranks >= 8
        and ranks & (ranks - 1) == 0
        and images_rep == 2 * ranks
        and piece % 16 == 0
        and conv_one.shape[0] % (devices * 48) == 0
        and channels % (devices * 16) == 0
        and noise_table.size % (devices * channels // 2) == 0
    )
    return fused_device(given) if fits else plain_device(*given.values())


def solution(mesh):
    in_specs = (
        P("rep", "wide", None),
        P("rep", "wide", None),
        P("rep"),
        P(),
        P(),
        P(),
        P(),
        P(),
        P(),
        P(),
        P(),
        P(),
        P(),
        P(),
        P(),
        P(),
        P(),
        P(),
        P(),
        P(),
        P(),
        P(),
        P(),
    )
    out_specs = (
        P("rep", "wide", None),
        P("rep", "wide", None),
        P(("wide", "rep")),
        P(("wide", "rep")),
        P(("wide", "rep")),
        P(("wide", "rep")),
        P(("wide", "rep")),
        P(("wide", "rep")),
        P(("wide", "rep")),
        P(("wide", "rep")),
        P(),
        P(),
        P(),
        P(),
        P(),
        P(),
        P(),
        P(),
        P(),
        P(),
        P(),
        P(),
    )
    return jax.shard_map(
        per_device, mesh=mesh, in_specs=in_specs, out_specs=out_specs, check_vma=False
    )
```

```python
import functools
import types

import jax
import jax.numpy as jnp
from jax import lax
from jax.experimental import pallas as pl
from jax.experimental.pallas import tpu as pltpu
from jax.sharding import PartitionSpec as P

GROUPS = 32
SIDE = 16
MESH = pl.DeviceIdType.MESH
CHUNK = 64


epsilon = 1e-05
highest = lax.Precision.HIGHEST


def swish(field):
    return field * jax.nn.sigmoid(field)


def group_norm(field, norm_gain, norm_shift):
    images_here = field.shape[0]
    channels = field.shape[2]
    grouped = field.reshape(images_here, field.shape[1], GROUPS, channels // GROUPS)
    center = jnp.mean(grouped, axis=(1, 3), keepdims=True)
    spread = grouped - center
    variance = jnp.mean(spread * spread, axis=(1, 3), keepdims=True)
    return (spread * lax.rsqrt(variance + epsilon)).reshape(field.shape) * norm_gain + norm_shift


def norm_swish(field, norm_gain, norm_shift):
    return swish(group_norm(field, norm_gain, norm_shift))


def matmul(left, right):
    return jnp.dot(left, right, preferred_element_type=jnp.float32)


def contract_rows(left, right):
    return lax.dot_general(
        left, right, (((0,), (0,)), ((), ())), preferred_element_type=jnp.float32
    )


def against(left, right):
    return lax.dot_general(
        left, right, (((1,), (1,)), ((), ())), preferred_element_type=jnp.float32
    )


def patches(activation):
    images_here = activation.shape[0]
    grid = activation.reshape(images_here, SIDE, SIDE, activation.shape[2])
    padded = jnp.pad(grid, ((0, 0), (1, 1), (1, 1), (0, 0)))
    pieces = [
        padded[
            :, kernel_tap // 3 : kernel_tap // 3 + SIDE, kernel_tap % 3 : kernel_tap % 3 + SIDE, :
        ]
        for kernel_tap in range(9)
    ]
    return jnp.concatenate(pieces, axis=-1).reshape(images_here * SIDE * SIDE, -1)


def unpatch(columns, images_here):
    channels = columns.shape[1] // 9
    grid = columns.reshape(images_here, SIDE, SIDE, 9, channels)
    summed = jnp.zeros((images_here, SIDE + 2, SIDE + 2, channels), jnp.float32)
    for kernel_tap in range(9):
        row_off = kernel_tap // 3
        col_off = kernel_tap % 3
        summed = summed + jnp.pad(
            grid[:, :, :, kernel_tap, :],
            ((0, 0), (row_off, 2 - row_off), (col_off, 2 - col_off), (0, 0)),
        )
    return summed[:, 1 : SIDE + 1, 1 : SIDE + 1, :].reshape(images_here, SIDE * SIDE, channels)


def plain_device(
    images,
    cotangent,
    levels,
    noise_table,
    gain_one,
    shift_one,
    conv_one,
    bias_one,
    embed_weight,
    embed_bias,
    gain_two,
    shift_two,
    conv_two,
    bias_two,
    gain_three,
    shift_three,
    query_weight,
    query_bias,
    key_weight,
    value_weight,
    value_bias,
    out_weight,
    out_bias,
):
    arrived, upstream = (
        lax.all_to_all(images, "wide", split_axis=0, concat_axis=1, tiled=True),
        lax.all_to_all(cotangent, "wide", split_axis=0, concat_axis=1, tiled=True),
    )
    images_here = arrived.shape[0]
    pixels = arrived.shape[1]
    channels = arrived.shape[2]
    flat_rows = images_here * pixels
    score_scale = channels ** (-0.5)
    table_rows = noise_table.shape[0]
    offset = lax.axis_index("wide") * images_here
    own_levels = lax.dynamic_slice_in_dim(levels, offset, images_here)
    selector = own_levels[:, None] == jnp.arange(table_rows, dtype=jnp.int32)[None, :]
    embedded = matmul(selector.astype(jnp.bfloat16), noise_table).astype(jnp.bfloat16)
    embed_shift = matmul(embedded, embed_weight) + embed_bias
    inputs = arrived.astype(jnp.float32)
    act_one, back_one = jax.vjp(norm_swish, inputs, gain_one, shift_one)
    cols_one = patches(act_one.astype(jnp.bfloat16))
    hidden_one = (matmul(cols_one, conv_one) + bias_one).reshape(images_here, pixels, channels)
    hidden_one = hidden_one + embed_shift[:, None, :]
    act_two, back_two = jax.vjp(norm_swish, hidden_one, gain_two, shift_two)
    cols_two = patches(act_two.astype(jnp.bfloat16))
    branch_out = matmul(cols_two, conv_two) + bias_two
    middle = inputs + branch_out.reshape(images_here, pixels, channels)
    normed, back_three = jax.vjp(group_norm, middle, gain_three, shift_three)
    normed_low = normed.astype(jnp.bfloat16).reshape(flat_rows, channels)
    query_block = (matmul(normed_low, query_weight) + query_bias).astype(jnp.bfloat16)
    key_block = matmul(normed_low, key_weight).astype(jnp.bfloat16)
    value_block = (matmul(normed_low, value_weight) + value_bias).astype(jnp.bfloat16)
    query_block = query_block.reshape(images_here, pixels, channels)
    key_block = key_block.reshape(images_here, pixels, channels)
    value_block = value_block.reshape(images_here, pixels, channels)
    scores = (
        jnp.einsum("npc,nqc->npq", query_block, key_block, preferred_element_type=jnp.float32)
        * score_scale
    )
    row_top = jnp.max(scores, axis=-1, keepdims=True)
    exponent = jnp.exp(scores - row_top)
    row_total = jnp.sum(exponent, axis=-1, keepdims=True)
    probs_low = (exponent / row_total).astype(jnp.bfloat16)
    log_total = row_top + jnp.log(row_total)
    mixed = jnp.einsum("npq,nqc->npc", probs_low, value_block, preferred_element_type=jnp.float32)
    mixed_low = mixed.astype(jnp.bfloat16).reshape(flat_rows, channels)
    result = middle.reshape(flat_rows, channels) + matmul(mixed_low, out_weight) + out_bias
    grad_out = upstream.reshape(flat_rows, channels)
    grad_out_bias = jnp.sum(grad_out.astype(jnp.float32), axis=0)
    grad_out_weight = contract_rows(mixed_low, grad_out)
    grad_mixed = (
        against(grad_out, out_weight).astype(jnp.bfloat16).reshape(images_here, pixels, channels)
    )
    scores_again = (
        jnp.einsum("npc,nqc->npq", query_block, key_block, preferred_element_type=jnp.float32)
        * score_scale
    )
    probs = jnp.exp(scores_again - log_total)
    probs_again = probs.astype(jnp.bfloat16)
    grad_probs = jnp.einsum(
        "npc,nqc->npq", grad_mixed, value_block, preferred_element_type=jnp.float32
    )
    grad_values = jnp.einsum(
        "npq,npc->nqc", probs_again, grad_mixed, preferred_element_type=jnp.float32
    ).astype(jnp.bfloat16)
    grad_scores = probs * (grad_probs - jnp.sum(grad_probs * probs, axis=-1, keepdims=True))
    grad_scores = grad_scores.astype(jnp.bfloat16)
    grad_query = (
        (
            jnp.einsum("npq,nqc->npc", grad_scores, key_block, preferred_element_type=jnp.float32)
            * score_scale
        )
        .astype(jnp.bfloat16)
        .reshape(flat_rows, channels)
    )
    grad_keys = (
        (
            jnp.einsum("npq,npc->nqc", grad_scores, query_block, preferred_element_type=jnp.float32)
            * score_scale
        )
        .astype(jnp.bfloat16)
        .reshape(flat_rows, channels)
    )
    grad_values = grad_values.reshape(flat_rows, channels)
    grad_query_weight = contract_rows(normed_low, grad_query)
    grad_key_weight = contract_rows(normed_low, grad_keys)
    grad_value_weight = contract_rows(normed_low, grad_values)
    grad_query_bias = jnp.sum(grad_query.astype(jnp.float32), axis=0)
    grad_value_bias = jnp.sum(grad_values.astype(jnp.float32), axis=0)
    grad_normed = against(grad_query, query_weight) + against(grad_keys, key_weight)
    grad_normed = grad_normed + against(grad_values, value_weight)
    grad_middle, grad_gain_three, grad_shift_three = back_three(
        grad_normed.reshape(images_here, pixels, channels)
    )
    grad_middle = grad_middle + upstream.astype(jnp.float32)
    grad_branch = grad_middle.astype(jnp.bfloat16).reshape(flat_rows, channels)
    grad_bias_two = jnp.sum(grad_branch.astype(jnp.float32), axis=0)
    grad_conv_two = contract_rows(cols_two, grad_branch)
    grad_act_two = unpatch(against(grad_branch, conv_two), images_here)
    grad_hidden, grad_gain_two, grad_shift_two = back_two(grad_act_two)
    grad_hidden_low = grad_hidden.astype(jnp.bfloat16)
    hidden_rows = grad_hidden_low.reshape(flat_rows, channels)
    grad_bias_one = jnp.sum(hidden_rows.astype(jnp.float32), axis=0)
    grad_conv_one = contract_rows(cols_one, hidden_rows)
    grad_shift = jnp.sum(grad_hidden_low.astype(jnp.float32), axis=1)
    grad_embed_bias = jnp.sum(grad_shift, axis=0)
    grad_embed_weight = jnp.dot(embedded.astype(jnp.float32).T, grad_shift, precision=highest)
    embed_float = embed_weight.astype(jnp.float32)
    grad_act_one = unpatch(against(hidden_rows, conv_one), images_here)
    grad_input_part, grad_gain_one, grad_shift_one = back_one(grad_act_one)
    grad_input = grad_middle + grad_input_part
    output_back, input_back = (
        lax.all_to_all(
            result.reshape(images_here, pixels, channels).astype(jnp.bfloat16),
            "wide",
            split_axis=1,
            concat_axis=0,
            tiled=True,
        ),
        lax.all_to_all(
            grad_input.astype(jnp.bfloat16), "wide", split_axis=1, concat_axis=0, tiled=True
        ),
    )
    wide_count = lax.axis_size("wide")
    rep_count = lax.axis_size("rep")
    device_count = wide_count * rep_count
    weight_grads = (
        grad_conv_one,
        grad_conv_two,
        grad_embed_weight,
        grad_query_weight,
        grad_key_weight,
        grad_value_weight,
        grad_out_weight,
    )
    grad_embedded = jnp.dot(grad_shift, embed_float.T, precision=highest)
    grad_table = jnp.dot(selector.astype(jnp.float32).T, grad_embedded, precision=highest)
    members = (grad_table,) + weight_grads
    widths = [member.size // device_count for member in members]
    packed = jnp.concatenate([member.reshape(device_count, -1) for member in members], axis=1)
    packed = lax.psum_scatter(packed, ("wide", "rep"), scatter_dimension=0, tiled=True)
    packed = packed.reshape(-1)
    large_grads = []
    start_at = 0
    for width in widths:
        large_grads.append(packed[start_at : start_at + width])
        start_at = start_at + width
    large_grads = tuple(large_grads)
    small_grads = lax.psum(
        (
            grad_gain_one,
            grad_shift_one,
            grad_bias_one,
            grad_embed_bias,
            grad_gain_two,
            grad_shift_two,
            grad_bias_two,
            grad_gain_three,
            grad_shift_three,
            grad_query_bias,
            grad_value_bias,
            grad_out_bias,
        ),
        ("wide", "rep"),
    )
    return (output_back, input_back) + large_grads + tuple(small_grads)


def by_rows(left, right):
    return lax.dot_general(
        left, right, (((0,), (0,)), ((), ())), preferred_element_type=jnp.float32
    )


def group_sum(rows, same_group):
    width = same_group.shape[0]
    first = rows.astype(jnp.bfloat16).astype(jnp.float32)
    rest = rows - first
    second = rest.astype(jnp.bfloat16).astype(jnp.float32)
    terms = (first, second, rest - second)
    spans = [slice(start, start + width) for start in range(0, rows.shape[1], width)]
    stacked = jnp.concatenate([term[:, span] for span in spans for term in terms], axis=0)
    summed = matmul(stacked.astype(jnp.bfloat16), same_group)
    parts = [summed[24 * k : 24 * k + 24] for k in range(len(spans))]
    return jnp.concatenate([part[0:8] + part[8:16] + part[16:24] for part in parts], axis=1)


def stack_rows(members):
    shape = (8, members[0].shape[1])
    place = lax.broadcasted_iota(jnp.int32, shape, 0)
    stacked = jnp.zeros(shape, jnp.float32)
    for index, member in enumerate(members):
        stacked = jnp.where(place == index, jnp.broadcast_to(member, shape), stacked)
    return stacked


def sigmoid(field):
    return 0.5 + 0.5 * jnp.tanh(0.5 * field)


SUMS = tuple(
    dict(
        gain_one=0,
        shift_one=0,
        bias_one=0,
        gain_two=0,
        shift_two=0,
        bias_two=0,
        gain_three=0,
        shift_three=0,
        query_bias=0,
        value_bias=0,
        out_bias=0,
    )
)
GIVEN_BACK = SUMS[:3] + SUMS[2:]


class Flight:
    def __init__(self, flights, make, offsets=None, whole=None, own=None):
        self.flights, self.make, self.offsets, self.own = flights, make, offsets, own
        self.whole = make if whole is None else whole
        self.arrived = self.left = False

    def start(self):
        if self.offsets is None:
            self.make().start()
        else:

            def go(offset, carry):
                self.make(offset).start()
                return carry

            lax.fori_loop(*self.offsets, go, 0)
        if self.own is not None:
            self.own().start()
        self.flights.append(self)
        return self

    def arrive(self):
        self.whole().wait_recv()
        if self.own is not None:
            self.own().wait()
        self.arrived = True

    def leave(self):
        self.whole().wait_send()
        self.left = True

    def land(self):
        if not self.arrived:
            self.arrive()
        if not self.left:
            self.leave()


class Reduce:
    def __init__(self, flights, place, blocks, orders, landing, kept, send, recv, last, spread):
        self.flights, self.place = flights, place
        self.blocks, self.orders, self.last = blocks, orders, last
        self.landing, self.kept, self.send, self.recv = landing, kept, send, recv
        self.spread, self.stages = spread, max(len(order) for order in orders)
        self.rows = blocks.shape[2]
        self.parts = send.shape[1]
        self.under_way = {}

    def cut(self, part):
        size = self.rows // self.parts
        return pl.ds(part * size, size)

    def copy(self, stage, part):
        place, rows = self.place, self.cut(part)
        if stage == 0:
            source = self.blocks.at[:, 1 - place.core, rows, :]
            target = place.other_core
        else:
            count = self.blocks.shape[0] >> stage
            bit = self.orders[part][stage - 1]
            source = self.kept[stage - 1].at[
                pl.ds((1 - place.bit(bit)) * count, count), rows, :
            ]
            target = place.across(bit)
        return pltpu.make_async_remote_copy(
            src_ref=source,
            dst_ref=self.landing[stage].at[:, rows, :],
            send_sem=self.send.at[stage, part],
            recv_sem=self.recv.at[stage, part],
            device_id=target,
            device_id_type=MESH,
        )

    def start(self, stage, part):
        copy = functools.partial(self.copy, stage, part)
        self.under_way[stage, part] = Flight(self.flights, copy).start()

    def step(self, stage, part):
        self.finish(stage, part)
        if stage < len(self.orders[part]):
            self.start(stage + 1, part)
        elif stage < self.stages:
            self.spread(self.kept[stage], self.cut(part))

    def finish(self, stage, part):
        place, rows = self.place, self.cut(part)
        self.under_way[stage, part].arrive()
        count = self.blocks.shape[0] >> stage
        if stage == 0:
            own = self.blocks[:, place.core, rows, :]
        else:
            first = place.bit(self.orders[part][stage - 1]) * count
            own = self.kept[stage - 1][pl.ds(first, count), rows, :]
        landed = self.landing[stage][:, rows, :]
        if stage < self.stages:
            self.kept[stage][:, rows, :] = own + landed
        else:
            self.last(rows, own.astype(jnp.float32) + landed.astype(jnp.float32))


class Place:
    def __init__(self, ranks):
        self.ranks = ranks
        self.rank = lax.axis_index("wide")
        self.core = lax.axis_index("rep")
        self.other_core = (self.rank, 1 - self.core)

    def bit(self, index):
        return (self.rank // (1 << index)) % 2

    def across(self, index):
        step = 1 << index
        return (self.rank + step - 2 * step * self.bit(index), self.core)


def block_order(ranks, order):
    places = []
    for rank in range(ranks):
        spot = 0
        for bit in order:
            spot = spot * 2 + (rank >> bit) % 2
        places.append(spot)
    return places


def fused_kernel(names, spans, ranks, table_rows, *refs):
    s = types.SimpleNamespace(**dict(zip(names, refs, strict=True)))
    place = Place(ranks)
    bits = (ranks - 1).bit_length()
    far = list(range(2, bits))
    images_here, pixels, channels = s.arrived.shape
    every_image = range(images_here)
    flat_rows = images_here * pixels
    piece = pixels // ranks
    half = channels // 2
    steps = pixels // CHUNK
    score_scale = channels ** (-0.5)
    count_inverse = 1.0 / (pixels * (channels // GROUPS))
    col = lax.broadcasted_iota(jnp.int32, (CHUNK, 1), 0) % SIDE
    flights = []

    def image_rows(image):
        return slice(image * pixels, (image + 1) * pixels)

    barrier = pltpu.get_barrier_semaphore()

    def greet(offset, carry):
        pl.semaphore_signal(
            barrier,
            inc=1,
            device_id=((place.rank + offset) % ranks, place.core),
            device_id_type=MESH,
        )
        return carry

    lax.fori_loop(1, ranks, greet, 0)
    pl.semaphore_signal(barrier, inc=1, device_id=place.other_core, device_id_type=MESH)

    pairs = (
        (s.noise_table, s.noise_table_here.at[pl.ds(0, table_rows), :]),
        (s.embed_weight, s.embed_weight_here),
        (s.conv_one, s.conv_one_here),
        (s.conv_two, s.conv_two_here),
        (s.query_weight, s.query_weight_here),
        (s.key_weight, s.key_weight_here),
        (s.value_weight, s.value_weight_here),
        (s.out_weight, s.out_weight_here),
    )
    loads = []
    for index, (source, target) in enumerate(pairs):
        loads.append(pltpu.make_async_copy(source, target, s.load_sem.at[index]))
        loads[-1].start()
    pl.semaphore_wait(barrier, ranks)

    def gather_copy(slot, source, target, image, offset):
        peer = (place.rank + offset) % ranks
        return pltpu.make_async_remote_copy(
            src_ref=source.at[peer * images_here + image],
            dst_ref=target.at[image, pl.ds(pl.multiple_of(place.rank * piece, 16), piece)],
            send_sem=s.swap_send.at[slot],
            recv_sem=s.swap_recv.at[slot],
            device_id=(peer, place.core),
            device_id_type=MESH,
        )

    def gather_own(slot, source, target, image):
        return pltpu.make_async_copy(
            source.at[place.rank * images_here + image],
            target.at[image, pl.ds(pl.multiple_of(place.rank * piece, 16), piece)],
            s.swap_own.at[slot],
        )

    def scatter_copy(slot, source, target, image, offset):
        peer = (place.rank + offset) % ranks
        return pltpu.make_async_remote_copy(
            src_ref=source.at[image, pl.ds(pl.multiple_of(peer * piece, 16), piece)],
            dst_ref=target.at[place.rank * images_here + image],
            send_sem=s.swap_send.at[slot],
            recv_sem=s.swap_recv.at[slot],
            device_id=(peer, place.core),
            device_id_type=MESH,
        )

    def scatter_own(slot, source, target, image):
        return pltpu.make_async_copy(
            source.at[image, pl.ds(pl.multiple_of(place.rank * piece, 16), piece)],
            target.at[place.rank * images_here + image],
            s.swap_own.at[slot],
        )

    def swap_whole(slot, held, image):
        others = held.at[image, pl.ds(0, pixels - piece)]
        return pltpu.make_async_remote_copy(
            src_ref=others,
            dst_ref=others,
            send_sem=s.swap_send.at[slot],
            recv_sem=s.swap_recv.at[slot],
            device_id=place.across(0),
            device_id_type=MESH,
        )

    def swaps(copy, own, which, source, target, held):
        return [
            Flight(
                flights,
                functools.partial(copy, which * images_here + image, source, target, image),
                (1, ranks),
                functools.partial(swap_whole, which * images_here + image, held, image),
                functools.partial(own, which * images_here + image, source, target, image),
            )
            for image in every_image
        ]

    swap_images = swaps(gather_copy, gather_own, 0, s.images, s.arrived, s.arrived)
    swap_upstream = swaps(gather_copy, gather_own, 1, s.cotangent, s.upstream, s.upstream)
    swap_output = swaps(scatter_copy, scatter_own, 2, s.leaving, s.output, s.leaving)
    swap_grad = swaps(scatter_copy, scatter_own, 3, s.leaving_grad, s.input_grad, s.leaving_grad)
    for image in every_image:
        swap_images[image].start()
    for image in every_image:
        swap_upstream[image].start()

    for padded in (s.spread_act, s.spread_two, s.spread_one, s.spread_far):
        for image in every_image:
            edge = jnp.zeros((SIDE, padded.shape[2]), jnp.bfloat16)
            padded[image, 0:SIDE, :] = edge
            padded[image, pixels + SIDE : pixels + 2 * SIDE, :] = edge
    tail = s.noise_table_here.shape[0] - table_rows
    if tail:
        s.noise_table_here[table_rows:, :] = jnp.zeros((tail, channels), jnp.bfloat16)
    own_levels = [s.levels[place.rank * images_here + image] for image in every_image]
    lane = lax.broadcasted_iota(jnp.int32, s.levels_all.shape[1:], 1)
    tile = jnp.zeros(lane.shape, jnp.float32)
    for index in range(ranks * images_here):
        tile = jnp.where(lane == index, s.levels[index].astype(jnp.float32), tile)
    s.levels_all[place.core] = tile

    def levels_copy():
        return pltpu.make_async_remote_copy(
            src_ref=s.levels_all.at[place.core],
            dst_ref=s.levels_all.at[place.core],
            send_sem=s.slots_send.at[2],
            recv_sem=s.slots_recv.at[2],
            device_id=place.other_core,
            device_id_type=MESH,
        )

    levels_pair = Flight(flights, levels_copy).start()
    entry = lax.broadcasted_iota(jnp.int32, (8, s.noise_table_here.shape[0]), 1)
    line = lax.broadcasted_iota(jnp.int32, entry.shape, 0)
    selected = jnp.zeros(entry.shape, jnp.float32)
    for image in every_image:
        hit = jnp.where(entry == own_levels[image], 1.0, 0.0)
        selected = jnp.where(line == image, hit, selected)
    loads[0].wait()
    loads[1].wait()
    embedded = matmul(selected.astype(jnp.bfloat16), s.noise_table_here[...])
    embed_shift = matmul(embedded.astype(jnp.bfloat16), s.embed_weight_here[...])
    embed_shift = embed_shift + s.embed_bias[...] + s.bias_one[...]

    def over(image, body, start):
        return lax.fori_loop(0, steps, functools.partial(body, image), start)

    def at(step):
        return pl.ds(pl.multiple_of(step * CHUNK, CHUNK), CHUNK)

    def flat_at(image, step):
        return pl.ds(pl.multiple_of(image * pixels + step * CHUNK, CHUNK), CHUNK)

    def fold(chunk):
        return jnp.sum(chunk.reshape(CHUNK // 8, 8, channels), axis=0)

    none = jnp.zeros((8, channels), jnp.float32)

    def whole(part):
        return jnp.sum(part, axis=0, keepdims=True)

    group_width = s.same_group.shape[0]
    same_group = [
        lax.broadcasted_iota(jnp.int32, (group_width, group_width), axis)
        // (channels // GROUPS)
        for axis in range(2)
    ]
    s.same_group[...] = jnp.where(same_group[0] == same_group[1], 1.0, 0.0).astype(jnp.bfloat16)

    def group_total(row):
        rows = jnp.broadcast_to(row, (8, channels))
        return group_sum(rows, s.same_group[...])[0:1] * count_inverse

    def statistics(load, image):
        def first(image, step, total):
            return total + fold(load(image, step))

        center = group_total(whole(over(image, first, none)))

        def second(image, step, total):
            spread = load(image, step) - center
            return total + fold(spread * spread)

        variance = group_total(whole(over(image, second, none)))
        return center, lax.rsqrt(variance + epsilon)

    def spread_out(target, image, step, chunk, before, after):
        width = chunk.shape[1]
        rows = pl.ds(pl.multiple_of(step * CHUNK + SIDE, SIDE), CHUNK)
        target[image, rows, before * width : (before + 1) * width] = jnp.where(
            col > 0, pltpu.roll(chunk, 1, 0), 0.0
        ).astype(jnp.bfloat16)
        target[image, rows, width : 2 * width] = chunk.astype(jnp.bfloat16)
        target[image, rows, after * width : (after + 1) * width] = jnp.where(
            col < SIDE - 1, pltpu.roll(chunk, CHUNK - 1, 0), 0.0
        ).astype(jnp.bfloat16)

    def activate(load, image, moments, gain, shift, keep):
        center, rate = moments
        slope = rate * gain

        def apply(image, step, carry):
            field = (load(image, step) - center) * slope + shift
            act = field * sigmoid(field)
            spread_out(s.spread_act, image, step, act, 0, 2)
            keep[flat_at(image, step), :] = act.astype(jnp.bfloat16)
            return carry

        over(image, apply, 0)

    def convolve(weight, image):
        total = None
        for row_tap in range(3):
            term = matmul(
                s.spread_act[image, SIDE * row_tap : SIDE * row_tap + pixels, :],
                weight[3 * channels * row_tap : 3 * channels * (row_tap + 1), :],
            )
            total = term if total is None else total + term
        return total

    def tap_rows(row_tap):
        return slice(SIDE * (2 - row_tap), SIDE * (2 - row_tap) + pixels)

    def convolve_back(source, weight, images):
        total = None
        for tap in range(9):
            window = source[
                images, tap_rows(tap // 3), (tap % 3) * channels : (tap % 3 + 1) * channels
            ]
            term = against(
                window.reshape(-1, channels), weight[channels * tap : channels * (tap + 1), :]
            )
            total = term if total is None else total + term
        return total

    def share_copy(slot, source, target, bit):
        def make():
            return pltpu.make_async_remote_copy(
                src_ref=source,
                dst_ref=target,
                send_sem=s.share_send.at[slot],
                recv_sem=s.share_recv.at[slot],
                device_id=place.across(bit),
                device_id_type=MESH,
            )

        return Flight(flights, make)

    bit_one, bit_two = 1, 0
    half_one, half_two = place.bit(bit_one), place.bit(bit_two)

    def shares(which, source, target, bit, mine=None):
        made = []
        for image in every_image:
            rows = pl.ds(image * pixels, pixels)
            lanes_sent = pl.ds(0, channels)
            if mine is not None:
                lanes_sent = pl.ds(pl.multiple_of((1 - mine) * half, half), half)
            made.append(
                share_copy(
                    which * images_here + image,
                    source.at[rows, lanes_sent],
                    target.at[rows, :],
                    bit,
                )
            )
        return made

    share_act_one = shares(0, s.act_one, s.act_one_far, bit_one)
    share_act_two = shares(1, s.act_two, s.act_two_far, bit_two)
    share_grad_two = shares(2, s.grad_two, s.grad_two_far, bit_two, half_two)
    share_grad_one = shares(3, s.grad_one, s.grad_one_far, bit_one, half_one)

    def weigh(spread, mine, act, act_far, grad_far, blocks, spots):
        def unfold(image, step, carry):
            chunk = grad_far[flat_at(image, step), :].astype(jnp.float32)
            spread_out(s.spread_far, image, step, chunk, 2, 0)
            return carry

        for image in every_image:
            over(image, unfold, 0)
        rows_block = blocks.shape[2]
        rows_part = rows_block // len(spots)
        for tap in range(9):
            rows, side_tap = tap_rows(tap // 3), tap % 3
            near = spread[
                :, rows, pl.ds(pl.multiple_of(side_tap * channels + mine * half, half), half)
            ]
            beyond = s.spread_far[:, rows, side_tap * half : (side_tap + 1) * half]
            product = by_rows(act[...], near.reshape(flat_rows, half)) + by_rows(
                act_far[...], beyond.reshape(flat_rows, half)
            )
            product = product.astype(jnp.bfloat16)
            done = 0
            while done < channels:
                block, inside = divmod(tap * channels + done, rows_block)
                part = inside // rows_part
                size = min(rows_part * (part + 1) - inside, channels - done)
                blocks[spots[part][block // 2], block % 2, inside : inside + size, :] = product[
                    done : done + size
                ]
                done = done + size

    orders_one = [[1 - bit_one] + far, far + [1 - bit_one], [1 - bit_one]]
    orders_two = [[1 - bit_two] + far, far + [1 - bit_two], [1 - bit_two]]
    orders_mix = [[0, 1] + far, [1, 0] + far]
    tails_one, tails_two = ([bit_one],) * 2 + (far + [bit_one],), ([bit_two],) * 2 + (far + [bit_two],)
    spots_one = [
        block_order(ranks, order + end) for order, end in zip(orders_one, tails_one, strict=True)
    ]
    spots_two = [
        block_order(ranks, order + end) for order, end in zip(orders_two, tails_two, strict=True)
    ]
    spots_mix = [block_order(ranks, order) for order in orders_mix]

    def put_one(rows, total):
        s.sum_one[:, rows, :] = total
        s.fin_one[:, rows, :] = total.astype(jnp.bfloat16)

    def put_two(rows, total):
        s.sum_two[:, rows, :] = total
        s.fin_two[:, rows, :] = total.astype(jnp.bfloat16)

    def put_mix(rows, total):
        s.share_mix[rows, :] = total[0]

    owners = ranks // 2

    def straight(slot, bit, land):
        order = far + [bit]
        weights = [1 << (len(order) - 1 - k) for k in range(len(order))]
        own = sum(place.bit(b) * weight for b, weight in zip(order, weights, strict=True))
        other = 1 - bit

        def send(kept, rows):
            land[own] = kept[own, rows, :]

            def make(offset):
                target = (own + offset) % owners
                rank = place.bit(other) * (1 << other)
                for b, weight in zip(order, weights, strict=True):
                    rank = rank + (target // weight) % 2 * (1 << b)
                return pltpu.make_async_remote_copy(
                    src_ref=kept.at[target, rows, :],
                    dst_ref=land.at[own],
                    send_sem=s.straight_send.at[slot],
                    recv_sem=s.straight_recv.at[slot],
                    device_id=(rank, place.core),
                    device_id_type=MESH,
                )

            def everything():
                others = land.at[pl.ds(0, owners - 1)]
                return pltpu.make_async_remote_copy(
                    src_ref=others,
                    dst_ref=others,
                    send_sem=s.straight_send.at[slot],
                    recv_sem=s.straight_recv.at[slot],
                    device_id=place.across(0),
                    device_id_type=MESH,
                )

            flight_to[slot] = Flight(flights, make, (1, owners), everything).start()

        return send

    flight_to = {}

    def gather_straight(slot, land):
        flight_to[slot].arrive()
        sides = []
        for side in (0, 1):
            total = land[side].astype(jnp.float32)
            for index in range(side + 2, owners, 2):
                total = total + land[index].astype(jnp.float32)
            sides.append(total)
        return jnp.concatenate(sides, axis=1)

    def staged(ref, first, stages):
        views, start = [], 0
        for stage in range(stages):
            views.append(ref.at[pl.ds(start, first >> stage)])
            start = start + (first >> stage)
        return views

    def reduction(blocks, order, landing, kept, send, recv, put, spread=None):
        stages = len(order[0])
        return Reduce(
            flights,
            place,
            blocks,
            order,
            staged(landing, ranks, stages + 1),
            staged(kept, ranks, stages),
            send,
            recv,
            put,
            spread,
        )

    reduce_one = reduction(
        s.blocks_one,
        orders_one,
        s.land_one,
        s.kept_one,
        s.reduce_send_one,
        s.reduce_recv_one,
        put_one,
        straight(0, bit_one, s.straight_one),
    )
    reduce_two = reduction(
        s.blocks_two,
        orders_two,
        s.land_two,
        s.kept_two,
        s.reduce_send_two,
        s.reduce_recv_two,
        put_two,
        straight(1, bit_two, s.straight_two),
    )
    reduce_mix = reduction(
        s.blocks_mix,
        orders_mix,
        s.land_mix,
        s.kept_mix,
        s.reduce_send_mix,
        s.reduce_recv_mix,
        put_mix,
    )
    parts = reduce_one.parts
    chain_rows = s.last_one.shape[0]
    chain = pl.ds(0, chain_rows)

    def settle(flight, sums, target, mine):
        flight.arrive()
        own = sums[mine, 0:chain_rows, :]
        other = target[...].astype(jnp.float32)
        left = jnp.where(mine == 0, own, other)
        right = jnp.where(mine == 0, other, own)
        return jnp.concatenate([left, right], axis=1)

    def small_copy(stage):
        return pltpu.make_async_remote_copy(
            src_ref=s.small_sum.at[stage],
            dst_ref=s.small_land.at[stage],
            send_sem=s.small_send.at[stage],
            recv_sem=s.small_recv.at[stage],
            device_id=place.other_core if stage == 0 else place.across(stage - 1),
            device_id_type=MESH,
        )

    small = [Flight(flights, functools.partial(small_copy, k)) for k in range(bits + 1)]

    def small_step(stage):
        small[stage].arrive()
        s.small_sum[stage + 1] = s.small_sum[stage] + s.small_land[stage]
        if stage < bits:
            small[stage + 1].start()

    slot_rows = 8
    lanes = s.slots.shape[1]

    def pair_window():
        return s.slots.at[pl.ds(pl.multiple_of(place.rank * 2 * slot_rows, 16), 2 * slot_rows), :]

    def slot_copy():
        first = pl.multiple_of((place.rank * 2 + place.core) * slot_rows, slot_rows)
        window = s.slots.at[pl.ds(first, slot_rows), :]
        return pltpu.make_async_remote_copy(
            src_ref=window,
            dst_ref=window,
            send_sem=s.slots_send.at[0],
            recv_sem=s.slots_recv.at[0],
            device_id=place.other_core,
            device_id_type=MESH,
        )

    def pair_copy(offset):
        return pltpu.make_async_remote_copy(
            src_ref=pair_window(),
            dst_ref=pair_window(),
            send_sem=s.slots_send.at[1],
            recv_sem=s.slots_recv.at[1],
            device_id=((place.rank + offset) % ranks, place.core),
            device_id_type=MESH,
        )

    slots_pair = Flight(flights, slot_copy)
    def pairs_whole():
        others = s.slots.at[pl.ds(0, (ranks - 1) * 2 * slot_rows), :]
        return pltpu.make_async_remote_copy(
            src_ref=others,
            dst_ref=others,
            send_sem=s.slots_send.at[1],
            recv_sem=s.slots_recv.at[1],
            device_id=place.across(0),
            device_id_type=MESH,
        )

    slots_all = Flight(flights, pair_copy, (1, ranks), pairs_whole)

    def load_input(image, step):
        return s.arrived[image, at(step), :].astype(jnp.float32)

    def load_hidden(image, step):
        return s.hidden[flat_at(image, step), :]

    def load_middle(image, step):
        return s.middle[flat_at(image, step), :]

    def load_upstream(image, step):
        return s.upstream[image, at(step), :].astype(jnp.float32)

    def delta_at(image, step):
        return s.delta[flat_at(image, step), :]

    def load_low(ref):
        return lambda image, step: ref[flat_at(image, step), :].astype(jnp.float32)

    gain_one, shift_one = s.gain_one[...], s.shift_one[...]
    gain_two, shift_two = s.gain_two[...], s.shift_two[...]
    gain_three, shift_three = s.gain_three[...], s.shift_three[...]
    moments_one, moments_two, moments_three = [], [], []
    sums = {name: [] for name in SUMS}

    def forward(image):
        rows = image_rows(image)
        swap_images[image].arrive()
        moments_one.append(statistics(load_input, image))
        activate(load_input, image, moments_one[image], gain_one, shift_one, s.act_one)
        share_act_one[image].start()
        if image == 0:
            loads[2].wait()
        s.hidden[rows, :] = convolve(s.conv_one_here, image) + embed_shift[image : image + 1]
        moments_two.append(statistics(load_hidden, image))
        activate(load_hidden, image, moments_two[image], gain_two, shift_two, s.act_two)
        share_act_two[image].start()
        if image == 0:
            loads[3].wait()
        s.middle[rows, :] = (
            convolve(s.conv_two_here, image)
            + s.bias_two[...]
            + s.arrived[image].astype(jnp.float32)
        )
        moments_three.append(statistics(load_middle, image))
        center, rate = moments_three[image]
        slope = rate * gain_three

        def normalize(image, step, carry):
            field = (load_middle(image, step) - center) * slope + shift_three
            s.normed[flat_at(image, step), :] = field.astype(jnp.bfloat16)
            return carry

        over(image, normalize, 0)
        if image == 0:
            for load in loads[4:]:
                load.wait()
        normed = s.normed[rows, :]
        query = (matmul(normed, s.query_weight_here[...]) + s.query_bias[...]).astype(jnp.bfloat16)
        key = matmul(normed, s.key_weight_here[...]).astype(jnp.bfloat16)
        value = (matmul(normed, s.value_weight_here[...]) + s.value_bias[...]).astype(jnp.bfloat16)
        s.query[rows, :] = query
        s.key[rows, :] = key
        s.value[rows, :] = value
        scores = against(query, key) * score_scale
        exponent = jnp.exp(scores - jnp.max(scores, axis=1, keepdims=True))
        probs = exponent / jnp.sum(exponent, axis=1, keepdims=True)
        s.probs[rows, :] = probs
        mixed = matmul(probs.astype(jnp.bfloat16), value).astype(jnp.bfloat16)
        s.mixed[rows, :] = mixed
        result = s.middle[rows, :] + matmul(mixed, s.out_weight_here[...]) + s.out_bias[...]
        s.leaving[image] = result.astype(jnp.bfloat16)

    def norm_back_terms(gain, shift_sum, gain_sum):
        rows = stack_rows([gain * shift_sum, gain * gain_sum])
        means = group_sum(rows, s.same_group[...]) * count_inverse
        return means[0:1], means[1:2]

    def backward(image):
        rows = image_rows(image)
        swap_upstream[image].arrive()
        probs = s.probs[rows, :]
        query, key, value = s.query[rows, :], s.key[rows, :], s.value[rows, :]
        grad_mixed = against(s.upstream[image], s.out_weight_here[...]).astype(jnp.bfloat16)
        grad_probs = against(grad_mixed, value)
        grad_value = by_rows(probs.astype(jnp.bfloat16), grad_mixed).astype(jnp.bfloat16)
        inner = jnp.sum(grad_probs * probs, axis=1, keepdims=True)
        grad_scores = (probs * (grad_probs - inner)).astype(jnp.bfloat16)
        grad_query = (matmul(grad_scores, key) * score_scale).astype(jnp.bfloat16)
        grad_key = (by_rows(grad_scores, query) * score_scale).astype(jnp.bfloat16)
        s.grad_value[rows, :] = grad_value
        s.grad_query[rows, :] = grad_query
        s.grad_key[rows, :] = grad_key
        s.delta[rows, :] = (
            against(grad_query, s.query_weight_here[...])
            + against(grad_key, s.key_weight_here[...])
            + against(grad_value, s.value_weight_here[...])
        )

    def backward_rest(image, between=None):
        rows = image_rows(image)
        center, rate = moments_three[image]

        def sums_three(image, step, totals):
            grad = delta_at(image, step)
            unit = (load_middle(image, step) - center) * rate
            return totals[0] + fold(grad), totals[1] + fold(grad * unit)

        shift_sum, gain_sum = map(whole, over(image, sums_three, (none, none)))
        sums["gain_three"].append(gain_sum)
        sums["shift_three"].append(shift_sum)
        mean_shift, mean_gain = norm_back_terms(gain_three, shift_sum, gain_sum)

        def back_three(image, step, total):
            unit = (load_middle(image, step) - center) * rate
            grad = rate * (delta_at(image, step) * gain_three - mean_shift - unit * mean_gain)
            grad = grad + load_upstream(image, step)
            s.grad_middle[flat_at(image, step), :] = grad
            low = grad.astype(jnp.bfloat16)
            s.grad_two[flat_at(image, step), :] = low
            low = low.astype(jnp.float32)
            spread_out(s.spread_two, image, step, low, 2, 0)
            return total + fold(low)

        sums["bias_two"].append(whole(over(image, back_three, none)))
        share_grad_two[image].start()
        if between is not None:
            between()

        s.delta[rows, :] = convolve_back(s.spread_two, s.conv_two_here, slice(image, image + 1))

        def put_hidden(image, step, grad, total):
            low = grad.astype(jnp.bfloat16)
            s.grad_one[flat_at(image, step), :] = low
            low = low.astype(jnp.float32)
            spread_out(s.spread_one, image, step, low, 2, 0)
            return total + fold(low)

        gain_sum, shift_sum, total = swish_norm_back(
            load_hidden, image, moments_two[image], gain_two, shift_two, put_hidden, none
        )
        share_grad_one[image].start()
        sums["gain_two"].append(gain_sum)
        sums["shift_two"].append(shift_sum)
        sums["bias_one"].append(whole(total))

    def swish_norm_back(load, image, moments, gain, shift, put, start):
        center, rate = moments

        def totals(image, step, carry):
            unit = (load(image, step) - center) * rate
            field = unit * gain + shift
            gate = sigmoid(field)
            grad = delta_at(image, step) * (gate * (1.0 + field * (1.0 - gate)))
            s.delta[flat_at(image, step), :] = grad
            return carry[0] + fold(grad), carry[1] + fold(grad * unit)

        shift_sum, gain_sum = map(whole, over(image, totals, (none, none)))
        mean_shift, mean_gain = norm_back_terms(gain, shift_sum, gain_sum)

        def back(image, step, carry):
            unit = (load(image, step) - center) * rate
            grad = rate * (delta_at(image, step) * gain - mean_shift - unit * mean_gain)
            return put(image, step, grad, carry)

        return gain_sum, shift_sum, over(image, back, start)

    def backward_input(image):
        s.delta[image_rows(image), :] = convolve_back(
            s.spread_one, s.conv_one_here, slice(image, image + 1)
        )
        def put_input(image, step, grad, carry):
            total = grad + s.grad_middle[flat_at(image, step), :]
            s.leaving_grad[image, at(step), :] = total.astype(jnp.bfloat16)
            return carry

        gain_sum, shift_sum, _ = swish_norm_back(
            load_input, image, moments_one[image], gain_one, shift_one, put_input, 0
        )
        swap_grad[image].start()
        sums["gain_one"].append(gain_sum)
        sums["shift_one"].append(shift_sum)

    mix_rows = s.blocks_mix.shape[2] // 4

    def store_mix(which, product):
        product = product.astype(jnp.bfloat16)
        for rank in range(ranks):
            for core in range(2):
                block = rank * 2 + core
                spot = spots_mix[which // 2][rank]
                s.blocks_mix[spot, core, which * mix_rows : (which + 1) * mix_rows, :] = product[
                    block * mix_rows : (block + 1) * mix_rows
                ]

    def weigh_mix():
        upstream = s.upstream[...].reshape(flat_rows, channels)
        normed = s.normed[...]
        store_mix(3, by_rows(s.mixed[...], upstream))
        store_mix(0, by_rows(normed, s.grad_query[...]))
        store_mix(1, by_rows(normed, s.grad_key[...]))
        store_mix(2, by_rows(normed, s.grad_value[...]))

    def column_sums(load):
        def body(image, step, total):
            return total + fold(load(image, step))

        total = none
        for image in every_image:
            total = over(image, body, total)
        return whole(total)

    def fill_slot():
        slot_place = lax.broadcasted_iota(jnp.int32, (slot_rows, lanes), 0)
        slot = jnp.zeros((slot_rows, lanes), jnp.float32)
        for image in every_image:
            for index in range(per_image):
                row = sums["bias_one"][image][:, index * lanes : (index + 1) * lanes]
                slot = jnp.where(
                    slot_place == image * per_image + index,
                    jnp.broadcast_to(row, slot.shape),
                    slot,
                )
        device = place.rank * 2 + place.core
        s.slots[pl.ds(pl.multiple_of(device * slot_rows, slot_rows), slot_rows), :] = slot

    per_image = channels // lanes

    def flat(first, rows):
        count, width = rows.shape[0], rows.shape[1] // lanes
        for index in range(width):
            s.flat[pl.ds(first + index, count, stride=width), :] = rows[
                :, index * lanes : (index + 1) * lanes
            ]

    def embedding_gradients():
        def every(index):
            return s.slots[pl.ds(index, ranks * 2, stride=slot_rows), :]

        device = place.rank * 2 + place.core
        de = jnp.concatenate(
            [
                jnp.concatenate([every(image * per_image + j) for j in range(per_image)], axis=1)
                for image in every_image
            ],
            axis=0,
        )
        place_of = lax.broadcasted_iota(jnp.int32, (images_here * ranks * 2, lanes), 0)
        lane = lax.broadcasted_iota(jnp.int32, place_of.shape, 1)
        wanted = (place_of % (ranks * 2)) // 2 * images_here + place_of // (ranks * 2)
        tiles = [jnp.broadcast_to(s.levels_all[core, 0:1, :], place_of.shape) for core in (0, 1)]
        chosen = jnp.where(place_of % 2 == 0, tiles[0], tiles[1])
        levels = jnp.sum(jnp.where(lane == wanted, chosen, 0.0), axis=1, keepdims=True)
        levels = levels.astype(jnp.int32)
        entry = lax.broadcasted_iota(
            jnp.int32, (levels.shape[0], s.noise_table_here.shape[0]), 1
        )
        hit = jnp.where(entry == levels, 1.0, 0.0).astype(jnp.bfloat16)
        everywhere = matmul(hit, s.noise_table_here[...])
        exact = dict(preferred_element_type=jnp.float32, precision=lax.Precision.HIGHEST)
        own_rows = channels // (ranks * 2)
        s.product[...] = lax.dot_general(everywhere, de, (((0,), (0,)), ((), ())), **exact)
        first = pl.multiple_of(device * own_rows, own_rows)
        flat(spans["embed"], s.product[pl.ds(first, own_rows), :])
        grad_rows = lax.dot_general(
            de, s.embed_weight_here[...].astype(jnp.float32), (((1,), (1,)), ((), ())), **exact
        )
        halves = table_rows * 2 // (ranks * 2)
        wide = -(-halves // 128) * 128
        spot = lax.broadcasted_iota(jnp.int32, (levels.shape[0], wide), 1) + device * halves
        total = jnp.zeros((wide, half), jnp.float32)
        for side in range(2):
            pick = jnp.where(2 * levels + side == spot, 1.0, 0.0)
            total = total + lax.dot_general(
                pick,
                grad_rows[:, side * half : (side + 1) * half],
                (((0,), (0,)), ((), ())),
                **exact,
            )
        flat(spans["table"], total)

    def sum_biases():
        sums["query_bias"].append(column_sums(load_low(s.grad_query)))
        sums["value_bias"].append(column_sums(load_low(s.grad_value)))
        sums["out_bias"].append(column_sums(load_upstream))

    def start_small():
        rows = [functools.reduce(jnp.add, sums[name]) for name in SUMS]
        s.small_sum[0, 0:8, :] = stack_rows(rows[:8])
        s.small_sum[0, 8:16, :] = stack_rows(rows[8:])
        small[0].start()

    def step_all(reduction, stage):
        for part in range(reduction.parts):
            reduction.step(stage, part)

    for image in every_image:
        forward(image)
    for image in every_image[:-1]:
        backward(image)
        backward_rest(image)
        backward_input(image)
    for image in every_image:
        swap_output[image].start()
    backward(images_here - 1)
    backward_rest(images_here - 1)
    fill_slot()
    slots_pair.start()
    weigh_mix()
    reduce_mix.start(0, 0)
    reduce_mix.start(0, 1)
    backward_input(images_here - 1)
    step_all(reduce_mix, 0)
    slots_pair.arrive()
    slots_all.start()
    for image in every_image:
        share_act_two[image].arrive()
        share_grad_two[image].arrive()
    weigh(
        s.spread_two, half_two, s.act_two, s.act_two_far, s.grad_two_far, s.blocks_two, spots_two
    )
    for part in range(parts):
        reduce_two.start(0, part)
    for image in every_image:
        share_act_one[image].arrive()
        share_grad_one[image].arrive()
    weigh(
        s.spread_one, half_one, s.act_one, s.act_one_far, s.grad_one_far, s.blocks_one, spots_one
    )
    for part in range(parts):
        reduce_one.start(0, part)
    step_all(reduce_two, 0)
    sum_biases()
    start_small()
    step_all(reduce_one, 0)
    reduce_two.step(1, 0)
    reduce_two.step(1, 1)
    reduce_mix.step(1, 1)
    reduce_mix.step(1, 0)
    reduce_one.step(1, 1)
    reduce_one.step(1, 0)
    reduce_two.step(1, 2)
    reduce_two.step(2, 0)
    reduce_two.step(2, 1)
    small_step(0)
    levels_pair.arrive()
    slots_all.arrive()
    embedding_gradients()
    reduce_one.step(2, 1)
    reduce_one.step(2, 0)
    reduce_one.step(1, 2)
    reduce_two.step(3, 0)
    reduce_two.step(3, 1)
    end_two = share_copy(4 * images_here, s.fin_two.at[1 - half_two, chain], s.last_two, bit_two).start()
    small_step(1)
    reduce_mix.step(2, 1)
    reduce_mix.step(2, 0)
    reduce_one.step(3, 0)
    reduce_one.step(3, 1)
    end_one = share_copy(
        4 * images_here + 1, s.fin_one.at[1 - half_one, chain], s.last_one, bit_one
    ).start()
    small_step(2)
    reduce_mix.step(3, 1)
    reduce_mix.step(3, 0)
    small_step(3)
    reduce_mix.step(4, 1)
    reduce_mix.step(4, 0)
    for index, name in enumerate(dict(query=0, key=0, value=0, out=0)):
        flat(spans[name], s.share_mix[index * mix_rows : (index + 1) * mix_rows, :])
    flat(spans["conv_two"] + chain_rows * per_image, gather_straight(1, s.straight_two))
    flat(spans["conv_two"], settle(end_two, s.sum_two, s.last_two, half_two))
    flat(spans["conv_one"] + chain_rows * per_image, gather_straight(0, s.straight_one))
    flat(spans["conv_one"], settle(end_one, s.sum_one, s.last_one, half_one))
    small_step(4)
    s.sums[...] = s.small_sum[bits + 1]

    for flight in flights:
        flight.land()


def last_kernel(starts, rows, *refs):
    output_in, grad_in, flat_in, sums_in, output, grad = refs[:6]
    flats, sums = refs[6 : 6 + len(starts)], refs[6 + len(starts) : -4]
    output_here, grad_here, flat_here, sems = refs[-4:]
    arrive = [
        pltpu.make_async_copy(output_in, output_here, sems.at[0]),
        pltpu.make_async_copy(grad_in, grad_here, sems.at[1]),
        pltpu.make_async_copy(flat_in, flat_here, sems.at[2]),
    ]
    for move in arrive:
        move.start()
    for row, target in zip(rows, sums, strict=True):
        target[...] = sums_in[row : row + 1, :]
    leave = [
        pltpu.make_async_copy(output_here, output, sems.at[3]),
        pltpu.make_async_copy(grad_here, grad, sems.at[4]),
    ]
    for index, (start, target) in enumerate(zip(starts, flats, strict=True)):
        span = flat_here.at[pl.ds(start, target.shape[0]), :]
        leave.append(pltpu.make_async_copy(span, target, sems.at[5 + index]))
    for index, move in enumerate(arrive):
        move.wait()
        for out in leave[index : index + 1] if index < 2 else leave[2:]:
            out.start()
    for move in leave:
        move.wait()


def fused_device(given):
    ranks = lax.axis_size("wide")
    bits = (ranks - 1).bit_length()
    images = given["images"]
    images_rep, piece, channels = images.shape
    images_here, pixels = images_rep // ranks, piece * ranks
    flat_rows = images_here * pixels
    half = channels // 2
    devices = ranks * 2
    table_rows = given["noise_table"].shape[0]
    padded_rows = -(-table_rows // 128) * 128
    conv_rows = given["conv_one"].shape[0] // devices
    mix_rows = 4 * channels // devices
    low, full = jnp.bfloat16, jnp.float32
    parts = 3
    lanes = 128

    def struct(shape, kind):
        return jax.ShapeDtypeStruct(shape, kind)

    def hold(*shape, kind=low):
        return pltpu.VMEM(shape, kind)

    def semaphores(*shape):
        return pltpu.SemaphoreType.DMA(shape)

    def activations():
        return hold(flat_rows, channels)

    def fields():
        return hold(flat_rows, channels, kind=full)

    def square():
        return hold(channels, channels)

    def images_low():
        return hold(images_here, pixels, channels)

    def flat_span(size, pad=False):
        rows = size // lanes
        return -(-rows // 128) * 128 if pad else rows

    share = channels * channels // devices
    sizes = dict(
        conv_one=flat_span(conv_rows * channels),
        conv_two=flat_span(conv_rows * channels),
        query=flat_span(share),
        key=flat_span(share),
        value=flat_span(share),
        out=flat_span(share),
        embed=flat_span(share),
        table=flat_span(table_rows * channels // devices, True),
    )
    spans, start = {}, 0
    for name, size in sizes.items():
        spans[name] = start
        start = start + size

    outputs = dict(
        output=struct(images.shape, low),
        input_grad=struct(images.shape, low),
        flat=struct((start, lanes), full),
        sums=struct((16, channels), full),
    )
    padded = pixels + 2 * SIDE
    halvings = sum(ranks >> stage for stage in range(bits + 1))
    scratch = dict(
        noise_table_here=hold(padded_rows, channels),
        embed_weight_here=square(),
        conv_one_here=hold(*given["conv_one"].shape),
        conv_two_here=hold(*given["conv_two"].shape),
        query_weight_here=square(),
        key_weight_here=square(),
        value_weight_here=square(),
        out_weight_here=square(),
        arrived=images_low(),
        upstream=images_low(),
        leaving=images_low(),
        leaving_grad=images_low(),
        spread_act=hold(images_here, padded, 3 * channels),
        spread_two=hold(images_here, padded, 3 * channels),
        spread_one=hold(images_here, padded, 3 * channels),
        spread_far=hold(images_here, padded, 3 * half),
        hidden=fields(),
        middle=fields(),
        delta=fields(),
        grad_middle=fields(),
        probs=hold(flat_rows, pixels, kind=full),
        act_one=activations(),
        act_two=activations(),
        act_one_far=activations(),
        act_two_far=activations(),
        normed=activations(),
        query=activations(),
        key=activations(),
        value=activations(),
        mixed=activations(),
        grad_mixed=activations(),
        grad_query=activations(),
        grad_key=activations(),
        grad_value=activations(),
        grad_one=activations(),
        grad_two=activations(),
        grad_one_far=hold(flat_rows, half),
        grad_two_far=hold(flat_rows, half),
        blocks_one=hold(ranks, 2, conv_rows, half),
        blocks_two=hold(ranks, 2, conv_rows, half),
        blocks_mix=hold(ranks, 2, mix_rows, channels),
        land_one=hold(halvings - 1, conv_rows, half),
        land_two=hold(halvings - 1, conv_rows, half),
        land_mix=hold(halvings, mix_rows, channels),
        kept_one=hold(halvings - 3, conv_rows, half),
        kept_two=hold(halvings - 3, conv_rows, half),
        kept_mix=hold(halvings - 1, mix_rows, channels),
        sum_one=hold(2, conv_rows, half, kind=full),
        sum_two=hold(2, conv_rows, half, kind=full),
        fin_one=hold(2, conv_rows, half),
        fin_two=hold(2, conv_rows, half),
        last_one=hold(conv_rows // parts * (parts - 1), half),
        last_two=hold(conv_rows // parts * (parts - 1), half),
        straight_one=hold(ranks // 2, conv_rows // parts, half),
        straight_two=hold(ranks // 2, conv_rows // parts, half),
        straight_send=semaphores(2),
        straight_recv=semaphores(2),
        share_mix=hold(mix_rows, channels, kind=full),
        small_sum=hold(bits + 2, 16, channels, kind=full),
        small_land=hold(bits + 1, 16, channels, kind=full),
        slots=hold(devices * 8, lanes, kind=full),
        levels_all=hold(2, 8, lanes, kind=full),
        product=hold(channels, channels, kind=full),
        same_group=hold(half, half),
        load_sem=semaphores(8),
        swap_send=semaphores(4 * images_here),
        swap_recv=semaphores(4 * images_here),
        swap_own=semaphores(4 * images_here),
        share_send=semaphores(4 * images_here + 2),
        share_recv=semaphores(4 * images_here + 2),
        small_send=semaphores(bits + 1),
        small_recv=semaphores(bits + 1),
        slots_send=semaphores(3),
        slots_recv=semaphores(3),
        reduce_send_one=semaphores(bits, parts),
        reduce_recv_one=semaphores(bits, parts),
        reduce_send_two=semaphores(bits, parts),
        reduce_recv_two=semaphores(bits, parts),
        reduce_send_mix=semaphores(bits + 1, 2),
        reduce_recv_mix=semaphores(bits + 1, 2),
    )

    in_vmem = pl.BlockSpec(memory_space=pltpu.VMEM)
    anywhere = pl.BlockSpec(memory_space=pl.ANY)
    in_smem = pl.BlockSpec(memory_space=pltpu.SMEM)
    arrays, in_specs = {}, []
    for name, value in given.items():
        if value.ndim == 1 and value.dtype == full:
            value = value.reshape(1, channels)
            in_specs.append(in_vmem)
        else:
            in_specs.append(in_smem if value.ndim == 1 else anywhere)
        arrays[name] = value
    names = tuple(arrays) + tuple(outputs) + tuple(scratch)
    output, input_grad, flat, sums = pl.pallas_call(
        functools.partial(fused_kernel, names, spans, ranks, table_rows),
        out_shape=tuple(outputs.values()),
        in_specs=in_specs,
        out_specs=(anywhere, anywhere, in_vmem, in_vmem),
        scratch_shapes=list(scratch.values()),
        compiler_params=pltpu.CompilerParams(
            collective_id=0, has_side_effects=True, vmem_limit_bytes=63 << 20
        ),
        name="block",
    )(*arrays.values())

    order = dict(table=0, conv_one=0, conv_two=0, embed=0, query=0, key=0, value=0, out=0)
    sizes["table"] = table_rows * channels // devices // lanes
    finals = [struct((sizes[name], lanes), full) for name in order]
    rows = [SUMS.index(name) for name in GIVEN_BACK]
    results = pl.pallas_call(
        functools.partial(last_kernel, [spans[name] for name in order], rows),
        out_shape=(outputs["output"], outputs["input_grad"], *finals)
        + (struct((1, channels), full),) * len(rows),
        in_specs=[anywhere, anywhere, anywhere, in_vmem],
        out_specs=(anywhere,) * (2 + len(finals)) + (in_vmem,) * len(rows),
        scratch_shapes=[
            hold(*images.shape),
            hold(*images.shape),
            hold(start, lanes, kind=full),
            semaphores(5 + len(finals)),
        ],
        compiler_params=pltpu.CompilerParams(vmem_limit_bytes=63 << 20),
        name="finish",
    )(output, input_grad, flat, sums)
    return tuple(results[:2]) + tuple(member.reshape(-1) for member in results[2:])


def per_device(
    images,
    cotangent,
    levels,
    noise_table,
    gain_one,
    shift_one,
    conv_one,
    bias_one,
    embed_weight,
    embed_bias,
    gain_two,
    shift_two,
    conv_two,
    bias_two,
    gain_three,
    shift_three,
    query_weight,
    query_bias,
    key_weight,
    value_weight,
    value_bias,
    out_weight,
    out_bias,
):
    given = dict(
        images=images,
        cotangent=cotangent,
        levels=levels,
        noise_table=noise_table,
        gain_one=gain_one,
        shift_one=shift_one,
        conv_one=conv_one,
        bias_one=bias_one,
        embed_weight=embed_weight,
        embed_bias=embed_bias,
        gain_two=gain_two,
        shift_two=shift_two,
        conv_two=conv_two,
        bias_two=bias_two,
        gain_three=gain_three,
        shift_three=shift_three,
        query_weight=query_weight,
        query_bias=query_bias,
        key_weight=key_weight,
        value_weight=value_weight,
        value_bias=value_bias,
        out_weight=out_weight,
        out_bias=out_bias,
    )
    ranks, cores = lax.axis_size("wide"), lax.axis_size("rep")
    images_rep, piece, channels = images.shape
    devices = ranks * cores
    fits = (
        cores == 2
        and ranks >= 8
        and ranks & (ranks - 1) == 0
        and images_rep == 2 * ranks
        and piece % 16 == 0
        and conv_one.shape[0] % (devices * 48) == 0
        and channels % (devices * 16) == 0
        and noise_table.size % (devices * channels // 2) == 0
    )
    return fused_device(given) if fits else plain_device(*given.values())


def solution(mesh):
    in_specs = (
        P("rep", "wide", None),
        P("rep", "wide", None),
        P("rep"),
        P(),
        P(),
        P(),
        P(),
        P(),
        P(),
        P(),
        P(),
        P(),
        P(),
        P(),
        P(),
        P(),
        P(),
        P(),
        P(),
        P(),
        P(),
        P(),
        P(),
    )
    out_specs = (
        P("rep", "wide", None),
        P("rep", "wide", None),
        P(("wide", "rep")),
        P(("wide", "rep")),
        P(("wide", "rep")),
        P(("wide", "rep")),
        P(("wide", "rep")),
        P(("wide", "rep")),
        P(("wide", "rep")),
        P(("wide", "rep")),
        P(),
        P(),
        P(),
        P(),
        P(),
        P(),
        P(),
        P(),
        P(),
        P(),
        P(),
        P(),
    )
    return jax.shard_map(
        per_device, mesh=mesh, in_specs=in_specs, out_specs=out_specs, check_vma=False
    )
```

```python
import functools
import types

import jax
import jax.numpy as jnp
from jax import lax
from jax.experimental import pallas as pl
from jax.experimental.pallas import tpu as pltpu
from jax.sharding import PartitionSpec as P

GROUPS = 32
SIDE = 16
MESH = pl.DeviceIdType.MESH
CHUNK = 64


epsilon = 1e-05
highest = lax.Precision.HIGHEST


def swish(field):
    return field * jax.nn.sigmoid(field)


def group_norm(field, norm_gain, norm_shift):
    images_here = field.shape[0]
    channels = field.shape[2]
    grouped = field.reshape(images_here, field.shape[1], GROUPS, channels // GROUPS)
    center = jnp.mean(grouped, axis=(1, 3), keepdims=True)
    spread = grouped - center
    variance = jnp.mean(spread * spread, axis=(1, 3), keepdims=True)
    return (spread * lax.rsqrt(variance + epsilon)).reshape(field.shape) * norm_gain + norm_shift


def norm_swish(field, norm_gain, norm_shift):
    return swish(group_norm(field, norm_gain, norm_shift))


def matmul(left, right):
    return jnp.dot(left, right, preferred_element_type=jnp.float32)


def contract_rows(left, right):
    return lax.dot_general(
        left, right, (((0,), (0,)), ((), ())), preferred_element_type=jnp.float32
    )


def against(left, right):
    return lax.dot_general(
        left, right, (((1,), (1,)), ((), ())), preferred_element_type=jnp.float32
    )


def patches(activation):
    images_here = activation.shape[0]
    grid = activation.reshape(images_here, SIDE, SIDE, activation.shape[2])
    padded = jnp.pad(grid, ((0, 0), (1, 1), (1, 1), (0, 0)))
    pieces = [
        padded[
            :, kernel_tap // 3 : kernel_tap // 3 + SIDE, kernel_tap % 3 : kernel_tap % 3 + SIDE, :
        ]
        for kernel_tap in range(9)
    ]
    return jnp.concatenate(pieces, axis=-1).reshape(images_here * SIDE * SIDE, -1)


def unpatch(columns, images_here):
    channels = columns.shape[1] // 9
    grid = columns.reshape(images_here, SIDE, SIDE, 9, channels)
    summed = jnp.zeros((images_here, SIDE + 2, SIDE + 2, channels), jnp.float32)
    for kernel_tap in range(9):
        row_off = kernel_tap // 3
        col_off = kernel_tap % 3
        summed = summed + jnp.pad(
            grid[:, :, :, kernel_tap, :],
            ((0, 0), (row_off, 2 - row_off), (col_off, 2 - col_off), (0, 0)),
        )
    return summed[:, 1 : SIDE + 1, 1 : SIDE + 1, :].reshape(images_here, SIDE * SIDE, channels)


def plain_device(
    images,
    cotangent,
    levels,
    noise_table,
    gain_one,
    shift_one,
    conv_one,
    bias_one,
    embed_weight,
    embed_bias,
    gain_two,
    shift_two,
    conv_two,
    bias_two,
    gain_three,
    shift_three,
    query_weight,
    query_bias,
    key_weight,
    value_weight,
    value_bias,
    out_weight,
    out_bias,
):
    arrived, upstream = (
        lax.all_to_all(images, "wide", split_axis=0, concat_axis=1, tiled=True),
        lax.all_to_all(cotangent, "wide", split_axis=0, concat_axis=1, tiled=True),
    )
    images_here = arrived.shape[0]
    pixels = arrived.shape[1]
    channels = arrived.shape[2]
    flat_rows = images_here * pixels
    score_scale = channels ** (-0.5)
    table_rows = noise_table.shape[0]
    offset = lax.axis_index("wide") * images_here
    own_levels = lax.dynamic_slice_in_dim(levels, offset, images_here)
    selector = own_levels[:, None] == jnp.arange(table_rows, dtype=jnp.int32)[None, :]
    embedded = matmul(selector.astype(jnp.bfloat16), noise_table).astype(jnp.bfloat16)
    embed_shift = matmul(embedded, embed_weight) + embed_bias
    inputs = arrived.astype(jnp.float32)
    act_one, back_one = jax.vjp(norm_swish, inputs, gain_one, shift_one)
    cols_one = patches(act_one.astype(jnp.bfloat16))
    hidden_one = (matmul(cols_one, conv_one) + bias_one).reshape(images_here, pixels, channels)
    hidden_one = hidden_one + embed_shift[:, None, :]
    act_two, back_two = jax.vjp(norm_swish, hidden_one, gain_two, shift_two)
    cols_two = patches(act_two.astype(jnp.bfloat16))
    branch_out = matmul(cols_two, conv_two) + bias_two
    middle = inputs + branch_out.reshape(images_here, pixels, channels)
    normed, back_three = jax.vjp(group_norm, middle, gain_three, shift_three)
    normed_low = normed.astype(jnp.bfloat16).reshape(flat_rows, channels)
    query_block = (matmul(normed_low, query_weight) + query_bias).astype(jnp.bfloat16)
    key_block = matmul(normed_low, key_weight).astype(jnp.bfloat16)
    value_block = (matmul(normed_low, value_weight) + value_bias).astype(jnp.bfloat16)
    query_block = query_block.reshape(images_here, pixels, channels)
    key_block = key_block.reshape(images_here, pixels, channels)
    value_block = value_block.reshape(images_here, pixels, channels)
    scores = (
        jnp.einsum("npc,nqc->npq", query_block, key_block, preferred_element_type=jnp.float32)
        * score_scale
    )
    row_top = jnp.max(scores, axis=-1, keepdims=True)
    exponent = jnp.exp(scores - row_top)
    row_total = jnp.sum(exponent, axis=-1, keepdims=True)
    probs_low = (exponent / row_total).astype(jnp.bfloat16)
    log_total = row_top + jnp.log(row_total)
    mixed = jnp.einsum("npq,nqc->npc", probs_low, value_block, preferred_element_type=jnp.float32)
    mixed_low = mixed.astype(jnp.bfloat16).reshape(flat_rows, channels)
    result = middle.reshape(flat_rows, channels) + matmul(mixed_low, out_weight) + out_bias
    grad_out = upstream.reshape(flat_rows, channels)
    grad_out_bias = jnp.sum(grad_out.astype(jnp.float32), axis=0)
    grad_out_weight = contract_rows(mixed_low, grad_out)
    grad_mixed = (
        against(grad_out, out_weight).astype(jnp.bfloat16).reshape(images_here, pixels, channels)
    )
    scores_again = (
        jnp.einsum("npc,nqc->npq", query_block, key_block, preferred_element_type=jnp.float32)
        * score_scale
    )
    probs = jnp.exp(scores_again - log_total)
    probs_again = probs.astype(jnp.bfloat16)
    grad_probs = jnp.einsum(
        "npc,nqc->npq", grad_mixed, value_block, preferred_element_type=jnp.float32
    )
    grad_values = jnp.einsum(
        "npq,npc->nqc", probs_again, grad_mixed, preferred_element_type=jnp.float32
    ).astype(jnp.bfloat16)
    grad_scores = probs * (grad_probs - jnp.sum(grad_probs * probs, axis=-1, keepdims=True))
    grad_scores = grad_scores.astype(jnp.bfloat16)
    grad_query = (
        (
            jnp.einsum("npq,nqc->npc", grad_scores, key_block, preferred_element_type=jnp.float32)
            * score_scale
        )
        .astype(jnp.bfloat16)
        .reshape(flat_rows, channels)
    )
    grad_keys = (
        (
            jnp.einsum("npq,npc->nqc", grad_scores, query_block, preferred_element_type=jnp.float32)
            * score_scale
        )
        .astype(jnp.bfloat16)
        .reshape(flat_rows, channels)
    )
    grad_values = grad_values.reshape(flat_rows, channels)
    grad_query_weight = contract_rows(normed_low, grad_query)
    grad_key_weight = contract_rows(normed_low, grad_keys)
    grad_value_weight = contract_rows(normed_low, grad_values)
    grad_query_bias = jnp.sum(grad_query.astype(jnp.float32), axis=0)
    grad_value_bias = jnp.sum(grad_values.astype(jnp.float32), axis=0)
    grad_normed = against(grad_query, query_weight) + against(grad_keys, key_weight)
    grad_normed = grad_normed + against(grad_values, value_weight)
    grad_middle, grad_gain_three, grad_shift_three = back_three(
        grad_normed.reshape(images_here, pixels, channels)
    )
    grad_middle = grad_middle + upstream.astype(jnp.float32)
    grad_branch = grad_middle.astype(jnp.bfloat16).reshape(flat_rows, channels)
    grad_bias_two = jnp.sum(grad_branch.astype(jnp.float32), axis=0)
    grad_conv_two = contract_rows(cols_two, grad_branch)
    grad_act_two = unpatch(against(grad_branch, conv_two), images_here)
    grad_hidden, grad_gain_two, grad_shift_two = back_two(grad_act_two)
    grad_hidden_low = grad_hidden.astype(jnp.bfloat16)
    hidden_rows = grad_hidden_low.reshape(flat_rows, channels)
    grad_bias_one = jnp.sum(hidden_rows.astype(jnp.float32), axis=0)
    grad_conv_one = contract_rows(cols_one, hidden_rows)
    grad_shift = jnp.sum(grad_hidden_low.astype(jnp.float32), axis=1)
    grad_embed_bias = jnp.sum(grad_shift, axis=0)
    grad_embed_weight = jnp.dot(embedded.astype(jnp.float32).T, grad_shift, precision=highest)
    embed_float = embed_weight.astype(jnp.float32)
    grad_act_one = unpatch(against(hidden_rows, conv_one), images_here)
    grad_input_part, grad_gain_one, grad_shift_one = back_one(grad_act_one)
    grad_input = grad_middle + grad_input_part
    output_back, input_back = (
        lax.all_to_all(
            result.reshape(images_here, pixels, channels).astype(jnp.bfloat16),
            "wide",
            split_axis=1,
            concat_axis=0,
            tiled=True,
        ),
        lax.all_to_all(
            grad_input.astype(jnp.bfloat16), "wide", split_axis=1, concat_axis=0, tiled=True
        ),
    )
    wide_count = lax.axis_size("wide")
    rep_count = lax.axis_size("rep")
    device_count = wide_count * rep_count
    weight_grads = (
        grad_conv_one,
        grad_conv_two,
        grad_embed_weight,
        grad_query_weight,
        grad_key_weight,
        grad_value_weight,
        grad_out_weight,
    )
    grad_embedded = jnp.dot(grad_shift, embed_float.T, precision=highest)
    grad_table = jnp.dot(selector.astype(jnp.float32).T, grad_embedded, precision=highest)
    members = (grad_table,) + weight_grads
    widths = [member.size // device_count for member in members]
    packed = jnp.concatenate([member.reshape(device_count, -1) for member in members], axis=1)
    packed = lax.psum_scatter(packed, ("wide", "rep"), scatter_dimension=0, tiled=True)
    packed = packed.reshape(-1)
    large_grads = []
    start_at = 0
    for width in widths:
        large_grads.append(packed[start_at : start_at + width])
        start_at = start_at + width
    large_grads = tuple(large_grads)
    small_grads = lax.psum(
        (
            grad_gain_one,
            grad_shift_one,
            grad_bias_one,
            grad_embed_bias,
            grad_gain_two,
            grad_shift_two,
            grad_bias_two,
            grad_gain_three,
            grad_shift_three,
            grad_query_bias,
            grad_value_bias,
            grad_out_bias,
        ),
        ("wide", "rep"),
    )
    return (output_back, input_back) + large_grads + tuple(small_grads)


def by_rows(left, right):
    return lax.dot_general(
        left, right, (((0,), (0,)), ((), ())), preferred_element_type=jnp.float32
    )


def group_sum(rows, same_group):
    width = same_group.shape[0]
    first = rows.astype(jnp.bfloat16).astype(jnp.float32)
    rest = rows - first
    second = rest.astype(jnp.bfloat16).astype(jnp.float32)
    terms = (first, second, rest - second)
    spans = [slice(start, start + width) for start in range(0, rows.shape[1], width)]
    stacked = jnp.concatenate([term[:, span] for span in spans for term in terms], axis=0)
    summed = matmul(stacked.astype(jnp.bfloat16), same_group)
    parts = [summed[24 * k : 24 * k + 24] for k in range(len(spans))]
    return jnp.concatenate([part[0:8] + part[8:16] + part[16:24] for part in parts], axis=1)


def stack_rows(members):
    shape = (8, members[0].shape[1])
    place = lax.broadcasted_iota(jnp.int32, shape, 0)
    stacked = jnp.zeros(shape, jnp.float32)
    for index, member in enumerate(members):
        stacked = jnp.where(place == index, jnp.broadcast_to(member, shape), stacked)
    return stacked


def sigmoid(field):
    return 0.5 + 0.5 * jnp.tanh(0.5 * field)


SUMS = tuple(
    dict(
        gain_one=0,
        shift_one=0,
        bias_one=0,
        gain_two=0,
        shift_two=0,
        bias_two=0,
        gain_three=0,
        shift_three=0,
        query_bias=0,
        value_bias=0,
        out_bias=0,
    )
)
GIVEN_BACK = SUMS[:3] + SUMS[2:]


class Flight:
    def __init__(self, flights, make, offsets=None, whole=None, own=None):
        self.flights, self.make, self.offsets, self.own = flights, make, offsets, own
        self.whole = make if whole is None else whole
        self.arrived = self.left = False

    def start(self):
        if self.offsets is None:
            self.make().start()
        else:

            def go(offset, carry):
                self.make(offset).start()
                return carry

            lax.fori_loop(*self.offsets, go, 0)
        if self.own is not None:
            self.own().start()
        self.flights.append(self)
        return self

    def arrive(self):
        self.whole().wait_recv()
        if self.own is not None:
            self.own().wait()
        self.arrived = True

    def leave(self):
        self.whole().wait_send()
        self.left = True

    def land(self):
        if not self.arrived:
            self.arrive()
        if not self.left:
            self.leave()


class Reduce:
    def __init__(self, flights, place, blocks, orders, landing, kept, send, recv, last, spread):
        self.flights, self.place = flights, place
        self.blocks, self.orders, self.last = blocks, orders, last
        self.landing, self.kept, self.send, self.recv = landing, kept, send, recv
        self.spread, self.stages = spread, max(len(order) for order in orders)
        self.rows = blocks.shape[2]
        self.parts = send.shape[1]
        self.under_way = {}

    def cut(self, part):
        size = self.rows // self.parts
        return pl.ds(part * size, size)

    def copy(self, stage, part):
        place, rows = self.place, self.cut(part)
        if stage == 0:
            source = self.blocks.at[:, 1 - place.core, rows, :]
            target = place.other_core
        else:
            count = self.blocks.shape[0] >> stage
            bit = self.orders[part][stage - 1]
            source = self.kept[stage - 1].at[
                pl.ds((1 - place.bit(bit)) * count, count), rows, :
            ]
            target = place.across(bit)
        return pltpu.make_async_remote_copy(
            src_ref=source,
            dst_ref=self.landing[stage].at[:, rows, :],
            send_sem=self.send.at[stage, part],
            recv_sem=self.recv.at[stage, part],
            device_id=target,
            device_id_type=MESH,
        )

    def start(self, stage, part):
        copy = functools.partial(self.copy, stage, part)
        self.under_way[stage, part] = Flight(self.flights, copy).start()

    def step(self, stage, part):
        self.finish(stage, part)
        if stage < len(self.orders[part]):
            self.start(stage + 1, part)
        elif stage < self.stages:
            self.spread(self.kept[stage], self.cut(part))

    def finish(self, stage, part):
        place, rows = self.place, self.cut(part)
        self.under_way[stage, part].arrive()
        count = self.blocks.shape[0] >> stage
        if stage == 0:
            own = self.blocks[:, place.core, rows, :]
        else:
            first = place.bit(self.orders[part][stage - 1]) * count
            own = self.kept[stage - 1][pl.ds(first, count), rows, :]
        landed = self.landing[stage][:, rows, :]
        if stage < self.stages:
            self.kept[stage][:, rows, :] = own + landed
        else:
            self.last(rows, own.astype(jnp.float32) + landed.astype(jnp.float32))


class Place:
    def __init__(self, ranks):
        self.ranks = ranks
        self.rank = lax.axis_index("wide")
        self.core = lax.axis_index("rep")
        self.other_core = (self.rank, 1 - self.core)

    def bit(self, index):
        return (self.rank // (1 << index)) % 2

    def across(self, index):
        step = 1 << index
        return (self.rank + step - 2 * step * self.bit(index), self.core)


def block_order(ranks, order):
    places = []
    for rank in range(ranks):
        spot = 0
        for bit in order:
            spot = spot * 2 + (rank >> bit) % 2
        places.append(spot)
    return places


def fused_kernel(names, spans, ranks, table_rows, *refs):
    s = types.SimpleNamespace(**dict(zip(names, refs, strict=True)))
    place = Place(ranks)
    bits = (ranks - 1).bit_length()
    far = list(range(2, bits))
    images_here, pixels, channels = s.arrived.shape
    every_image = range(images_here)
    flat_rows = images_here * pixels
    piece = pixels // ranks
    half = channels // 2
    steps = pixels // CHUNK
    score_scale = channels ** (-0.5)
    count_inverse = 1.0 / (pixels * (channels // GROUPS))
    col = lax.broadcasted_iota(jnp.int32, (CHUNK, 1), 0) % SIDE
    flights = []

    def image_rows(image):
        return slice(image * pixels, (image + 1) * pixels)

    barrier = pltpu.get_barrier_semaphore()

    def greet(offset, carry):
        pl.semaphore_signal(
            barrier,
            inc=1,
            device_id=((place.rank + offset) % ranks, place.core),
            device_id_type=MESH,
        )
        return carry

    lax.fori_loop(1, ranks, greet, 0)
    pl.semaphore_signal(barrier, inc=1, device_id=place.other_core, device_id_type=MESH)

    pairs = (
        (s.noise_table, s.noise_table_here.at[pl.ds(0, table_rows), :]),
        (s.embed_weight, s.embed_weight_here),
        (s.conv_one, s.conv_one_here),
        (s.conv_two, s.conv_two_here),
        (s.query_weight, s.query_weight_here),
        (s.key_weight, s.key_weight_here),
        (s.value_weight, s.value_weight_here),
        (s.out_weight, s.out_weight_here),
    )
    loads = []
    for index, (source, target) in enumerate(pairs):
        loads.append(pltpu.make_async_copy(source, target, s.load_sem.at[index]))
        loads[-1].start()
    pl.semaphore_wait(barrier, ranks)

    def gather_copy(slot, source, target, image, offset):
        peer = (place.rank + offset) % ranks
        return pltpu.make_async_remote_copy(
            src_ref=source.at[peer * images_here + image],
            dst_ref=target.at[image, pl.ds(pl.multiple_of(place.rank * piece, 16), piece)],
            send_sem=s.swap_send.at[slot],
            recv_sem=s.swap_recv.at[slot],
            device_id=(peer, place.core),
            device_id_type=MESH,
        )

    def gather_own(slot, source, target, image):
        return pltpu.make_async_copy(
            source.at[place.rank * images_here + image],
            target.at[image, pl.ds(pl.multiple_of(place.rank * piece, 16), piece)],
            s.swap_own.at[slot],
        )

    def scatter_copy(slot, source, target, image, offset):
        peer = (place.rank + offset) % ranks
        return pltpu.make_async_remote_copy(
            src_ref=source.at[image, pl.ds(pl.multiple_of(peer * piece, 16), piece)],
            dst_ref=target.at[place.rank * images_here + image],
            send_sem=s.swap_send.at[slot],
            recv_sem=s.swap_recv.at[slot],
            device_id=(peer, place.core),
            device_id_type=MESH,
        )

    def scatter_own(slot, source, target, image):
        return pltpu.make_async_copy(
            source.at[image, pl.ds(pl.multiple_of(place.rank * piece, 16), piece)],
            target.at[place.rank * images_here + image],
            s.swap_own.at[slot],
        )

    def swap_whole(slot, held, image):
        others = held.at[image, pl.ds(0, pixels - piece)]
        return pltpu.make_async_remote_copy(
            src_ref=others,
            dst_ref=others,
            send_sem=s.swap_send.at[slot],
            recv_sem=s.swap_recv.at[slot],
            device_id=place.across(0),
            device_id_type=MESH,
        )

    def swaps(copy, own, which, source, target, held):
        return [
            Flight(
                flights,
                functools.partial(copy, which * images_here + image, source, target, image),
                (1, ranks),
                functools.partial(swap_whole, which * images_here + image, held, image),
                functools.partial(own, which * images_here + image, source, target, image),
            )
            for image in every_image
        ]

    swap_images = swaps(gather_copy, gather_own, 0, s.images, s.arrived, s.arrived)
    swap_upstream = swaps(gather_copy, gather_own, 1, s.cotangent, s.upstream, s.upstream)
    swap_output = swaps(scatter_copy, scatter_own, 2, s.leaving, s.output, s.leaving)
    swap_grad = swaps(scatter_copy, scatter_own, 3, s.leaving_grad, s.input_grad, s.leaving_grad)
    for image in every_image:
        swap_images[image].start()
    for image in every_image:
        swap_upstream[image].start()

    for padded in (s.spread_act, s.spread_two, s.spread_one, s.spread_far):
        for image in every_image:
            edge = jnp.zeros((SIDE, padded.shape[2]), jnp.bfloat16)
            padded[image, 0:SIDE, :] = edge
            padded[image, pixels + SIDE : pixels + 2 * SIDE, :] = edge
    tail = s.noise_table_here.shape[0] - table_rows
    if tail:
        s.noise_table_here[table_rows:, :] = jnp.zeros((tail, channels), jnp.bfloat16)
    own_levels = [s.levels[place.rank * images_here + image] for image in every_image]
    lane = lax.broadcasted_iota(jnp.int32, s.levels_all.shape[1:], 1)
    tile = jnp.zeros(lane.shape, jnp.float32)
    for index in range(ranks * images_here):
        tile = jnp.where(lane == index, s.levels[index].astype(jnp.float32), tile)
    s.levels_all[place.core] = tile

    def levels_copy():
        return pltpu.make_async_remote_copy(
            src_ref=s.levels_all.at[place.core],
            dst_ref=s.levels_all.at[place.core],
            send_sem=s.slots_send.at[2],
            recv_sem=s.slots_recv.at[2],
            device_id=place.other_core,
            device_id_type=MESH,
        )

    levels_pair = Flight(flights, levels_copy).start()
    entry = lax.broadcasted_iota(jnp.int32, (8, s.noise_table_here.shape[0]), 1)
    line = lax.broadcasted_iota(jnp.int32, entry.shape, 0)
    selected = jnp.zeros(entry.shape, jnp.float32)
    for image in every_image:
        hit = jnp.where(entry == own_levels[image], 1.0, 0.0)
        selected = jnp.where(line == image, hit, selected)
    loads[0].wait()
    loads[1].wait()
    embedded = matmul(selected.astype(jnp.bfloat16), s.noise_table_here[...])
    embed_shift = matmul(embedded.astype(jnp.bfloat16), s.embed_weight_here[...])
    embed_shift = embed_shift + s.embed_bias[...] + s.bias_one[...]

    def over(image, body, start):
        return lax.fori_loop(0, steps, functools.partial(body, image), start)

    def at(step):
        return pl.ds(pl.multiple_of(step * CHUNK, CHUNK), CHUNK)

    def flat_at(image, step):
        return pl.ds(pl.multiple_of(image * pixels + step * CHUNK, CHUNK), CHUNK)

    def fold(chunk):
        return jnp.sum(chunk.reshape(CHUNK // 8, 8, channels), axis=0)

    none = jnp.zeros((8, channels), jnp.float32)

    def whole(part):
        return jnp.sum(part, axis=0, keepdims=True)

    group_width = s.same_group.shape[0]
    same_group = [
        lax.broadcasted_iota(jnp.int32, (group_width, group_width), axis)
        // (channels // GROUPS)
        for axis in range(2)
    ]
    s.same_group[...] = jnp.where(same_group[0] == same_group[1], 1.0, 0.0).astype(jnp.bfloat16)

    def group_total(row):
        rows = jnp.broadcast_to(row, (8, channels))
        return group_sum(rows, s.same_group[...])[0:1] * count_inverse

    def statistics(load, image):
        def first(image, step, total):
            return total + fold(load(image, step))

        center = group_total(whole(over(image, first, none)))

        def second(image, step, total):
            spread = load(image, step) - center
            return total + fold(spread * spread)

        variance = group_total(whole(over(image, second, none)))
        return center, lax.rsqrt(variance + epsilon)

    def spread_out(target, image, step, chunk, before, after):
        width = chunk.shape[1]
        rows = pl.ds(pl.multiple_of(step * CHUNK + SIDE, SIDE), CHUNK)
        target[image, rows, before * width : (before + 1) * width] = jnp.where(
            col > 0, pltpu.roll(chunk, 1, 0), 0.0
        ).astype(jnp.bfloat16)
        target[image, rows, width : 2 * width] = chunk.astype(jnp.bfloat16)
        target[image, rows, after * width : (after + 1) * width] = jnp.where(
            col < SIDE - 1, pltpu.roll(chunk, CHUNK - 1, 0), 0.0
        ).astype(jnp.bfloat16)

    def activate(load, image, moments, gain, shift, keep):
        center, rate = moments
        slope = rate * gain

        def apply(image, step, carry):
            field = (load(image, step) - center) * slope + shift
            act = field * sigmoid(field)
            spread_out(s.spread_act, image, step, act, 0, 2)
            keep[flat_at(image, step), :] = act.astype(jnp.bfloat16)
            return carry

        over(image, apply, 0)

    def convolve(weight, image):
        total = None
        for row_tap in range(3):
            term = matmul(
                s.spread_act[image, SIDE * row_tap : SIDE * row_tap + pixels, :],
                weight[3 * channels * row_tap : 3 * channels * (row_tap + 1), :],
            )
            total = term if total is None else total + term
        return total

    def tap_rows(row_tap):
        return slice(SIDE * (2 - row_tap), SIDE * (2 - row_tap) + pixels)

    def convolve_back(source, weight, images):
        total = None
        for tap in range(9):
            window = source[
                images, tap_rows(tap // 3), (tap % 3) * channels : (tap % 3 + 1) * channels
            ]
            term = against(
                window.reshape(-1, channels), weight[channels * tap : channels * (tap + 1), :]
            )
            total = term if total is None else total + term
        return total

    def share_copy(slot, source, target, bit):
        def make():
            return pltpu.make_async_remote_copy(
                src_ref=source,
                dst_ref=target,
                send_sem=s.share_send.at[slot],
                recv_sem=s.share_recv.at[slot],
                device_id=place.across(bit),
                device_id_type=MESH,
            )

        return Flight(flights, make)

    bit_one, bit_two = 1, 0
    half_one, half_two = place.bit(bit_one), place.bit(bit_two)

    def shares(which, source, target, bit, mine=None):
        made = []
        for image in every_image:
            rows = pl.ds(image * pixels, pixels)
            lanes_sent = pl.ds(0, channels)
            if mine is not None:
                lanes_sent = pl.ds(pl.multiple_of((1 - mine) * half, half), half)
            made.append(
                share_copy(
                    which * images_here + image,
                    source.at[rows, lanes_sent],
                    target.at[rows, :],
                    bit,
                )
            )
        return made

    share_act_one = shares(0, s.act_one, s.act_one_far, bit_one)
    share_act_two = shares(1, s.act_two, s.act_two_far, bit_two)
    share_grad_two = shares(2, s.grad_two, s.grad_two_far, bit_two, half_two)
    share_grad_one = shares(3, s.grad_one, s.grad_one_far, bit_one, half_one)

    def weigh(spread, mine, act, act_far, grad_far, blocks, spots):
        def unfold(image, step, carry):
            chunk = grad_far[flat_at(image, step), :].astype(jnp.float32)
            spread_out(s.spread_far, image, step, chunk, 2, 0)
            return carry

        for image in every_image:
            over(image, unfold, 0)
        rows_block = blocks.shape[2]
        rows_part = rows_block // len(spots)
        for tap in range(9):
            rows, side_tap = tap_rows(tap // 3), tap % 3
            near = spread[
                :, rows, pl.ds(pl.multiple_of(side_tap * channels + mine * half, half), half)
            ]
            beyond = s.spread_far[:, rows, side_tap * half : (side_tap + 1) * half]
            product = by_rows(act[...], near.reshape(flat_rows, half)) + by_rows(
                act_far[...], beyond.reshape(flat_rows, half)
            )
            product = product.astype(jnp.bfloat16)
            done = 0
            while done < channels:
                block, inside = divmod(tap * channels + done, rows_block)
                part = inside // rows_part
                size = min(rows_part * (part + 1) - inside, channels - done)
                blocks[spots[part][block // 2], block % 2, inside : inside + size, :] = product[
                    done : done + size
                ]
                done = done + size

    orders_one = [[1 - bit_one] + far] * 2 + [[1 - bit_one]]
    orders_two = [[1 - bit_two] + far] * 2 + [[1 - bit_two]]
    orders_mix = [[0, 1] + far, [1, 0] + far]
    tails_one, tails_two = ([bit_one],) * 2 + (far + [bit_one],), ([bit_two],) * 2 + (far + [bit_two],)
    spots_one = [
        block_order(ranks, order + end) for order, end in zip(orders_one, tails_one, strict=True)
    ]
    spots_two = [
        block_order(ranks, order + end) for order, end in zip(orders_two, tails_two, strict=True)
    ]
    spots_mix = [block_order(ranks, order) for order in orders_mix]

    def put_one(rows, total):
        s.sum_one[:, rows, :] = total
        s.fin_one[:, rows, :] = total.astype(jnp.bfloat16)

    def put_two(rows, total):
        s.sum_two[:, rows, :] = total
        s.fin_two[:, rows, :] = total.astype(jnp.bfloat16)

    def put_mix(rows, total):
        s.share_mix[rows, :] = total[0]

    owners = ranks // 2

    def straight(slot, bit, land):
        order = far + [bit]
        weights = [1 << (len(order) - 1 - k) for k in range(len(order))]
        own = sum(place.bit(b) * weight for b, weight in zip(order, weights, strict=True))
        other = 1 - bit

        def send(kept, rows):
            land[own] = kept[own, rows, :]

            def make(offset):
                target = (own + offset) % owners
                rank = place.bit(other) * (1 << other)
                for b, weight in zip(order, weights, strict=True):
                    rank = rank + (target // weight) % 2 * (1 << b)
                return pltpu.make_async_remote_copy(
                    src_ref=kept.at[target, rows, :],
                    dst_ref=land.at[own],
                    send_sem=s.straight_send.at[slot],
                    recv_sem=s.straight_recv.at[slot],
                    device_id=(rank, place.core),
                    device_id_type=MESH,
                )

            def everything():
                others = land.at[pl.ds(0, owners - 1)]
                return pltpu.make_async_remote_copy(
                    src_ref=others,
                    dst_ref=others,
                    send_sem=s.straight_send.at[slot],
                    recv_sem=s.straight_recv.at[slot],
                    device_id=place.across(0),
                    device_id_type=MESH,
                )

            flight_to[slot] = Flight(flights, make, (1, owners), everything).start()

        return send

    flight_to = {}

    def gather_straight(slot, land):
        flight_to[slot].arrive()
        sides = []
        for side in (0, 1):
            total = land[side].astype(jnp.float32)
            for index in range(side + 2, owners, 2):
                total = total + land[index].astype(jnp.float32)
            sides.append(total)
        return jnp.concatenate(sides, axis=1)

    def staged(ref, first, stages):
        views, start = [], 0
        for stage in range(stages):
            views.append(ref.at[pl.ds(start, first >> stage)])
            start = start + (first >> stage)
        return views

    def reduction(blocks, order, landing, kept, send, recv, put, spread=None):
        stages = len(order[0])
        return Reduce(
            flights,
            place,
            blocks,
            order,
            staged(landing, ranks, stages + 1),
            staged(kept, ranks, stages),
            send,
            recv,
            put,
            spread,
        )

    reduce_one = reduction(
        s.blocks_one,
        orders_one,
        s.land_one,
        s.kept_one,
        s.reduce_send_one,
        s.reduce_recv_one,
        put_one,
        straight(0, bit_one, s.straight_one),
    )
    reduce_two = reduction(
        s.blocks_two,
        orders_two,
        s.land_two,
        s.kept_two,
        s.reduce_send_two,
        s.reduce_recv_two,
        put_two,
        straight(1, bit_two, s.straight_two),
    )
    reduce_mix = reduction(
        s.blocks_mix,
        orders_mix,
        s.land_mix,
        s.kept_mix,
        s.reduce_send_mix,
        s.reduce_recv_mix,
        put_mix,
    )
    parts = reduce_one.parts
    chain_rows = s.last_one.shape[0]
    chain = pl.ds(0, chain_rows)

    def settle(flight, sums, target, mine):
        flight.arrive()
        own = sums[mine, 0:chain_rows, :]
        other = target[...].astype(jnp.float32)
        left = jnp.where(mine == 0, own, other)
        right = jnp.where(mine == 0, other, own)
        return jnp.concatenate([left, right], axis=1)

    def small_copy(stage):
        return pltpu.make_async_remote_copy(
            src_ref=s.small_sum.at[stage],
            dst_ref=s.small_land.at[stage],
            send_sem=s.small_send.at[stage],
            recv_sem=s.small_recv.at[stage],
            device_id=place.other_core if stage == 0 else place.across(stage - 1),
            device_id_type=MESH,
        )

    small = [Flight(flights, functools.partial(small_copy, k)) for k in range(bits + 1)]

    def small_step(stage):
        small[stage].arrive()
        s.small_sum[stage + 1] = s.small_sum[stage] + s.small_land[stage]
        if stage < bits:
            small[stage + 1].start()

    slot_rows = 8
    lanes = s.slots.shape[1]

    def pair_window():
        return s.slots.at[pl.ds(pl.multiple_of(place.rank * 2 * slot_rows, 16), 2 * slot_rows), :]

    def slot_copy():
        first = pl.multiple_of((place.rank * 2 + place.core) * slot_rows, slot_rows)
        window = s.slots.at[pl.ds(first, slot_rows), :]
        return pltpu.make_async_remote_copy(
            src_ref=window,
            dst_ref=window,
            send_sem=s.slots_send.at[0],
            recv_sem=s.slots_recv.at[0],
            device_id=place.other_core,
            device_id_type=MESH,
        )

    def pair_copy(offset):
        return pltpu.make_async_remote_copy(
            src_ref=pair_window(),
            dst_ref=pair_window(),
            send_sem=s.slots_send.at[1],
            recv_sem=s.slots_recv.at[1],
            device_id=((place.rank + offset) % ranks, place.core),
            device_id_type=MESH,
        )

    slots_pair = Flight(flights, slot_copy)
    def pairs_whole():
        others = s.slots.at[pl.ds(0, (ranks - 1) * 2 * slot_rows), :]
        return pltpu.make_async_remote_copy(
            src_ref=others,
            dst_ref=others,
            send_sem=s.slots_send.at[1],
            recv_sem=s.slots_recv.at[1],
            device_id=place.across(0),
            device_id_type=MESH,
        )

    slots_all = Flight(flights, pair_copy, (1, ranks), pairs_whole)

    def load_input(image, step):
        return s.arrived[image, at(step), :].astype(jnp.float32)

    def load_hidden(image, step):
        return s.hidden[flat_at(image, step), :]

    def load_middle(image, step):
        return s.middle[flat_at(image, step), :]

    def load_upstream(image, step):
        return s.upstream[image, at(step), :].astype(jnp.float32)

    def delta_at(image, step):
        return s.delta[flat_at(image, step), :]

    def load_low(ref):
        return lambda image, step: ref[flat_at(image, step), :].astype(jnp.float32)

    gain_one, shift_one = s.gain_one[...], s.shift_one[...]
    gain_two, shift_two = s.gain_two[...], s.shift_two[...]
    gain_three, shift_three = s.gain_three[...], s.shift_three[...]
    moments_one, moments_two, moments_three = [], [], []
    sums = {name: [] for name in SUMS}

    def forward(image):
        rows = image_rows(image)
        swap_images[image].arrive()
        moments_one.append(statistics(load_input, image))
        activate(load_input, image, moments_one[image], gain_one, shift_one, s.act_one)
        share_act_one[image].start()
        if image == 0:
            loads[2].wait()
        s.hidden[rows, :] = convolve(s.conv_one_here, image) + embed_shift[image : image + 1]
        moments_two.append(statistics(load_hidden, image))
        activate(load_hidden, image, moments_two[image], gain_two, shift_two, s.act_two)
        share_act_two[image].start()
        if image == 0:
            loads[3].wait()
        s.middle[rows, :] = (
            convolve(s.conv_two_here, image)
            + s.bias_two[...]
            + s.arrived[image].astype(jnp.float32)
        )
        moments_three.append(statistics(load_middle, image))
        center, rate = moments_three[image]
        slope = rate * gain_three

        def normalize(image, step, carry):
            field = (load_middle(image, step) - center) * slope + shift_three
            s.normed[flat_at(image, step), :] = field.astype(jnp.bfloat16)
            return carry

        over(image, normalize, 0)
        if image == 0:
            for load in loads[4:]:
                load.wait()
        normed = s.normed[rows, :]
        query = (matmul(normed, s.query_weight_here[...]) + s.query_bias[...]).astype(jnp.bfloat16)
        key = matmul(normed, s.key_weight_here[...]).astype(jnp.bfloat16)
        value = (matmul(normed, s.value_weight_here[...]) + s.value_bias[...]).astype(jnp.bfloat16)
        s.query[rows, :] = query
        s.key[rows, :] = key
        s.value[rows, :] = value
        scores = against(query, key) * score_scale
        exponent = jnp.exp(scores - jnp.max(scores, axis=1, keepdims=True))
        probs = exponent / jnp.sum(exponent, axis=1, keepdims=True)
        s.probs[rows, :] = probs
        mixed = matmul(probs.astype(jnp.bfloat16), value).astype(jnp.bfloat16)
        s.mixed[rows, :] = mixed
        result = s.middle[rows, :] + matmul(mixed, s.out_weight_here[...]) + s.out_bias[...]
        s.leaving[image] = result.astype(jnp.bfloat16)

    def norm_back_terms(gain, shift_sum, gain_sum):
        rows = stack_rows([gain * shift_sum, gain * gain_sum])
        means = group_sum(rows, s.same_group[...]) * count_inverse
        return means[0:1], means[1:2]

    def backward(image):
        rows = image_rows(image)
        swap_upstream[image].arrive()
        probs = s.probs[rows, :]
        query, key, value = s.query[rows, :], s.key[rows, :], s.value[rows, :]
        grad_mixed = against(s.upstream[image], s.out_weight_here[...]).astype(jnp.bfloat16)
        grad_probs = against(grad_mixed, value)
        grad_value = by_rows(probs.astype(jnp.bfloat16), grad_mixed).astype(jnp.bfloat16)
        inner = jnp.sum(grad_probs * probs, axis=1, keepdims=True)
        grad_scores = (probs * (grad_probs - inner)).astype(jnp.bfloat16)
        grad_query = (matmul(grad_scores, key) * score_scale).astype(jnp.bfloat16)
        grad_key = (by_rows(grad_scores, query) * score_scale).astype(jnp.bfloat16)
        s.grad_value[rows, :] = grad_value
        s.grad_query[rows, :] = grad_query
        s.grad_key[rows, :] = grad_key
        s.delta[rows, :] = (
            against(grad_query, s.query_weight_here[...])
            + against(grad_key, s.key_weight_here[...])
            + against(grad_value, s.value_weight_here[...])
        )

    def backward_rest(image, between=None):
        rows = image_rows(image)
        center, rate = moments_three[image]

        def sums_three(image, step, totals):
            grad = delta_at(image, step)
            unit = (load_middle(image, step) - center) * rate
            return totals[0] + fold(grad), totals[1] + fold(grad * unit)

        shift_sum, gain_sum = map(whole, over(image, sums_three, (none, none)))
        sums["gain_three"].append(gain_sum)
        sums["shift_three"].append(shift_sum)
        mean_shift, mean_gain = norm_back_terms(gain_three, shift_sum, gain_sum)

        def back_three(image, step, total):
            unit = (load_middle(image, step) - center) * rate
            grad = rate * (delta_at(image, step) * gain_three - mean_shift - unit * mean_gain)
            grad = grad + load_upstream(image, step)
            s.grad_middle[flat_at(image, step), :] = grad
            low = grad.astype(jnp.bfloat16)
            s.grad_two[flat_at(image, step), :] = low
            low = low.astype(jnp.float32)
            spread_out(s.spread_two, image, step, low, 2, 0)
            return total + fold(low)

        sums["bias_two"].append(whole(over(image, back_three, none)))
        share_grad_two[image].start()
        if between is not None:
            between()

        s.delta[rows, :] = convolve_back(s.spread_two, s.conv_two_here, slice(image, image + 1))

        def put_hidden(image, step, grad, total):
            low = grad.astype(jnp.bfloat16)
            s.grad_one[flat_at(image, step), :] = low
            low = low.astype(jnp.float32)
            spread_out(s.spread_one, image, step, low, 2, 0)
            return total + fold(low)

        gain_sum, shift_sum, total = swish_norm_back(
            load_hidden, image, moments_two[image], gain_two, shift_two, put_hidden, none
        )
        share_grad_one[image].start()
        sums["gain_two"].append(gain_sum)
        sums["shift_two"].append(shift_sum)
        sums["bias_one"].append(whole(total))

    def swish_norm_back(load, image, moments, gain, shift, put, start):
        center, rate = moments

        def totals(image, step, carry):
            unit = (load(image, step) - center) * rate
            field = unit * gain + shift
            gate = sigmoid(field)
            grad = delta_at(image, step) * (gate * (1.0 + field * (1.0 - gate)))
            s.delta[flat_at(image, step), :] = grad
            return carry[0] + fold(grad), carry[1] + fold(grad * unit)

        shift_sum, gain_sum = map(whole, over(image, totals, (none, none)))
        mean_shift, mean_gain = norm_back_terms(gain, shift_sum, gain_sum)

        def back(image, step, carry):
            unit = (load(image, step) - center) * rate
            grad = rate * (delta_at(image, step) * gain - mean_shift - unit * mean_gain)
            return put(image, step, grad, carry)

        return gain_sum, shift_sum, over(image, back, start)

    def backward_input(image):
        s.delta[image_rows(image), :] = convolve_back(
            s.spread_one, s.conv_one_here, slice(image, image + 1)
        )
        def put_input(image, step, grad, carry):
            total = grad + s.grad_middle[flat_at(image, step), :]
            s.leaving_grad[image, at(step), :] = total.astype(jnp.bfloat16)
            return carry

        gain_sum, shift_sum, _ = swish_norm_back(
            load_input, image, moments_one[image], gain_one, shift_one, put_input, 0
        )
        swap_grad[image].start()
        sums["gain_one"].append(gain_sum)
        sums["shift_one"].append(shift_sum)

    mix_rows = s.blocks_mix.shape[2] // 4

    def store_mix(which, product):
        product = product.astype(jnp.bfloat16)
        for rank in range(ranks):
            for core in range(2):
                block = rank * 2 + core
                spot = spots_mix[which // 2][rank]
                s.blocks_mix[spot, core, which * mix_rows : (which + 1) * mix_rows, :] = product[
                    block * mix_rows : (block + 1) * mix_rows
                ]

    def weigh_mix():
        upstream = s.upstream[...].reshape(flat_rows, channels)
        normed = s.normed[...]
        store_mix(3, by_rows(s.mixed[...], upstream))
        store_mix(0, by_rows(normed, s.grad_query[...]))
        store_mix(1, by_rows(normed, s.grad_key[...]))
        store_mix(2, by_rows(normed, s.grad_value[...]))

    def column_sums(load):
        def body(image, step, total):
            return total + fold(load(image, step))

        total = none
        for image in every_image:
            total = over(image, body, total)
        return whole(total)

    def fill_slot():
        slot_place = lax.broadcasted_iota(jnp.int32, (slot_rows, lanes), 0)
        slot = jnp.zeros((slot_rows, lanes), jnp.float32)
        for image in every_image:
            for index in range(per_image):
                row = sums["bias_one"][image][:, index * lanes : (index + 1) * lanes]
                slot = jnp.where(
                    slot_place == image * per_image + index,
                    jnp.broadcast_to(row, slot.shape),
                    slot,
                )
        device = place.rank * 2 + place.core
        s.slots[pl.ds(pl.multiple_of(device * slot_rows, slot_rows), slot_rows), :] = slot

    per_image = channels // lanes

    def flat(first, rows):
        count, width = rows.shape[0], rows.shape[1] // lanes
        for index in range(width):
            s.flat[pl.ds(first + index, count, stride=width), :] = rows[
                :, index * lanes : (index + 1) * lanes
            ]

    def embedding_gradients():
        def every(index):
            return s.slots[pl.ds(index, ranks * 2, stride=slot_rows), :]

        device = place.rank * 2 + place.core
        de = jnp.concatenate(
            [
                jnp.concatenate([every(image * per_image + j) for j in range(per_image)], axis=1)
                for image in every_image
            ],
            axis=0,
        )
        place_of = lax.broadcasted_iota(jnp.int32, (images_here * ranks * 2, lanes), 0)
        lane = lax.broadcasted_iota(jnp.int32, place_of.shape, 1)
        wanted = (place_of % (ranks * 2)) // 2 * images_here + place_of // (ranks * 2)
        tiles = [jnp.broadcast_to(s.levels_all[core, 0:1, :], place_of.shape) for core in (0, 1)]
        chosen = jnp.where(place_of % 2 == 0, tiles[0], tiles[1])
        levels = jnp.sum(jnp.where(lane == wanted, chosen, 0.0), axis=1, keepdims=True)
        levels = levels.astype(jnp.int32)
        entry = lax.broadcasted_iota(
            jnp.int32, (levels.shape[0], s.noise_table_here.shape[0]), 1
        )
        hit = jnp.where(entry == levels, 1.0, 0.0).astype(jnp.bfloat16)
        everywhere = matmul(hit, s.noise_table_here[...])
        exact = dict(preferred_element_type=jnp.float32, precision=lax.Precision.HIGHEST)
        own_rows = channels // (ranks * 2)
        s.product[...] = lax.dot_general(everywhere, de, (((0,), (0,)), ((), ())), **exact)
        first = pl.multiple_of(device * own_rows, own_rows)
        flat(spans["embed"], s.product[pl.ds(first, own_rows), :])
        grad_rows = lax.dot_general(
            de, s.embed_weight_here[...].astype(jnp.float32), (((1,), (1,)), ((), ())), **exact
        )
        halves = table_rows * 2 // (ranks * 2)
        wide = -(-halves // 128) * 128
        spot = lax.broadcasted_iota(jnp.int32, (levels.shape[0], wide), 1) + device * halves
        total = jnp.zeros((wide, half), jnp.float32)
        for side in range(2):
            pick = jnp.where(2 * levels + side == spot, 1.0, 0.0)
            total = total + lax.dot_general(
                pick,
                grad_rows[:, side * half : (side + 1) * half],
                (((0,), (0,)), ((), ())),
                **exact,
            )
        flat(spans["table"], total)

    def sum_biases():
        sums["query_bias"].append(column_sums(load_low(s.grad_query)))
        sums["value_bias"].append(column_sums(load_low(s.grad_value)))
        sums["out_bias"].append(column_sums(load_upstream))

    def start_small():
        rows = [functools.reduce(jnp.add, sums[name]) for name in SUMS]
        s.small_sum[0, 0:8, :] = stack_rows(rows[:8])
        s.small_sum[0, 8:16, :] = stack_rows(rows[8:])
        small[0].start()

    def step_all(reduction, stage):
        for part in range(reduction.parts):
            reduction.step(stage, part)

    for image in every_image:
        forward(image)
    for image in every_image[:-1]:
        backward(image)
        backward_rest(image)
        backward_input(image)
    for image in every_image:
        swap_output[image].start()
    backward(images_here - 1)
    backward_rest(images_here - 1)
    fill_slot()
    slots_pair.start()
    weigh_mix()
    reduce_mix.start(0, 0)
    reduce_mix.start(0, 1)
    backward_input(images_here - 1)
    step_all(reduce_mix, 0)
    slots_pair.arrive()
    slots_all.start()
    for image in every_image:
        share_act_two[image].arrive()
        share_grad_two[image].arrive()
    weigh(
        s.spread_two, half_two, s.act_two, s.act_two_far, s.grad_two_far, s.blocks_two, spots_two
    )
    for part in range(parts):
        reduce_two.start(0, part)
    for image in every_image:
        share_act_one[image].arrive()
        share_grad_one[image].arrive()
    weigh(
        s.spread_one, half_one, s.act_one, s.act_one_far, s.grad_one_far, s.blocks_one, spots_one
    )
    for part in range(parts):
        reduce_one.start(0, part)
    step_all(reduce_two, 0)
    step_all(reduce_one, 0)
    sum_biases()
    start_small()
    reduce_two.step(1, 0)
    reduce_one.step(1, 0)
    reduce_two.step(1, 1)
    reduce_two.step(2, 0)
    reduce_mix.step(1, 1)
    reduce_mix.step(1, 0)
    reduce_one.step(1, 1)
    reduce_one.step(2, 0)
    reduce_two.step(1, 2)
    reduce_two.step(2, 1)
    small_step(0)
    reduce_one.step(2, 1)
    reduce_two.step(3, 0)
    reduce_one.step(1, 2)
    levels_pair.arrive()
    slots_all.arrive()
    embedding_gradients()
    reduce_one.step(3, 0)
    reduce_two.step(3, 1)
    end_two = share_copy(4 * images_here, s.fin_two.at[1 - half_two, chain], s.last_two, bit_two).start()
    small_step(1)
    reduce_mix.step(2, 1)
    reduce_mix.step(2, 0)
    reduce_one.step(3, 1)
    end_one = share_copy(
        4 * images_here + 1, s.fin_one.at[1 - half_one, chain], s.last_one, bit_one
    ).start()
    small_step(2)
    reduce_mix.step(3, 1)
    reduce_mix.step(3, 0)
    small_step(3)
    reduce_mix.step(4, 1)
    reduce_mix.step(4, 0)
    for index, name in enumerate(dict(query=0, key=0, value=0, out=0)):
        flat(spans[name], s.share_mix[index * mix_rows : (index + 1) * mix_rows, :])
    flat(spans["conv_two"] + chain_rows * per_image, gather_straight(1, s.straight_two))
    flat(spans["conv_two"], settle(end_two, s.sum_two, s.last_two, half_two))
    flat(spans["conv_one"] + chain_rows * per_image, gather_straight(0, s.straight_one))
    flat(spans["conv_one"], settle(end_one, s.sum_one, s.last_one, half_one))
    small_step(4)
    for index in range(len(SUMS)):
        s.sums[index] = s.small_sum[bits + 1, index : index + 1, :]

    for flight in flights:
        flight.land()


def last_kernel(starts, rows, *refs):
    output_in, grad_in, flat_in, sums_in, output, grad = refs[:6]
    flats, sums = refs[6 : 6 + len(starts)], refs[6 + len(starts) : -5]
    output_here, grad_here, flat_here, sums_here, sems = refs[-5:]
    arrive = [
        pltpu.make_async_copy(sums_in, sums_here, sems.at[0]),
        pltpu.make_async_copy(output_in, output_here, sems.at[1]),
        pltpu.make_async_copy(grad_in, grad_here, sems.at[2]),
        pltpu.make_async_copy(flat_in, flat_here, sems.at[3]),
    ]
    for move in arrive:
        move.start()
    ways = [
        [(sums_here.at[row], target) for row, target in zip(rows, sums, strict=True)],
        [(output_here, output)],
        [(grad_here, grad)],
        [
            (flat_here.at[pl.ds(start, target.shape[0]), :], target)
            for start, target in zip(starts, flats, strict=True)
        ],
    ]
    leave = []
    for move, pairs in zip(arrive, ways, strict=True):
        move.wait()
        for source, target in pairs:
            leave.append(pltpu.make_async_copy(source, target, sems.at[4 + len(leave)]))
            leave[-1].start()
    for move in leave:
        move.wait()


def fused_device(given):
    ranks = lax.axis_size("wide")
    bits = (ranks - 1).bit_length()
    images = given["images"]
    images_rep, piece, channels = images.shape
    images_here, pixels = images_rep // ranks, piece * ranks
    flat_rows = images_here * pixels
    half = channels // 2
    devices = ranks * 2
    table_rows = given["noise_table"].shape[0]
    padded_rows = -(-table_rows // 128) * 128
    conv_rows = given["conv_one"].shape[0] // devices
    mix_rows = 4 * channels // devices
    low, full = jnp.bfloat16, jnp.float32
    parts = 3
    lanes = 128

    def struct(shape, kind):
        return jax.ShapeDtypeStruct(shape, kind)

    def hold(*shape, kind=low):
        return pltpu.VMEM(shape, kind)

    def semaphores(*shape):
        return pltpu.SemaphoreType.DMA(shape)

    def activations():
        return hold(flat_rows, channels)

    def fields():
        return hold(flat_rows, channels, kind=full)

    def square():
        return hold(channels, channels)

    def images_low():
        return hold(images_here, pixels, channels)

    def flat_span(size, pad=False):
        rows = size // lanes
        return -(-rows // 128) * 128 if pad else rows

    share = channels * channels // devices
    sizes = dict(
        conv_one=flat_span(conv_rows * channels),
        conv_two=flat_span(conv_rows * channels),
        query=flat_span(share),
        key=flat_span(share),
        value=flat_span(share),
        out=flat_span(share),
        embed=flat_span(share),
        table=flat_span(table_rows * channels // devices, True),
    )
    spans, start = {}, 0
    for name, size in sizes.items():
        spans[name] = start
        start = start + size

    outputs = dict(
        output=struct(images.shape, low),
        input_grad=struct(images.shape, low),
        flat=struct((start, lanes), full),
        sums=struct((len(SUMS), 1, channels), full),
    )
    padded = pixels + 2 * SIDE
    halvings = sum(ranks >> stage for stage in range(bits + 1))
    scratch = dict(
        noise_table_here=hold(padded_rows, channels),
        embed_weight_here=square(),
        conv_one_here=hold(*given["conv_one"].shape),
        conv_two_here=hold(*given["conv_two"].shape),
        query_weight_here=square(),
        key_weight_here=square(),
        value_weight_here=square(),
        out_weight_here=square(),
        arrived=images_low(),
        upstream=images_low(),
        leaving=images_low(),
        leaving_grad=images_low(),
        spread_act=hold(images_here, padded, 3 * channels),
        spread_two=hold(images_here, padded, 3 * channels),
        spread_one=hold(images_here, padded, 3 * channels),
        spread_far=hold(images_here, padded, 3 * half),
        hidden=fields(),
        middle=fields(),
        delta=fields(),
        grad_middle=fields(),
        probs=hold(flat_rows, pixels, kind=full),
        act_one=activations(),
        act_two=activations(),
        act_one_far=activations(),
        act_two_far=activations(),
        normed=activations(),
        query=activations(),
        key=activations(),
        value=activations(),
        mixed=activations(),
        grad_mixed=activations(),
        grad_query=activations(),
        grad_key=activations(),
        grad_value=activations(),
        grad_one=activations(),
        grad_two=activations(),
        grad_one_far=hold(flat_rows, half),
        grad_two_far=hold(flat_rows, half),
        blocks_one=hold(ranks, 2, conv_rows, half),
        blocks_two=hold(ranks, 2, conv_rows, half),
        blocks_mix=hold(ranks, 2, mix_rows, channels),
        land_one=hold(halvings - 1, conv_rows, half),
        land_two=hold(halvings - 1, conv_rows, half),
        land_mix=hold(halvings, mix_rows, channels),
        kept_one=hold(halvings - 3, conv_rows, half),
        kept_two=hold(halvings - 3, conv_rows, half),
        kept_mix=hold(halvings - 1, mix_rows, channels),
        sum_one=hold(2, conv_rows, half, kind=full),
        sum_two=hold(2, conv_rows, half, kind=full),
        fin_one=hold(2, conv_rows, half),
        fin_two=hold(2, conv_rows, half),
        last_one=hold(conv_rows // parts * (parts - 1), half),
        last_two=hold(conv_rows // parts * (parts - 1), half),
        straight_one=hold(ranks // 2, conv_rows // parts, half),
        straight_two=hold(ranks // 2, conv_rows // parts, half),
        straight_send=semaphores(2),
        straight_recv=semaphores(2),
        share_mix=hold(mix_rows, channels, kind=full),
        small_sum=hold(bits + 2, 16, channels, kind=full),
        small_land=hold(bits + 1, 16, channels, kind=full),
        slots=hold(devices * 8, lanes, kind=full),
        levels_all=hold(2, 8, lanes, kind=full),
        product=hold(channels, channels, kind=full),
        same_group=hold(half, half),
        load_sem=semaphores(8),
        swap_send=semaphores(4 * images_here),
        swap_recv=semaphores(4 * images_here),
        swap_own=semaphores(4 * images_here),
        share_send=semaphores(4 * images_here + 2),
        share_recv=semaphores(4 * images_here + 2),
        small_send=semaphores(bits + 1),
        small_recv=semaphores(bits + 1),
        slots_send=semaphores(3),
        slots_recv=semaphores(3),
        reduce_send_one=semaphores(bits, parts),
        reduce_recv_one=semaphores(bits, parts),
        reduce_send_two=semaphores(bits, parts),
        reduce_recv_two=semaphores(bits, parts),
        reduce_send_mix=semaphores(bits + 1, 2),
        reduce_recv_mix=semaphores(bits + 1, 2),
    )

    in_vmem = pl.BlockSpec(memory_space=pltpu.VMEM)
    anywhere = pl.BlockSpec(memory_space=pl.ANY)
    in_smem = pl.BlockSpec(memory_space=pltpu.SMEM)
    arrays, in_specs = {}, []
    for name, value in given.items():
        if value.ndim == 1 and value.dtype == full:
            value = value.reshape(1, channels)
            in_specs.append(in_vmem)
        else:
            in_specs.append(in_smem if value.ndim == 1 else anywhere)
        arrays[name] = value
    names = tuple(arrays) + tuple(outputs) + tuple(scratch)
    output, input_grad, flat, sums = pl.pallas_call(
        functools.partial(fused_kernel, names, spans, ranks, table_rows),
        out_shape=tuple(outputs.values()),
        in_specs=in_specs,
        out_specs=(anywhere, anywhere, in_vmem, in_vmem),
        scratch_shapes=list(scratch.values()),
        compiler_params=pltpu.CompilerParams(
            collective_id=0, has_side_effects=True, vmem_limit_bytes=63 << 20
        ),
        name="block",
    )(*arrays.values())

    order = dict(table=0, conv_one=0, conv_two=0, embed=0, query=0, key=0, value=0, out=0)
    sizes["table"] = table_rows * channels // devices // lanes
    finals = [struct((sizes[name], lanes), full) for name in order]
    rows = [SUMS.index(name) for name in GIVEN_BACK]
    results = pl.pallas_call(
        functools.partial(last_kernel, [spans[name] for name in order], rows),
        out_shape=(outputs["output"], outputs["input_grad"], *finals)
        + (struct((1, channels), full),) * len(rows),
        in_specs=[anywhere] * 4,
        out_specs=(anywhere,) * (2 + len(finals) + len(rows)),
        scratch_shapes=[
            hold(*images.shape),
            hold(*images.shape),
            hold(start, lanes, kind=full),
            hold(*outputs["sums"].shape, kind=full),
            semaphores(6 + len(finals) + len(rows)),
        ],
        compiler_params=pltpu.CompilerParams(vmem_limit_bytes=63 << 20),
        name="finish",
    )(output, input_grad, flat, sums)
    return tuple(results[:2]) + tuple(member.reshape(-1) for member in results[2:])


def per_device(
    images,
    cotangent,
    levels,
    noise_table,
    gain_one,
    shift_one,
    conv_one,
    bias_one,
    embed_weight,
    embed_bias,
    gain_two,
    shift_two,
    conv_two,
    bias_two,
    gain_three,
    shift_three,
    query_weight,
    query_bias,
    key_weight,
    value_weight,
    value_bias,
    out_weight,
    out_bias,
):
    given = dict(
        images=images,
        cotangent=cotangent,
        levels=levels,
        noise_table=noise_table,
        gain_one=gain_one,
        shift_one=shift_one,
        conv_one=conv_one,
        bias_one=bias_one,
        embed_weight=embed_weight,
        embed_bias=embed_bias,
        gain_two=gain_two,
        shift_two=shift_two,
        conv_two=conv_two,
        bias_two=bias_two,
        gain_three=gain_three,
        shift_three=shift_three,
        query_weight=query_weight,
        query_bias=query_bias,
        key_weight=key_weight,
        value_weight=value_weight,
        value_bias=value_bias,
        out_weight=out_weight,
        out_bias=out_bias,
    )
    ranks, cores = lax.axis_size("wide"), lax.axis_size("rep")
    images_rep, piece, channels = images.shape
    devices = ranks * cores
    fits = (
        cores == 2
        and ranks >= 8
        and ranks & (ranks - 1) == 0
        and images_rep == 2 * ranks
        and piece % 16 == 0
        and conv_one.shape[0] % (devices * 48) == 0
        and channels % (devices * 16) == 0
        and noise_table.size % (devices * channels // 2) == 0
    )
    return fused_device(given) if fits else plain_device(*given.values())


def solution(mesh):
    in_specs = (
        P("rep", "wide", None),
        P("rep", "wide", None),
        P("rep"),
        P(),
        P(),
        P(),
        P(),
        P(),
        P(),
        P(),
        P(),
        P(),
        P(),
        P(),
        P(),
        P(),
        P(),
        P(),
        P(),
        P(),
        P(),
        P(),
        P(),
    )
    out_specs = (
        P("rep", "wide", None),
        P("rep", "wide", None),
        P(("wide", "rep")),
        P(("wide", "rep")),
        P(("wide", "rep")),
        P(("wide", "rep")),
        P(("wide", "rep")),
        P(("wide", "rep")),
        P(("wide", "rep")),
        P(("wide", "rep")),
        P(),
        P(),
        P(),
        P(),
        P(),
        P(),
        P(),
        P(),
        P(),
        P(),
        P(),
        P(),
    )
    return jax.shard_map(
        per_device, mesh=mesh, in_specs=in_specs, out_specs=out_specs, check_vma=False
    )
```
